32 devices in a mesh: groups: 2 (over y), dp: 4 (over z), tensor: 4 (over x, core).
Axes of the slice: x: 2, y: 2, z: 4, core: 2. Of those that a mesh axis runs over, the one named last changes fastest.
Arguments:
- activations: bfloat16 [64, 256, 4096], P(('groups', 'dp'), None, 'tensor'), parts along dimension 0, may hold values from -6 to 6
- out_grads: bfloat16 [64, 256, 14336], P(('groups', 'dp'), None, 'tensor'), parts along dimension 0, may hold values from -6 to 6
- proj_in: bfloat16 [4096, 64], P('tensor'), may hold values from -0.09375 to 0.09375
- proj_out: bfloat16 [14336, 64], P('tensor'), may hold values from -0.046875 to 0.046875
- lengths: int32 [64], P(('groups', 'dp')), parts along dimension 0, may hold values from 1 to 256, 6144 in all
- test_grads: bfloat16 [1024, 4096], P(('groups', 'dp')), parts along dimension 0, may hold values from -0.09375 to 0.09375
Outputs:
- scores: float32 [64, 512], P(('groups', 'dp')), parts along dimension 0
The draws below stay inside these ranges and needn't reach their ends.
There are 2 independent parts, one for each index of `groups`. The reference program is written for one: setup_inputs(seed, part) draws one part's arguments, and reference() takes and returns one part's arrays. A program takes and returns all parts, laid end to end along the dimension named above; an argument that names none is the same for every part. Nothing has to cross between parts.
All inputs are finite; a program needn't handle non-finite values. No bound on the sum of `lengths` on one device may be relied on, other than what follows from the above.
Results may differ from the reference program's by a relative error of at most 0.0029.
Values may be sent and summed in bfloat16 or wider, within the bound.
No kernel may reach another device: no remote copies, remote signals or barrier semaphores. Data moves between devices by JAX's collectives and lax.ppermute only.
A program may use at most 128 MiB of HBM per device.

```python
import math
import jax
import jax.numpy as jnp
import numpy as np
from jax import lax

D = 4096
FF = 14336
RANK = 64
SEQ_LEN = 256
SEQS = 32
TEST = 512


def level_of(own_key, extent, cuts, least, top_value):
    gain, own = 1.0, jax.random.fold_in(own_key, 6)
    for dim, parts in cuts:
        steps = jnp.exp(jax.random.uniform(jax.random.fold_in(own, dim), (parts,), jnp.float32, least / len(cuts), top_value / len(cuts)))
        gain = gain * jnp.repeat(steps, extent[dim] // parts).reshape([-1 if axis == dim else 1 for axis in range(len(extent))])
    return gain


def length_profile(count, total, bound, skew):
    portions = [(1 << 20) // math.isqrt(grade ** skew) + 1 for grade in range(2, count + 1)]
    rest, given = total - bound - (count - 1), [1] * (count - 1)
    while rest > 0:
        free = [i for i in range(count - 1) if given[i] < bound]
        whole, budget = sum([portions[i] for i in free]), rest
        for i in free:
            extra = min(bound - given[i], max(1, budget * portions[i] // whole), rest)
            given[i] = given[i] + extra
            rest = rest - extra
    return np.array([bound] + given)


def uneven_parts(own_key, amount, total, most, skew):
    if amount == 2:
        one = jax.random.randint(own_key, (), max(1, total - most), min(most, total - 1) + 1)
        return jnp.stack([one, total - one])
    sizes = jnp.asarray(length_profile(amount, total, most, skew), jnp.int32)
    pairs = (amount - 1) // 2
    donor, sink = sizes[1:1 + 2 * pairs:2], sizes[2:2 + 2 * pairs:2]
    slack = jnp.minimum(donor - 1, most - sink)
    moved = jax.random.randint(jax.random.fold_in(own_key, 1), (pairs,), 0, 1 << 20) % (slack + 1)
    sizes = sizes.at[1:1 + 2 * pairs:2].set(donor - moved).at[2:2 + 2 * pairs:2].set(sink + moved)
    return sizes[jax.random.permutation(jax.random.fold_in(own_key, 2), amount)]


def bell_draw(own_key, dims, deviation, most, cuts=(), kind=jnp.bfloat16):
    gain = level_of(own_key, dims, cuts, -0.22, 0.18) if cuts else 1.0
    result = jax.random.normal(own_key, dims, jnp.float32) * deviation * gain
    return jnp.minimum(jnp.maximum(result, -most), most).astype(kind)


def setup_inputs(seed: int = 0, part: int = 0) -> dict:
    streams_of = jax.random.split(jax.random.key(seed), 7)
    part_splits = jax.random.split(jax.random.fold_in(streams_of[6], part), 7)
    activations = bell_draw(part_splits[0], (SEQS, SEQ_LEN, D), 1.0, 6.0, ((0, 4), (2, 4)))
    out_grads = bell_draw(part_splits[1], (SEQS, SEQ_LEN, FF), 1.0, 6.0, ((0, 4), (2, 4)))
    proj_in = bell_draw(streams_of[2], (D, RANK), D ** -0.5, 0.09375, ((0, 4),))
    proj_out = bell_draw(streams_of[3], (FF, RANK), FF ** -0.5, 0.046875, ((0, 4),))
    lengths = uneven_parts(part_splits[4], SEQS, SEQS * SEQ_LEN * 3 // 4, SEQ_LEN, 0).astype(jnp.int32)
    test_grads = bell_draw(part_splits[5], (TEST, RANK * RANK), (RANK * RANK) ** -0.5, 0.09375, ((0, 4),))
    return dict(activations=activations, out_grads=out_grads, proj_in=proj_in, proj_out=proj_out, lengths=lengths, test_grads=test_grads)


def reference(activations, out_grads, proj_in, proj_out, lengths, test_grads):
    in_factor = jnp.dot(activations.reshape(SEQS * SEQ_LEN, D), proj_in, preferred_element_type=jnp.float32)
    out_factor = jnp.dot(out_grads.reshape(SEQS * SEQ_LEN, FF), proj_out, preferred_element_type=jnp.float32)
    in_factor = in_factor.reshape(SEQS, SEQ_LEN, RANK)
    out_factor = out_factor.reshape(SEQS, SEQ_LEN, RANK)
    position = jnp.arange(SEQ_LEN, dtype=jnp.int32)
    keep = (position[None, :] < lengths[:, None]).astype(jnp.float32)
    masked = in_factor * keep[:, :, None]
    example_grads = jnp.einsum('nti,ntj->nij', masked, out_factor, precision=lax.Precision.HIGHEST)
    example_grads = example_grads / lengths.astype(jnp.float32)[:, None, None]
    flat = example_grads.reshape(SEQS, RANK * RANK)
    scale = jnp.sqrt(lax.optimization_barrier(jnp.mean(flat * flat, axis=1, keepdims=True)) + 1e-06)
    unit = (flat / scale).astype(jnp.bfloat16)
    return lax.dot_general(unit, test_grads, (((1,), (1,)), ((), ())), preferred_element_type=jnp.float32)
```

```python
import functools

import jax
import jax.numpy as jnp
from jax import lax
from jax.experimental import pallas as pl
from jax.experimental.pallas import tpu as pltpu
from jax.sharding import PartitionSpec as P

CORES = 2
NT = (((1,), (1,)), ((), ()))
TN = (((0,), (0,)), ((), ()))


def xor_permute(value, axis, size, step):
    return lax.ppermute(value, axis, [(i, i ^ step) for i in range(size)])


def project_kernel(steps, share, act, og, wi, wo, out, abuf, obuf, asem, osem):
    me = lax.axis_index("tensor")
    copies = []
    for at, step in enumerate(steps):
        for k in range(share):
            slot = at * share + k
            seq = (me ^ step) * share + k
            copies.append(
                (
                    pltpu.make_async_copy(act.at[seq], abuf.at[slot], asem.at[slot]),
                    pltpu.make_async_copy(og.at[seq], obuf.at[slot], osem.at[slot]),
                )
            )
    for a_copy, o_copy in copies:
        a_copy.start()
        o_copy.start()
    wide_in = jnp.concatenate([wi[...], jnp.zeros_like(wi)], axis=0)
    wide_out = jnp.concatenate([jnp.zeros_like(wo), wo[...]], axis=0)
    for slot, (a_copy, o_copy) in enumerate(copies):
        a_copy.wait()
        part = lax.dot_general(abuf[slot], wide_in, NT, preferred_element_type=jnp.float32)
        o_copy.wait()
        out[slot] = part + lax.dot_general(obuf[slot], wide_out, NT, preferred_element_type=jnp.float32)


def project(act, og, wi, wo, steps, share):
    count = len(steps) * share
    slots, feat, hidden = act.shape[1], act.shape[2], og.shape[2]
    rank = wi.shape[0]
    return pl.pallas_call(
        functools.partial(project_kernel, steps, share),
        out_shape=jax.ShapeDtypeStruct((count, slots, 2 * rank), jnp.float32),
        in_specs=[pl.BlockSpec(memory_space=pl.ANY)] * 2 + [pl.BlockSpec(memory_space=pltpu.VMEM)] * 2,
        out_specs=pl.BlockSpec(memory_space=pltpu.VMEM),
        scratch_shapes=[
            pltpu.VMEM((count, slots, feat), act.dtype),
            pltpu.VMEM((count, slots, hidden), og.dtype),
            pltpu.SemaphoreType.DMA((count,)),
            pltpu.SemaphoreType.DMA((count,)),
        ],
        compiler_params=pltpu.CompilerParams(vmem_limit_bytes=40 << 20),
        cost_estimate=pl.CostEstimate(
            flops=2 * count * slots * (feat + hidden) * 256,
            bytes_accessed=2 * count * slots * (feat + hidden),
            transcendentals=0,
        ),
    )(act, og, wi, wo)


def unit_kernel(share, rank, size, lens, *refs):
    parts, outs, pair, held = refs[: -2 - size], refs[-2 - size : -2], refs[-2], refs[-1]
    me = lax.axis_index("tensor")
    slots = parts[0].shape[1]
    rows = rank * rank // 128
    span = rows // size
    lane = lax.broadcasted_iota(jnp.int32, (rows, 2 * rank), 1)
    row = lax.broadcasted_iota(jnp.int32, (slots, 2 * rank), 0)
    for k in range(share):
        full = parts[0][k]
        for part in parts[1:]:
            full = full + part[k]
        length = lens[me * share + k]
        masked = jnp.where(row < length, full, 0.0)
        both = lax.dot_general(
            masked, full, TN, precision=lax.Precision.HIGHEST, preferred_element_type=jnp.float32
        )
        pair[...] = both[:rank] / length.astype(jnp.float32)
        even = pltpu.roll(pair[pl.ds(0, rows, stride=2), :], rank, 1)
        odd = pair[pl.ds(1, rows, stride=2), :]
        flat = jnp.where(lane < rank, even, odd)
        scale = jnp.sqrt(jnp.sum(flat * flat) / (rank * rank) + 1e-06)
        unit = flat / scale
        for at in range(size):
            held[at] = unit[at * span : (at + 1) * span]
        for step in range(size):
            outs[step][k] = held[me ^ step]


def units(lens, parts, share, rank, size):
    rows = rank * rank // 128
    span = rows // size
    return pl.pallas_call(
        functools.partial(unit_kernel, share, rank, size),
        out_shape=[jax.ShapeDtypeStruct((share, span, 128), jnp.float32)] * size,
        in_specs=[pl.BlockSpec(memory_space=pltpu.SMEM)] + [pl.BlockSpec(memory_space=pltpu.VMEM)] * len(parts),
        out_specs=[pl.BlockSpec(memory_space=pltpu.VMEM)] * size,
        scratch_shapes=[
            pltpu.VMEM((rank, 2 * rank), jnp.float32),
            pltpu.VMEM((size, span, 128), jnp.float32),
        ],
    )(lens, *parts)


def score_kernel(share, size, groups, *refs):
    unit_refs, test_refs, out, held = refs[:size], refs[size : size + groups], refs[-2], refs[-1]
    me, dp = lax.axis_index("tensor"), lax.axis_index("dp")
    span = unit_refs[0].shape[1]
    for step in range(size):
        for k in range(share):
            held[(me ^ step) * share + k] = unit_refs[step][k]
    unit = jnp.concatenate([held[:, c, :] for c in range(span)], axis=1).astype(jnp.bfloat16)
    tests = test_refs[0].shape[0]
    for step in range(groups):
        part = lax.dot_general(unit, test_refs[step][...], NT, preferred_element_type=jnp.float32)
        out[:, pl.ds(pl.multiple_of((dp ^ step) * tests, 128), tests)] = part


def score(unit_parts, test_parts, share):
    size, groups = len(unit_parts), len(test_parts)
    tests, width = test_parts[0].shape
    return pl.pallas_call(
        functools.partial(score_kernel, share, size, groups),
        out_shape=jax.ShapeDtypeStruct((share * size, tests * groups), jnp.float32),
        in_specs=[pl.BlockSpec(memory_space=pltpu.VMEM)] * (size + groups),
        out_specs=pl.BlockSpec(memory_space=pltpu.VMEM),
        scratch_shapes=[pltpu.VMEM((share * size, width // 128, 128), jnp.float32)],
        compiler_params=pltpu.CompilerParams(vmem_limit_bytes=40 << 20),
    )(*unit_parts, *test_parts)


def shards(size, groups, activations, out_grads, proj_in, proj_out, lengths, test_grads):
    rank = proj_in.shape[1]
    share = activations.shape[0] // size
    me = lax.axis_index("tensor")
    width = test_grads.shape[1] // size
    own_tests = lax.dynamic_slice_in_dim(test_grads, me * width, width, 1)
    test_parts = [own_tests] + [xor_permute(own_tests, "dp", groups, step) for step in range(1, groups)]

    wi, wo = proj_in.T, proj_out.T
    chips = size // CORES
    far = [CORES * x for x in range(1, chips)]
    other = project(activations, out_grads, wi, wo, [step ^ 1 for step in far] + [1], share)
    arrived = xor_permute(other, "tensor", size, 1)
    far_part = project(activations, out_grads, wi, wo, far, share)
    cut = len(far) * share
    send = far_part + arrived[:cut]
    sums = [xor_permute(send[i * share : (i + 1) * share], "tensor", size, step) for i, step in enumerate(far)]
    near_part = project(activations, out_grads, wi, wo, [0], share)
    unit_outs = units(lengths, [near_part, arrived[cut:]] + sums, share, rank, size)
    unit_parts = [unit_outs[0]] + [xor_permute(unit_outs[step], "tensor", size, step) for step in range(1, size)]
    part = score(unit_parts, test_parts, share)
    step = 1
    parts = [part] + [xor_permute(part, "tensor", size, step) for step in range(1, size)]
    while len(parts) > 1:
        parts = [parts[i] + parts[i + 1] for i in range(0, len(parts), 2)]
    return parts[0]


def solution(mesh):
    placed = (
        P(("groups", "dp"), None, "tensor"),
        P(("groups", "dp"), None, "tensor"),
        P("tensor", None),
        P("tensor", None),
        P(("groups", "dp")),
        P(("groups", "dp"), None),
    )
    return jax.shard_map(
        functools.partial(shards, mesh.shape["tensor"], mesh.shape["dp"]),
        mesh=mesh,
        in_specs=placed,
        out_specs=P(("groups", "dp"), None),
        check_vma=False,
    )
```

```python
import functools

import jax
import jax.numpy as jnp
from jax import lax
from jax.experimental import pallas as pl
from jax.experimental.pallas import tpu as pltpu
from jax.sharding import PartitionSpec as P

CORES = 2
AHEAD = 2
NT = (((1,), (1,)), ((), ()))
NN = (((1,), (0,)), ((), ()))
TN = (((0,), (0,)), ((), ()))
VMEM_BYTES = 60 << 20


def xor_permute(value, axis, size, step):
    return lax.ppermute(value, axis, [(i, i ^ step) for i in range(size)])


def project_kernel(steps, share, after, act, og, wi, wo, lens, *refs):
    refs = refs[after:]
    outs, (abuf, obuf, wibuf, wobuf, wide_in, wide_out, lenbuf, asem, osem, wsem) = refs[:-10], refs[-10:]
    me = lax.axis_index("tensor")
    rank, feat = wibuf.shape
    hidden = wobuf.shape[1]
    slots = abuf.shape[1]
    count = len(steps) * share
    seqs = [(me ^ step) * share + k for step in steps for k in range(share)]
    small = [
        pltpu.make_async_copy(lens, lenbuf, wsem.at[0]),
        pltpu.make_async_copy(wi, wibuf, wsem.at[1]),
        pltpu.make_async_copy(wo, wobuf, wsem.at[2]),
    ]
    copies = [
        (
            pltpu.make_async_copy(act.at[seq], abuf.at[slot], asem.at[slot]),
            pltpu.make_async_copy(og.at[seq], obuf.at[slot], osem.at[slot]),
        )
        for slot, seq in enumerate(seqs)
    ]
    for copy in small:
        copy.start()
    for slot in range(min(AHEAD, count)):
        copies[slot][0].start()
        copies[slot][1].start()
    for copy in small:
        copy.wait()
    wide_in[...] = jnp.concatenate([wibuf[...], jnp.zeros_like(wibuf)], axis=0).T
    wide_out[...] = jnp.concatenate([jnp.zeros_like(wobuf), wobuf[...]], axis=0).T
    row = lax.broadcasted_iota(jnp.int32, (slots, 2 * rank), 0)
    lane = lax.broadcasted_iota(jnp.int32, (slots, 2 * rank), 1)
    per = count // len(outs)
    for slot in range(count):
        copies[slot][0].wait()
        part = lax.dot_general(abuf[slot], wide_in[...], NN, preferred_element_type=jnp.float32)
        copies[slot][1].wait()
        if slot + AHEAD < count:
            copies[slot + AHEAD][0].start()
            copies[slot + AHEAD][1].start()
        part = part + lax.dot_general(obuf[slot], wide_out[...], NN, preferred_element_type=jnp.float32)
        length = lenbuf[seqs[slot]]
        scale = jnp.where(lane < rank, 1.0 / length.astype(jnp.float32), 1.0)
        outs[slot // per][slot % per] = jnp.where(row < length, part * scale, 0.0)


def project(act, og, wi, wo, lens, groups, share, after=()):
    steps = [step for group in groups for step in group]
    count = len(steps) * share
    slots, feat, hidden = act.shape[1], act.shape[2], og.shape[2]
    rank = wi.shape[0]
    return pl.pallas_call(
        functools.partial(project_kernel, steps, share, len(after)),
        out_shape=[jax.ShapeDtypeStruct((len(group) * share, slots, 2 * rank), jnp.float32) for group in groups],
        in_specs=[pl.BlockSpec(memory_space=pl.ANY)] * (5 + len(after)),
        out_specs=[pl.BlockSpec(memory_space=pltpu.VMEM)] * len(groups),
        scratch_shapes=[
            pltpu.VMEM((count, slots, feat), act.dtype),
            pltpu.VMEM((count, slots, hidden), og.dtype),
            pltpu.VMEM((rank, feat), wi.dtype),
            pltpu.VMEM((rank, hidden), wo.dtype),
            pltpu.VMEM((feat, 2 * rank), wi.dtype),
            pltpu.VMEM((hidden, 2 * rank), wo.dtype),
            pltpu.SMEM(lens.shape, lens.dtype),
            pltpu.SemaphoreType.DMA((count,)),
            pltpu.SemaphoreType.DMA((count,)),
            pltpu.SemaphoreType.DMA((3,)),
        ],
        compiler_params=pltpu.CompilerParams(vmem_limit_bytes=VMEM_BYTES),
        cost_estimate=pl.CostEstimate(
            flops=2 * count * slots * (feat + hidden) * 256,
            bytes_accessed=2 * count * slots * (feat + hidden),
            transcendentals=0,
        ),
    )(act, og, wi, wo, lens, *after)


def unit_kernel(share, rank, size, groups, *refs):
    parts, out, pairs = refs[:-2], refs[-2], refs[-1]
    rows = rank * rank // 128
    span = rows // size
    lane = lax.broadcasted_iota(jnp.int32, (rows, 2 * rank), 1)
    for k in range(share):
        full = parts[0][k]
        for part in parts[1:]:
            full = full + part[k]
        high = full.astype(jnp.bfloat16)
        low = (full - high.astype(jnp.float32)).astype(jnp.bfloat16)
        dot = functools.partial(lax.dot_general, dimension_numbers=TN, preferred_element_type=jnp.float32)
        both = dot(high, high) + (dot(high, low) + dot(low, high))
        pairs[k] = both[:rank]
    for k in range(share):
        even = pltpu.roll(pairs[k, pl.ds(0, rows, stride=2), :], rank, 1)
        odd = pairs[k, pl.ds(1, rows, stride=2), :]
        flat = jnp.where(lane < rank, even, odd)
        scale = jnp.sqrt(jnp.sum(flat * flat) / (rank * rank) + 1e-06)
        unit = (flat / scale).astype(jnp.bfloat16)
        for to in range(groups * size):
            at = to % size * span
            out[to, k] = unit[at : at + span]


def units(parts, share, rank, size, groups):
    span = rank * rank // 128 // size
    return pl.pallas_call(
        functools.partial(unit_kernel, share, rank, size, groups),
        out_shape=jax.ShapeDtypeStruct((groups * size, share, span, 128), jnp.bfloat16),
        in_specs=[pl.BlockSpec(memory_space=pltpu.VMEM)] * len(parts),
        out_specs=pl.BlockSpec(memory_space=pltpu.VMEM),
        scratch_shapes=[pltpu.VMEM((share, rank, 2 * rank), jnp.float32)],
    )(*parts)


def score_kernel(size, unit_ref, test_ref, out):
    span = unit_ref.shape[1]
    whole = unit_ref[...].astype(jnp.float32)
    unit = jnp.concatenate([whole[:, c, :] for c in range(span)], axis=1).astype(jnp.bfloat16)
    part = lax.dot_general(unit, test_ref[...], NT, preferred_element_type=jnp.float32)
    rows = out.shape[1]
    for to in range(out.shape[0]):
        at = to // size * rows
        out[to] = part[at : at + rows]


def score(unit_all, own_tests, size, groups):
    seqs, tests = unit_all.shape[0], own_tests.shape[0]
    return pl.pallas_call(
        functools.partial(score_kernel, size),
        out_shape=jax.ShapeDtypeStruct((groups * size, seqs // groups, tests), jnp.float32),
        in_specs=[pl.BlockSpec(memory_space=pltpu.VMEM)] * 2,
        out_specs=pl.BlockSpec(memory_space=pltpu.VMEM),
    )(unit_all, own_tests)


def finish_kernel(size, parts, out):
    tests = parts.shape[2]
    for group in range(parts.shape[0] // size):
        total = parts[group * size]
        for i in range(1, size):
            total = total + parts[group * size + i]
        out[:, group * tests : (group + 1) * tests] = total


def finish(parts, size):
    count, rows, tests = parts.shape
    return pl.pallas_call(
        functools.partial(finish_kernel, size),
        out_shape=jax.ShapeDtypeStruct((rows, count // size * tests), jnp.float32),
        in_specs=[pl.BlockSpec(memory_space=pltpu.VMEM)],
        out_specs=pl.BlockSpec(memory_space=pltpu.VMEM),
    )(parts)


def shards(size, groups, activations, out_grads, proj_in, proj_out, lengths, test_grads):
    rank = proj_in.shape[1]
    share = activations.shape[0] // size
    me = lax.axis_index("tensor")
    width = test_grads.shape[1] // size
    own_tests = lax.dynamic_slice_in_dim(test_grads, me * width, width, 1)

    far = [CORES * x for x in range(1, size // CORES)]
    arrays = (activations, out_grads, proj_in.T, proj_out.T, lengths)
    far_other, far_own = project(*arrays, [[step ^ 1 for step in far], far], share)
    far_sum = far_own + xor_permute(far_other, "tensor", size, 1)
    sums = [xor_permute(far_sum[i * share : (i + 1) * share], "tensor", size, step) for i, step in enumerate(far)]
    near_other, near_own = project(*arrays, [[1], [0]], share, [far_sum])
    arrived = xor_permute(near_other, "tensor", size, 1)
    unit_cut = units([near_own, arrived] + sums, share, rank, size, groups)
    unit_all = lax.all_to_all(unit_cut, ("dp", "tensor"), 0, 0, tiled=True)
    part = score(unit_all.reshape(-1, *unit_all.shape[2:]), own_tests, size, groups)
    parts = lax.all_to_all(part, ("dp", "tensor"), 0, 0, tiled=True)
    return finish(parts, size)


def solution(mesh):
    placed = (
        P(("groups", "dp"), None, "tensor"),
        P(("groups", "dp"), None, "tensor"),
        P("tensor", None),
        P("tensor", None),
        P(("groups", "dp")),
        P(("groups", "dp"), None),
    )
    return jax.shard_map(
        functools.partial(shards, mesh.shape["tensor"], mesh.shape["dp"]),
        mesh=mesh,
        in_specs=placed,
        out_specs=P(("groups", "dp"), None),
        check_vma=False,
    )
```

```python
import functools

import jax
import jax.numpy as jnp
from jax import lax
from jax.experimental import pallas as pl
from jax.experimental.pallas import tpu as pltpu
from jax.sharding import PartitionSpec as P

CORES = 2
PIECE = 512
AHEAD = 2
NT = (((1,), (1,)), ((), ()))
NN = (((1,), (0,)), ((), ()))
TN = (((0,), (0,)), ((), ()))
VMEM_BYTES = 60 << 20


def xor_permute(value, axis, size, step):
    return lax.ppermute(value, axis, [(i, i ^ step) for i in range(size)])


def project_kernel(steps, share, after, act, og, wi, wo, lens, *refs):
    refs = refs[after:]
    outs, (abuf, obuf, wibuf, wobuf, wide_in, wide_out, lenbuf, asem, osem, wsem) = refs[:-10], refs[-10:]
    me = lax.axis_index("tensor")
    rank, feat = wibuf.shape
    hidden = wobuf.shape[1]
    slots = abuf.shape[1]
    count = len(steps) * share
    seqs = [(me ^ step) * share + k for step in steps for k in range(share)]
    small = [
        pltpu.make_async_copy(lens, lenbuf, wsem.at[0]),
        pltpu.make_async_copy(wi, wibuf, wsem.at[1]),
        pltpu.make_async_copy(wo, wobuf, wsem.at[2]),
    ]
    copies = [
        (
            pltpu.make_async_copy(act.at[seq], abuf.at[slot], asem.at[slot]),
            pltpu.make_async_copy(og.at[seq], obuf.at[slot], osem.at[slot]),
        )
        for slot, seq in enumerate(seqs)
    ]
    for copy in small:
        copy.start()
    for slot in range(min(AHEAD, count)):
        copies[slot][0].start()
        copies[slot][1].start()
    for copy in small:
        copy.wait()
    wide_in[...] = jnp.concatenate([wibuf[...], jnp.zeros_like(wibuf)], axis=0).T
    wide_out[...] = jnp.concatenate([jnp.zeros_like(wobuf), wobuf[...]], axis=0).T
    row = lax.broadcasted_iota(jnp.int32, (slots, 2 * rank), 0)
    lane = lax.broadcasted_iota(jnp.int32, (slots, 2 * rank), 1)
    per = count // len(outs)
    for slot in range(count):
        copies[slot][0].wait()
        copies[slot][1].wait()
        if slot + AHEAD < count:
            copies[slot + AHEAD][0].start()
            copies[slot + AHEAD][1].start()
        pieces = [
            lax.dot_general(
                buf[slot, :, at : at + PIECE], wide[at : at + PIECE], NN, preferred_element_type=jnp.float32
            )
            for buf, wide in ((abuf, wide_in), (obuf, wide_out))
            for at in range(0, wide.shape[0], PIECE)
        ]
        part = sum(pieces[2::2], pieces[0]) + sum(pieces[3::2], pieces[1])
        length = lenbuf[seqs[slot]]
        scale = jnp.where(lane < rank, 1.0 / length.astype(jnp.float32), 1.0)
        outs[slot // per][slot % per] = jnp.where(row < length, part * scale, 0.0)


def project(act, og, wi, wo, lens, groups, share, after=()):
    steps = [step for group in groups for step in group]
    count = len(steps) * share
    slots, feat, hidden = act.shape[1], act.shape[2], og.shape[2]
    rank = wi.shape[0]
    return pl.pallas_call(
        functools.partial(project_kernel, steps, share, len(after)),
        out_shape=[jax.ShapeDtypeStruct((len(group) * share, slots, 2 * rank), jnp.float32) for group in groups],
        in_specs=[pl.BlockSpec(memory_space=pl.ANY)] * 5 + [pl.BlockSpec(memory_space=pltpu.VMEM)] * len(after),
        out_specs=[pl.BlockSpec(memory_space=pltpu.VMEM)] * len(groups),
        scratch_shapes=[
            pltpu.VMEM((count, slots, feat), act.dtype),
            pltpu.VMEM((count, slots, hidden), og.dtype),
            pltpu.VMEM((rank, feat), wi.dtype),
            pltpu.VMEM((rank, hidden), wo.dtype),
            pltpu.VMEM((feat, 2 * rank), wi.dtype),
            pltpu.VMEM((hidden, 2 * rank), wo.dtype),
            pltpu.SMEM(lens.shape, lens.dtype),
            pltpu.SemaphoreType.DMA((count,)),
            pltpu.SemaphoreType.DMA((count,)),
            pltpu.SemaphoreType.DMA((3,)),
        ],
        compiler_params=pltpu.CompilerParams(vmem_limit_bytes=VMEM_BYTES),
        cost_estimate=pl.CostEstimate(
            flops=2 * count * slots * (feat + hidden) * 256,
            bytes_accessed=2 * count * slots * (feat + hidden),
            transcendentals=0,
        ),
    )(act, og, wi, wo, lens, *after)


def unit_kernel(share, rank, size, *refs):
    parts, out, pairs = refs[:-2], refs[-2], refs[-1]
    rows = rank * rank // 128
    span = rows // size
    lane = lax.broadcasted_iota(jnp.int32, (rows, 2 * rank), 1)
    dot = functools.partial(lax.dot_general, dimension_numbers=TN, preferred_element_type=jnp.float32)
    for k in range(share):
        full = parts[0][k]
        for part in parts[1:]:
            full = full + part[k]
        high = full.astype(jnp.bfloat16)
        low = (full - high.astype(jnp.float32)).astype(jnp.bfloat16)
        both = dot(high, high) + (dot(high, low) + dot(low, high))
        pairs[k] = both[:rank]
    for k in range(share):
        even = pltpu.roll(pairs[k, pl.ds(0, rows, stride=2), :], rank, 1)
        odd = pairs[k, pl.ds(1, rows, stride=2), :]
        flat = jnp.where(lane < rank, even, odd)
        scale = jnp.sqrt(jnp.sum(flat * flat) / (rank * rank) + 1e-06)
        unit = flat / scale
        for to in range(size):
            out[to, k] = unit[to * span : (to + 1) * span]


def units(parts, share, rank, size):
    span = rank * rank // 128 // size
    return pl.pallas_call(
        functools.partial(unit_kernel, share, rank, size),
        out_shape=jax.ShapeDtypeStruct((size, share, span, 128), jnp.float32),
        in_specs=[pl.BlockSpec(memory_space=pltpu.VMEM)] * len(parts),
        out_specs=pl.BlockSpec(memory_space=pltpu.VMEM),
        scratch_shapes=[pltpu.VMEM((share, rank, 2 * rank), jnp.float32)],
    )(*parts)


def score_kernel(unit_ref, *refs):
    test_refs, out = refs[:-1], refs[-1]
    dp = lax.axis_index("dp")
    span = unit_ref.shape[1]
    unit = jnp.concatenate([unit_ref[:, c, :] for c in range(span)], axis=1).astype(jnp.bfloat16)
    tests = test_refs[0].shape[0]
    for step, test_ref in enumerate(test_refs):
        part = lax.dot_general(unit, test_ref[...], NT, preferred_element_type=jnp.float32)
        for to in range(out.shape[0]):
            out[to, :, pl.ds(pl.multiple_of((dp ^ step) * tests, 128), tests)] = part


def score(unit_all, test_parts, size):
    seqs, tests = unit_all.shape[0], test_parts[0].shape[0]
    return pl.pallas_call(
        score_kernel,
        out_shape=jax.ShapeDtypeStruct((size, seqs, tests * len(test_parts)), jnp.float32),
        in_specs=[pl.BlockSpec(memory_space=pltpu.VMEM)] * (1 + len(test_parts)),
        out_specs=pl.BlockSpec(memory_space=pltpu.VMEM),
    )(unit_all, *test_parts)


def gather_tests(own, groups):
    if groups == 4:
        across = xor_permute(own, "dp", groups, 3)
        beside = xor_permute(own, "dp", groups, 1)
        return [own, beside, xor_permute(across, "dp", groups, 1), across]
    return [own] + [xor_permute(own, "dp", groups, step) for step in range(1, groups)]


def shards(size, groups, activations, out_grads, proj_in, proj_out, lengths, test_grads):
    rank = proj_in.shape[1]
    share = activations.shape[0] // size
    me = lax.axis_index("tensor")
    width = test_grads.shape[1] // size
    own_tests = lax.dynamic_slice_in_dim(test_grads, me * width, width, 1)
    test_parts = gather_tests(own_tests, groups)

    far = [CORES * x for x in range(1, size // CORES)]
    arrays = (activations, out_grads, proj_in.T, proj_out.T)
    far_other, far_own = project(*arrays, lengths, [[step ^ 1 for step in far], far], share, [own_tests])
    far_sum = far_own + xor_permute(far_other, "tensor", size, 1)
    sums = [xor_permute(far_sum[i * share : (i + 1) * share], "tensor", size, step) for i, step in enumerate(far)]
    near_other, near_own = project(*arrays, lengths, [[1], [0]], share, [far_sum])
    arrived = xor_permute(near_other, "tensor", size, 1)
    unit_cut = units([near_own, arrived] + sums, share, rank, size)
    unit_all = lax.all_to_all(unit_cut, "tensor", 0, 0, tiled=True)
    part = score(unit_all.reshape(-1, *unit_all.shape[2:]), test_parts, size)
    parts = lax.all_to_all(part, "tensor", 0, 0, tiled=True)
    return functools.reduce(jnp.add, [parts[i] for i in range(size)])


def solution(mesh):
    placed = (
        P(("groups", "dp"), None, "tensor"),
        P(("groups", "dp"), None, "tensor"),
        P("tensor", None),
        P("tensor", None),
        P(("groups", "dp")),
        P(("groups", "dp"), None),
    )
    return jax.shard_map(
        functools.partial(shards, mesh.shape["tensor"], mesh.shape["dp"]),
        mesh=mesh,
        in_specs=placed,
        out_specs=P(("groups", "dp"), None),
        check_vma=False,
    )
```

```python
import functools

import jax
import jax.numpy as jnp
from jax import lax
from jax.experimental import pallas as pl
from jax.experimental.pallas import tpu as pltpu
from jax.sharding import PartitionSpec as P

CORES = 2
AHEAD = 2
NT = (((1,), (1,)), ((), ()))
HBM = pl.BlockSpec(memory_space=pltpu.HBM)
in_hbm = functools.partial(pltpu.with_memory_space_constraint, memory_space=pltpu.HBM)
VMEM = pl.BlockSpec(memory_space=pltpu.VMEM)


def xor_permute(value, axis, size, step):
    return lax.ppermute(value, axis, [(i, i ^ step) for i in range(size)])


def cut_kernel(tests, out, sem):
    width = out.shape[1]
    start = pl.multiple_of(lax.axis_index("tensor") * width, 128)
    copy = pltpu.make_async_copy(tests.at[:, pl.ds(start, width)], out, sem)
    copy.start()
    copy.wait()


def cut_tests(tests, size):
    rows, width = tests.shape
    return pl.pallas_call(
        cut_kernel,
        out_shape=jax.ShapeDtypeStruct((rows, width // size), tests.dtype),
        in_specs=[HBM],
        out_specs=VMEM,
        scratch_shapes=[pltpu.SemaphoreType.DMA],
    )(in_hbm(tests))


def project_kernel(steps, share, block, after, act, og, wi, wo, lens, *refs):
    refs = refs[after:]
    outs, (abuf, obuf, wibuf, wobuf, lenbuf, asem, osem, wsem) = refs[:-8], refs[-8:]
    me = lax.axis_index("tensor")
    rank, feat = wibuf.shape
    hidden = wobuf.shape[1]
    slots = abuf.shape[1]
    count = len(steps) * share
    seqs = [(me ^ step) * share + k for step in steps for k in range(share)]
    small = [
        pltpu.make_async_copy(wi, wibuf, wsem.at[0]),
        pltpu.make_async_copy(wo, wobuf, wsem.at[1]),
        pltpu.make_async_copy(lens, lenbuf, wsem.at[2]),
    ]
    copies = [
        (
            pltpu.make_async_copy(act.at[seq], abuf.at[slot], asem.at[slot]),
            pltpu.make_async_copy(og.at[seq], obuf.at[slot], osem.at[slot]),
        )
        for slot, seq in enumerate(seqs)
    ]
    for copy in small:
        copy.start()
    for slot in range(min(AHEAD * block, count)):
        copies[slot][0].start()
        copies[slot][1].start()
    for copy in small:
        copy.wait()
    col = lax.broadcasted_iota(jnp.int32, (rank, slots), 1)
    per = count // len(outs)
    for first in range(0, count, block):
        here = range(first, first + block)
        for slot in here:
            copies[slot][0].wait()
        tokens = abuf[first : first + block].reshape(block * slots, feat)
        part_in = lax.dot_general(wibuf[...], tokens, NT, preferred_element_type=jnp.float32)
        for slot in here:
            copies[slot][1].wait()
        for slot in here:
            if slot + AHEAD * block < count:
                copies[slot + AHEAD * block][0].start()
                copies[slot + AHEAD * block][1].start()
        tokens = obuf[first : first + block].reshape(block * slots, hidden)
        part_out = lax.dot_general(wobuf[...], tokens, NT, preferred_element_type=jnp.float32)
        for at, slot in enumerate(here):
            length = lenbuf[seqs[slot]]
            out = outs[slot // per]
            one = part_in[:, at * slots : (at + 1) * slots] * (1.0 / length.astype(jnp.float32))
            out[slot % per, :rank] = jnp.where(col < length, one, 0.0)
            out[slot % per, rank:] = part_out[:, at * slots : (at + 1) * slots]


def project(act, og, wi, wo, lens, groups, share, block, after=()):
    steps = [step for group in groups for step in group]
    count = len(steps) * share
    slots, feat, hidden = act.shape[1], act.shape[2], og.shape[2]
    rank = wi.shape[0]
    return pl.pallas_call(
        functools.partial(project_kernel, steps, share, block, len(after)),
        out_shape=[jax.ShapeDtypeStruct((len(group) * share, 2 * rank, slots), jnp.float32) for group in groups],
        in_specs=[HBM] * 5 + [VMEM] * len(after),
        out_specs=[VMEM] * len(groups),
        scratch_shapes=[
            pltpu.VMEM((count, slots, feat), act.dtype),
            pltpu.VMEM((count, slots, hidden), og.dtype),
            pltpu.VMEM((rank, feat), wi.dtype),
            pltpu.VMEM((rank, hidden), wo.dtype),
            pltpu.SMEM(lens.shape, lens.dtype),
            pltpu.SemaphoreType.DMA((count,)),
            pltpu.SemaphoreType.DMA((count,)),
            pltpu.SemaphoreType.DMA((3,)),
        ],
        compiler_params=pltpu.CompilerParams(vmem_limit_bytes=24 << 20),
        cost_estimate=pl.CostEstimate(
            flops=2 * count * slots * (feat + hidden) * 256,
            bytes_accessed=2 * count * slots * (feat + hidden),
            transcendentals=0,
        ),
    )(*map(in_hbm, (act, og, wi, wo, lens)), *after)


def unit_kernel(share, rank, size, *refs):
    singles, parts, outs = refs[:share], refs[share : -2 - size], refs[-2 - size : -2]
    pairs, held = refs[-2:]
    me = lax.axis_index("tensor")
    rows = rank * rank // 128
    span = rows // size
    dot = functools.partial(lax.dot_general, dimension_numbers=NT, preferred_element_type=jnp.float32)
    for k in range(share):
        full = singles[k][0]
        for part in parts:
            full = full + part[k]
        high = full.astype(jnp.bfloat16)
        low = (full - high.astype(jnp.float32)).astype(jnp.bfloat16)
        left, right = slice(None, rank), slice(rank, None)
        pairs[k] = dot(high[left], high[right]) + (dot(high[left], low[right]) + dot(low[left], high[right]))
    for k in range(share):
        even = pairs[k, pl.ds(0, rows, stride=2), :]
        odd = pairs[k, pl.ds(1, rows, stride=2), :]
        flat = jnp.concatenate([even, odd], axis=1)
        scale = jnp.sqrt(jnp.sum(flat * flat) / (rank * rank) + 1e-06)
        unit = flat / scale
        for to in range(size):
            held[to] = unit[to * span : (to + 1) * span]
        for step in range(size):
            outs[step][k] = held[me ^ step]


def units(parts, singles, share, rank, size):
    span = rank * rank // 128 // size
    return pl.pallas_call(
        functools.partial(unit_kernel, share, rank, size),
        out_shape=[jax.ShapeDtypeStruct((share, span, 128), jnp.float32)] * size,
        in_specs=[VMEM] * (share + len(parts)),
        out_specs=[VMEM] * size,
        scratch_shapes=[pltpu.VMEM((share, rank, rank), jnp.float32), pltpu.VMEM((size, span, 128), jnp.float32)],
    )(*singles, *parts)


def score_kernel(share, size, *refs):
    unit_refs, test_refs, out, held = refs[:size], refs[size:-2], refs[-2], refs[-1]
    me, dp = lax.axis_index("tensor"), lax.axis_index("dp")
    for step in range(size):
        for k in range(share):
            held[(me ^ step) * share + k] = unit_refs[step][k]
    unit = jnp.concatenate([held[:, c, :] for c in range(held.shape[1])], axis=1).astype(jnp.bfloat16)
    tests = test_refs[0].shape[0]
    for step, test_ref in enumerate(test_refs):
        part = lax.dot_general(unit, test_ref[...], NT, preferred_element_type=jnp.float32)
        out[:, pl.ds(pl.multiple_of((dp ^ step) * tests, 128), tests)] = part


def score(unit_parts, test_parts, share):
    size, groups = len(unit_parts), len(test_parts)
    tests, width = test_parts[0].shape
    return pl.pallas_call(
        functools.partial(score_kernel, share, size),
        out_shape=jax.ShapeDtypeStruct((share * size, tests * groups), jnp.float32),
        in_specs=[VMEM] * (size + groups),
        out_specs=VMEM,
        scratch_shapes=[pltpu.VMEM((share * size, width // 128, 128), jnp.float32)],
    )(*unit_parts, *test_parts)


def gather_tests(own, groups):
    if groups == 4:
        across = xor_permute(own, "dp", groups, 3)
        beside = xor_permute(own, "dp", groups, 1)
        return [own, beside, xor_permute(across, "dp", groups, 1), across]
    return [own] + [xor_permute(own, "dp", groups, step) for step in range(1, groups)]


def shards(size, groups, activations, out_grads, proj_in, proj_out, lengths, test_grads):
    rank = proj_in.shape[1]
    share = activations.shape[0] // size
    own_tests = cut_tests(test_grads, size)
    test_parts = gather_tests(own_tests, groups)

    far = [CORES * x for x in range(1, size // CORES)]
    arrays = (activations, out_grads, proj_in.T, proj_out.T, lengths)
    far_other, far_own = project(*arrays, [[step ^ 1 for step in far], far], share, 1, [own_tests])
    far_sum = far_own + xor_permute(far_other, "tensor", size, 1)
    sums = [xor_permute(far_sum[i * share : (i + 1) * share], "tensor", size, step) for i, step in enumerate(far)]
    near_other, near_own = project(*arrays, [[1], [0]], share, share, [far_sum])
    arrived = [xor_permute(near_other[k : k + 1], "tensor", size, 1) for k in range(share)]
    unit_outs = units([near_own] + sums, arrived, share, rank, size)
    unit_parts = [unit_outs[0]] + [xor_permute(unit_outs[step], "tensor", size, step) for step in range(1, size)]
    part = score(unit_parts, test_parts, share)
    parts = [part] + [xor_permute(part, "tensor", size, step) for step in range(1, size)]
    while len(parts) > 1:
        parts = [parts[i] + parts[i + 1] for i in range(0, len(parts), 2)]
    return parts[0]


def solution(mesh):
    placed = (
        P(("groups", "dp"), None, "tensor"),
        P(("groups", "dp"), None, "tensor"),
        P("tensor", None),
        P("tensor", None),
        P(("groups", "dp")),
        P(("groups", "dp"), None),
    )
    return jax.shard_map(
        functools.partial(shards, mesh.shape["tensor"], mesh.shape["dp"]),
        mesh=mesh,
        in_specs=placed,
        out_specs=P(("groups", "dp"), None),
        check_vma=False,
    )
```

```python
import functools

import jax
import jax.numpy as jnp
from jax import lax
from jax.experimental import pallas as pl
from jax.experimental.pallas import tpu as pltpu
from jax.sharding import PartitionSpec as P

CORES = 2
PIECE = 512
AHEAD = 4
SMALL = pltpu.CompilerParams(vmem_limit_bytes=8 << 20)
NT = (((1,), (1,)), ((), ()))
HBM = pl.BlockSpec(memory_space=pltpu.HBM)
in_hbm = functools.partial(pltpu.with_memory_space_constraint, memory_space=pltpu.HBM)
VMEM = pl.BlockSpec(memory_space=pltpu.VMEM)


def xor_permute(value, axis, size, step):
    return lax.ppermute(value, axis, [(i, i ^ step) for i in range(size)])


def cut_kernel(tests, out, sem):
    width = out.shape[1]
    start = pl.multiple_of(lax.axis_index("tensor") * width, 128)
    copy = pltpu.make_async_copy(tests.at[:, pl.ds(start, width)], out, sem)
    copy.start()
    copy.wait()


def cut_tests(tests, size):
    rows, width = tests.shape
    return pl.pallas_call(
        cut_kernel,
        out_shape=jax.ShapeDtypeStruct((rows, width // size), tests.dtype),
        in_specs=[HBM],
        out_specs=VMEM,
        scratch_shapes=[pltpu.SemaphoreType.DMA],
        compiler_params=SMALL,
    )(in_hbm(tests))


COST = 1 << 32


def project_kernel(steps, share, rows_first, after, act, og, wi, wo, lens, *refs):
    refs = refs[after:]
    outs, (buf, wibuf, wobuf, lenbuf, sem, wsem) = refs[:-6], refs[-6:]
    me = lax.axis_index("tensor")
    rank = wibuf.shape[0]
    slots = buf.shape[2]
    count = len(steps) * share
    tokens = count * slots
    small = [
        pltpu.make_async_copy(wi, wibuf, wsem.at[0]),
        pltpu.make_async_copy(wo, wobuf, wsem.at[1]),
        pltpu.make_async_copy(lens, lenbuf, wsem.at[2]),
    ]
    pieces = [(side, at) for side, ref in enumerate((act, og)) for at in range(0, ref.shape[2], PIECE)]
    copies = []
    for slot, (side, at) in enumerate(pieces):
        width = min(PIECE, (act, og)[side].shape[2] - at)
        copies.append(
            [
                pltpu.make_async_copy(
                    (act, og)[side].at[pl.ds((me ^ step) * share, share), :, pl.ds(at, width)],
                    buf.at[slot, pl.ds(i * share, share), :, pl.ds(0, width)],
                    sem.at[slot, i],
                )
                for i, step in enumerate(steps)
            ]
        )
    small[0].start()
    for slot, group in enumerate(copies):
        if slot == 1:
            small[1].start()
            small[2].start()
        if slot < AHEAD:
            for copy in group:
                copy.start()
    sums = [None, None]
    for slot, (side, at) in enumerate(pieces):
        if at == 0:
            small[side].wait()
        for copy in copies[slot]:
            copy.wait()
        if slot + AHEAD < len(pieces):
            for copy in copies[slot + AHEAD]:
                copy.start()
        weight = (wibuf, wobuf)[side][:, at : at + PIECE]
        token = buf[slot].reshape(tokens, PIECE)[:, : weight.shape[1]]
        pair = (token, weight) if rows_first else (weight, token)
        part = lax.dot_general(*pair, NT, preferred_element_type=jnp.float32)
        sums[side] = part if sums[side] is None else sums[side] + part
    if rows_first:
        sums = [one.T for one in sums]
    small[2].wait()
    col = lax.broadcasted_iota(jnp.int32, (rank, slots), 1)
    per = count // len(outs)
    for slot in range(count):
        length = lenbuf[(me ^ steps[slot // share]) * share + slot % share]
        out = outs[slot // per]
        one = sums[0][:, slot * slots : (slot + 1) * slots] * (1.0 / length.astype(jnp.float32))
        out[slot % per, :rank] = jnp.where(col < length, one, 0.0)
        out[slot % per, rank:] = sums[1][:, slot * slots : (slot + 1) * slots]


def project(act, og, wi, wo, lens, groups, share, rows_first, cost, after=()):
    steps = [step for group in groups for step in group]
    count = len(steps) * share
    slots, feat, hidden = act.shape[1], act.shape[2], og.shape[2]
    rank = wi.shape[0]
    pieces = -(-feat // PIECE) - (-hidden // PIECE)
    return pl.pallas_call(
        functools.partial(project_kernel, steps, share, rows_first, len(after)),
        out_shape=[jax.ShapeDtypeStruct((len(group) * share, 2 * rank, slots), jnp.float32) for group in groups],
        in_specs=[HBM] * 5 + [VMEM] * len(after),
        out_specs=[VMEM] * len(groups),
        scratch_shapes=[
            pltpu.VMEM((pieces, count, slots, PIECE), act.dtype),
            pltpu.VMEM((rank, feat), wi.dtype),
            pltpu.VMEM((rank, hidden), wo.dtype),
            pltpu.SMEM(lens.shape, lens.dtype),
            pltpu.SemaphoreType.DMA((pieces, len(steps))),
            pltpu.SemaphoreType.DMA((3,)),
        ],
        compiler_params=pltpu.CompilerParams(vmem_limit_bytes=32 << 20),
        cost_estimate=pl.CostEstimate(flops=cost, bytes_accessed=cost // 256, transcendentals=0),
    )(*map(in_hbm, (act, og, wi, wo, lens)), *after)


def unit_kernel(share, rank, size, *refs):
    singles, parts, outs = refs[:share], refs[share : -2 - size], refs[-2 - size : -2]
    pairs, held = refs[-2:]
    me = lax.axis_index("tensor")
    rows = rank * rank // 128
    span = rows // size
    dot = functools.partial(lax.dot_general, dimension_numbers=NT, preferred_element_type=jnp.float32)
    for k in range(share):
        full = singles[k][0]
        for part in parts:
            full = full + part[k]
        high = full.astype(jnp.bfloat16)
        low = (full - high.astype(jnp.float32)).astype(jnp.bfloat16)
        left, right = slice(None, rank), slice(rank, None)
        pairs[k] = dot(high[left], high[right]) + (dot(high[left], low[right]) + dot(low[left], high[right]))
    for k in range(share):
        even = pairs[k, pl.ds(0, rows, stride=2), :]
        odd = pairs[k, pl.ds(1, rows, stride=2), :]
        flat = jnp.concatenate([even, odd], axis=1)
        scale = jnp.sqrt(jnp.sum(flat * flat) / (rank * rank) + 1e-06)
        unit = flat / scale
        for to in range(size):
            held[to] = unit[to * span : (to + 1) * span]
        for step in range(size):
            outs[step][k] = held[me ^ step]


def units(parts, singles, share, rank, size):
    span = rank * rank // 128 // size
    return pl.pallas_call(
        functools.partial(unit_kernel, share, rank, size),
        out_shape=[jax.ShapeDtypeStruct((share, span, 128), jnp.float32)] * size,
        in_specs=[VMEM] * (share + len(parts)),
        out_specs=[VMEM] * size,
        scratch_shapes=[pltpu.VMEM((share, rank, rank), jnp.float32), pltpu.VMEM((size, span, 128), jnp.float32)],
        compiler_params=SMALL,
    )(*singles, *parts)


def score_kernel(share, size, shifts, *refs):
    unit_refs, test_refs, out, held = refs[:size], refs[size:-2], refs[-2], refs[-1]
    me, dp = lax.axis_index("tensor"), lax.axis_index("dp")
    for step in range(size):
        for k in range(share):
            held[(me ^ step) * share + k] = unit_refs[step][k]
    unit = jnp.concatenate([held[:, c, :] for c in range(held.shape[1])], axis=1).astype(jnp.bfloat16)
    tests = test_refs[0].shape[0]
    for step, test_ref in zip(shifts, test_refs):
        part = lax.dot_general(unit, test_ref[...], NT, preferred_element_type=jnp.float32)
        at = lax.rem(dp - step + len(shifts), len(shifts)) * tests
        out[:, pl.ds(pl.multiple_of(at, 128), tests)] = part


def score(unit_parts, test_parts, share):
    size, groups = len(unit_parts), len(test_parts)
    tests, width = test_parts[0].shape
    shifts = tuple(test_parts)
    return pl.pallas_call(
        functools.partial(score_kernel, share, size, shifts),
        out_shape=jax.ShapeDtypeStruct((share * size, tests * groups), jnp.float32),
        in_specs=[VMEM] * (size + groups),
        out_specs=VMEM,
        scratch_shapes=[pltpu.VMEM((share * size, width // 128, 128), jnp.float32)],
        compiler_params=SMALL,
    )(*unit_parts, *test_parts.values())


def shift(value, axis, size, step):
    return lax.ppermute(value, axis, [(i, (i + step) % size) for i in range(size)])


def shards(size, groups, activations, out_grads, proj_in, proj_out, lengths, test_grads):
    rank = proj_in.shape[1]
    share = activations.shape[0] // size
    own_tests = cut_tests(test_grads, size)
    tests = {0: own_tests, 1: shift(own_tests, "dp", groups, 1)}
    if groups == 4:
        tests[3] = shift(own_tests, "dp", groups, 3)
        tests[2] = shift(tests[1], "dp", groups, 1)
    else:
        tests.update({step: shift(own_tests, "dp", groups, step) for step in range(2, groups)})

    far = [CORES * x for x in range(1, size // CORES)]
    arrays = (activations, out_grads, proj_in.T, proj_out.T, lengths)
    far_other, far_own = project(*arrays, [[step ^ 1 for step in far], far], share, False, COST, [own_tests])
    far_sum = far_own + xor_permute(far_other, "tensor", size, 1)
    sums = [xor_permute(far_sum[i * share : (i + 1) * share], "tensor", size, step) for i, step in enumerate(far)]
    near_other, near_own = project(*arrays, [[1], [0]], share, True, COST, [far_sum])
    arrived = [xor_permute(near_other[k : k + 1], "tensor", size, 1) for k in range(share)]
    unit_outs = units([near_own] + sums, arrived, share, rank, size)
    unit_parts = [unit_outs[0]] + [xor_permute(unit_outs[step], "tensor", size, step) for step in range(1, size)]
    part = score(unit_parts, tests, share)
    parts = [part] + [xor_permute(part, "tensor", size, step) for step in range(1, size)]
    while len(parts) > 1:
        parts = [parts[i] + parts[i + 1] for i in range(0, len(parts), 2)]
    return parts[0]


def solution(mesh):
    placed = (
        P(("groups", "dp"), None, "tensor"),
        P(("groups", "dp"), None, "tensor"),
        P("tensor", None),
        P("tensor", None),
        P(("groups", "dp")),
        P(("groups", "dp"), None),
    )
    return jax.shard_map(
        functools.partial(shards, mesh.shape["tensor"], mesh.shape["dp"]),
        mesh=mesh,
        in_specs=placed,
        out_specs=P(("groups", "dp"), None),
        check_vma=False,
    )
```

```python
import functools

import jax
import jax.numpy as jnp
from jax import lax
from jax.experimental import pallas as pl
from jax.experimental.pallas import tpu as pltpu
from jax.sharding import PartitionSpec as P

CORES = 2
PIECE = 512
AHEAD = 4
SMALL = pltpu.CompilerParams(vmem_limit_bytes=8 << 20)
NT = (((1,), (1,)), ((), ()))
NN = (((1,), (0,)), ((), ()))
HBM = pl.BlockSpec(memory_space=pltpu.HBM)
in_hbm = functools.partial(pltpu.with_memory_space_constraint, memory_space=pltpu.HBM)
VMEM = pl.BlockSpec(memory_space=pltpu.VMEM)


def xor_permute(value, axis, size, step):
    return lax.ppermute(value, axis, [(i, i ^ step) for i in range(size)])


def cut_kernel(tests, out, sem):
    width = out.shape[1]
    start = pl.multiple_of(lax.axis_index("tensor") * width, 128)
    copy = pltpu.make_async_copy(tests.at[:, pl.ds(start, width)], out, sem)
    copy.start()
    copy.wait()


def cut_tests(tests, size):
    rows, width = tests.shape
    return pl.pallas_call(
        cut_kernel,
        out_shape=jax.ShapeDtypeStruct((rows, width // size), tests.dtype),
        in_specs=[HBM],
        out_specs=VMEM,
        scratch_shapes=[pltpu.SemaphoreType.DMA],
        compiler_params=SMALL,
    )(in_hbm(tests))


COST = 1 << 32


def project_kernel(steps, share, rows_first, ahead, after, act, og, wi, wo, lens, *refs):
    refs = refs[after:]
    outs, (buf, wibuf, wobuf, lenbuf, sem, wsem) = refs[:-6], refs[-6:]
    me = lax.axis_index("tensor")
    rank = wibuf.shape[0]
    slots = buf.shape[2]
    count = len(steps) * share
    tokens = count * slots
    small = [
        pltpu.make_async_copy(wi, wibuf, wsem.at[0]),
        pltpu.make_async_copy(wo, wobuf, wsem.at[1]),
        pltpu.make_async_copy(lens, lenbuf, wsem.at[2]),
    ]
    pieces = [(side, at) for side, ref in enumerate((act, og)) for at in range(0, ref.shape[2], PIECE)]
    copies = []
    for slot, (side, at) in enumerate(pieces):
        width = min(PIECE, (act, og)[side].shape[2] - at)
        copies.append(
            [
                pltpu.make_async_copy(
                    (act, og)[side].at[pl.ds((me ^ step) * share, share), :, pl.ds(at, width)],
                    buf.at[slot, pl.ds(i * share, share), :, pl.ds(0, width)],
                    sem.at[slot, i],
                )
                for i, step in enumerate(steps)
            ]
        )
    small[0].start()
    for slot, group in enumerate(copies):
        if slot == 1:
            small[1].start()
            small[2].start()
        if slot < ahead:
            for copy in group:
                copy.start()
    sums = [None, None]
    for slot, (side, at) in enumerate(pieces):
        if at == 0:
            small[side].wait()
        for copy in copies[slot]:
            copy.wait()
        if slot + ahead < len(pieces):
            for copy in copies[slot + ahead]:
                copy.start()
        weight = (wibuf, wobuf)[side][:, at : at + PIECE]
        token = buf[slot].reshape(tokens, PIECE)[:, : weight.shape[1]]
        if rows_first:
            none = jnp.zeros_like(weight)
            wide = jnp.concatenate([none, weight] if side else [weight, none], axis=0).T
            half = tokens // 2
            part = [
                lax.dot_general(token[i * half : (i + 1) * half], wide, NN, preferred_element_type=jnp.float32)
                for i in range(2)
            ]
            sums = part if slot == 0 else [sums[0] + part[0], sums[1] + part[1]]
        else:
            part = lax.dot_general(weight, token, NT, preferred_element_type=jnp.float32)
            sums[side] = part if sums[side] is None else sums[side] + part
    if rows_first:
        whole = jnp.concatenate([one.T for one in sums], axis=1)
        sums = [whole[:rank], whole[rank:]]
    small[2].wait()
    col = lax.broadcasted_iota(jnp.int32, (rank, slots), 1)
    per = count // len(outs)
    for slot in range(count):
        length = lenbuf[(me ^ steps[slot // share]) * share + slot % share]
        out = outs[slot // per]
        one = sums[0][:, slot * slots : (slot + 1) * slots] * (1.0 / length.astype(jnp.float32))
        out[slot % per, :rank] = jnp.where(col < length, one, 0.0)
        out[slot % per, rank:] = sums[1][:, slot * slots : (slot + 1) * slots]


def project(act, og, wi, wo, lens, groups, share, rows_first, ahead, after=()):
    steps = [step for group in groups for step in group]
    count = len(steps) * share
    slots, feat, hidden = act.shape[1], act.shape[2], og.shape[2]
    rank = wi.shape[0]
    pieces = -(-feat // PIECE) - (-hidden // PIECE)
    return pl.pallas_call(
        functools.partial(project_kernel, steps, share, rows_first, ahead, len(after)),
        out_shape=[jax.ShapeDtypeStruct((len(group) * share, 2 * rank, slots), jnp.float32) for group in groups],
        in_specs=[HBM] * 5 + [VMEM] * len(after),
        out_specs=[VMEM] * len(groups),
        scratch_shapes=[
            pltpu.VMEM((pieces, count, slots, PIECE), act.dtype),
            pltpu.VMEM((rank, feat), wi.dtype),
            pltpu.VMEM((rank, hidden), wo.dtype),
            pltpu.SMEM(lens.shape, lens.dtype),
            pltpu.SemaphoreType.DMA((pieces, len(steps))),
            pltpu.SemaphoreType.DMA((3,)),
        ],
        compiler_params=pltpu.CompilerParams(vmem_limit_bytes=32 << 20),
        cost_estimate=pl.CostEstimate(flops=COST, bytes_accessed=COST // 256, transcendentals=0),
    )(*map(in_hbm, (act, og, wi, wo, lens)), *after)


def unit_kernel(share, rank, size, *refs):
    singles, parts, outs = refs[:share], refs[share : -2 - size], refs[-2 - size : -2]
    pairs, held = refs[-2:]
    me = lax.axis_index("tensor")
    rows = rank * rank // 128
    span = rows // size
    dot = functools.partial(lax.dot_general, dimension_numbers=NT, preferred_element_type=jnp.float32)
    for k in range(share):
        full = singles[k][0]
        for part in parts:
            full = full + part[k]
        high = full.astype(jnp.bfloat16)
        low = (full - high.astype(jnp.float32)).astype(jnp.bfloat16)
        left, right = slice(None, rank), slice(rank, None)
        pairs[k] = dot(high[left], high[right]) + (dot(high[left], low[right]) + dot(low[left], high[right]))
    for k in range(share):
        even = pairs[k, pl.ds(0, rows, stride=2), :]
        odd = pairs[k, pl.ds(1, rows, stride=2), :]
        flat = jnp.concatenate([even, odd], axis=1)
        scale = jnp.sqrt(jnp.sum(flat * flat) / (rank * rank) + 1e-06)
        unit = flat / scale
        for to in range(size):
            held[to] = unit[to * span : (to + 1) * span]
        for step in range(size):
            outs[step][k] = held[me ^ step]


def units(parts, singles, share, rank, size):
    span = rank * rank // 128 // size
    return pl.pallas_call(
        functools.partial(unit_kernel, share, rank, size),
        out_shape=[jax.ShapeDtypeStruct((share, span, 128), jnp.float32)] * size,
        in_specs=[VMEM] * (share + len(parts)),
        out_specs=[VMEM] * size,
        scratch_shapes=[pltpu.VMEM((share, rank, rank), jnp.float32), pltpu.VMEM((size, span, 128), jnp.float32)],
        compiler_params=SMALL,
    )(*singles, *parts)


def score_kernel(share, size, shifts, *refs):
    unit_refs, test_refs, out, held = refs[:size], refs[size:-2], refs[-2], refs[-1]
    me, dp = lax.axis_index("tensor"), lax.axis_index("dp")
    for step in range(size):
        for k in range(share):
            held[(me ^ step) * share + k] = unit_refs[step][k]
    unit = jnp.concatenate([held[:, c, :] for c in range(held.shape[1])], axis=1).astype(jnp.bfloat16)
    tests = test_refs[0].shape[0]
    for step, test_ref in zip(shifts, test_refs):
        part = lax.dot_general(unit, test_ref[...], NT, preferred_element_type=jnp.float32)
        at = lax.rem(dp - step + len(shifts), len(shifts)) * tests
        out[:, pl.ds(pl.multiple_of(at, 128), tests)] = part


def score(unit_parts, test_parts, share):
    size, groups = len(unit_parts), len(test_parts)
    tests, width = test_parts[0].shape
    shifts = tuple(test_parts)
    return pl.pallas_call(
        functools.partial(score_kernel, share, size, shifts),
        out_shape=jax.ShapeDtypeStruct((share * size, tests * groups), jnp.float32),
        in_specs=[VMEM] * (size + groups),
        out_specs=VMEM,
        scratch_shapes=[pltpu.VMEM((share * size, width // 128, 128), jnp.float32)],
        compiler_params=SMALL,
    )(*unit_parts, *test_parts.values())


def shift(value, axis, size, step):
    return lax.ppermute(value, axis, [(i, (i + step) % size) for i in range(size)])


def shards(size, groups, activations, out_grads, proj_in, proj_out, lengths, test_grads):
    rank = proj_in.shape[1]
    share = activations.shape[0] // size
    own_tests = cut_tests(test_grads, size)
    tests = {0: own_tests, 1: shift(own_tests, "dp", groups, 1)}
    if groups == 4:
        tests[3] = shift(own_tests, "dp", groups, 3)
        tests[2] = shift(tests[1], "dp", groups, 1)
    else:
        tests.update({step: shift(own_tests, "dp", groups, step) for step in range(2, groups)})

    far = [CORES * x for x in range(1, size // CORES)]
    arrays = (activations, out_grads, proj_in.T, proj_out.T, lengths)
    far_other, far_own = project(*arrays, [[step ^ 1 for step in far], far], share, False, 9, [own_tests])
    far_other = far_other + 0.0 * tests[1][0, 0].astype(jnp.float32)
    far_sum = far_own + xor_permute(far_other, "tensor", size, 1)
    sums = [xor_permute(far_sum[i * share : (i + 1) * share], "tensor", size, step) for i, step in enumerate(far)]
    near_other, near_own = project(*arrays, [[1], [0]], share, True, 4, [far_sum, tests[1]])
    arrived = [xor_permute(near_other[k : k + 1], "tensor", size, 1) for k in range(share)]
    unit_outs = units([near_own] + sums, arrived, share, rank, size)
    unit_parts = [unit_outs[0]] + [xor_permute(unit_outs[step], "tensor", size, step) for step in range(1, size)]
    part = score(unit_parts, tests, share)
    parts = [part] + [xor_permute(part, "tensor", size, step) for step in range(1, size)]
    while len(parts) > 1:
        parts = [parts[i] + parts[i + 1] for i in range(0, len(parts), 2)]
    return parts[0]


def solution(mesh):
    placed = (
        P(("groups", "dp"), None, "tensor"),
        P(("groups", "dp"), None, "tensor"),
        P("tensor", None),
        P("tensor", None),
        P(("groups", "dp")),
        P(("groups", "dp"), None),
    )
    return jax.shard_map(
        functools.partial(shards, mesh.shape["tensor"], mesh.shape["dp"]),
        mesh=mesh,
        in_specs=placed,
        out_specs=P(("groups", "dp"), None),
        check_vma=False,
    )
```

```python
import functools

import jax
import jax.numpy as jnp
from jax import lax
from jax.experimental import pallas as pl
from jax.experimental.pallas import tpu as pltpu
from jax.sharding import PartitionSpec as P

CORES = 2
SMALL = pltpu.CompilerParams(vmem_limit_bytes=8 << 20)
NT = (((1,), (1,)), ((), ()))
NN = (((1,), (0,)), ((), ()))
HBM = pl.BlockSpec(memory_space=pltpu.HBM)
in_hbm = functools.partial(pltpu.with_memory_space_constraint, memory_space=pltpu.HBM)
VMEM = pl.BlockSpec(memory_space=pltpu.VMEM)


def xor_permute(value, axis, size, step):
    return lax.ppermute(value, axis, [(i, i ^ step) for i in range(size)])


def cut_kernel(tests, out, sem):
    width = out.shape[1]
    start = pl.multiple_of(lax.axis_index("tensor") * width, 128)
    copy = pltpu.make_async_copy(tests.at[:, pl.ds(start, width)], out, sem)
    copy.start()
    copy.wait()


def cut_tests(tests, size):
    rows, width = tests.shape
    return pl.pallas_call(
        cut_kernel,
        out_shape=jax.ShapeDtypeStruct((rows, width // size), tests.dtype),
        in_specs=[HBM],
        out_specs=VMEM,
        scratch_shapes=[pltpu.SemaphoreType.DMA],
        compiler_params=SMALL,
    )(in_hbm(tests))


COST = 1 << 32


def project_kernel(steps, share, rows_first, ahead, piece, after, act, og, wi, wo, lens, *refs):
    refs = refs[after:]
    outs, (buf, wibuf, wobuf, lenbuf, sem, wsem) = refs[:-6], refs[-6:]
    me = lax.axis_index("tensor")
    rank = wibuf.shape[0]
    slots = buf.shape[2]
    count = len(steps) * share
    tokens = count * slots
    small = [
        pltpu.make_async_copy(wi, wibuf, wsem.at[0]),
        pltpu.make_async_copy(wo, wobuf, wsem.at[1]),
        pltpu.make_async_copy(lens, lenbuf, wsem.at[2]),
    ]
    pieces = [(side, at) for side, ref in enumerate((act, og)) for at in range(0, ref.shape[2], piece)]
    copies = []
    for slot, (side, at) in enumerate(pieces):
        width = min(piece, (act, og)[side].shape[2] - at)
        copies.append(
            [
                pltpu.make_async_copy(
                    (act, og)[side].at[pl.ds((me ^ step) * share, share), :, pl.ds(at, width)],
                    buf.at[slot, pl.ds(i * share, share), :, pl.ds(0, width)],
                    sem.at[slot, i],
                )
                for i, step in enumerate(steps)
            ]
        )
    small[0].start()
    for slot, group in enumerate(copies):
        if slot == 1:
            small[1].start()
            small[2].start()
        if slot < ahead:
            for copy in group:
                copy.start()
    sums = [None, None]
    for slot, (side, at) in enumerate(pieces):
        if at == 0:
            small[side].wait()
        for copy in copies[slot]:
            copy.wait()
        if slot + ahead < len(pieces):
            for copy in copies[slot + ahead]:
                copy.start()
        weight = (wibuf, wobuf)[side][:, at : at + piece]
        token = buf[slot].reshape(tokens, piece)[:, : weight.shape[1]]
        if rows_first:
            none = jnp.zeros_like(weight)
            wide = jnp.concatenate([none, weight] if side else [weight, none], axis=0).T
            half = tokens // 2
            part = [
                lax.dot_general(token[i * half : (i + 1) * half], wide, NN, preferred_element_type=jnp.float32)
                for i in range(2)
            ]
            sums = part if slot == 0 else [sums[0] + part[0], sums[1] + part[1]]
        else:
            part = lax.dot_general(weight, token, NT, preferred_element_type=jnp.float32)
            sums[side] = part if sums[side] is None else sums[side] + part
    if rows_first:
        whole = jnp.concatenate([one.T for one in sums], axis=1)
        sums = [whole[:rank], whole[rank:]]
    small[2].wait()
    col = lax.broadcasted_iota(jnp.int32, (rank, slots), 1)
    per = count // len(outs)
    for slot in range(count):
        length = lenbuf[(me ^ steps[slot // share]) * share + slot % share]
        out = outs[slot // per]
        one = sums[0][:, slot * slots : (slot + 1) * slots] * (1.0 / length.astype(jnp.float32))
        out[slot % per, :rank] = jnp.where(col < length, one, 0.0)
        out[slot % per, rank:] = sums[1][:, slot * slots : (slot + 1) * slots]


def project(act, og, wi, wo, lens, groups, share, rows_first, ahead, piece, after=()):
    steps = [step for group in groups for step in group]
    count = len(steps) * share
    slots, feat, hidden = act.shape[1], act.shape[2], og.shape[2]
    rank = wi.shape[0]
    pieces = -(-feat // piece) - (-hidden // piece)
    return pl.pallas_call(
        functools.partial(project_kernel, steps, share, rows_first, ahead, piece, len(after)),
        out_shape=[jax.ShapeDtypeStruct((len(group) * share, 2 * rank, slots), jnp.float32) for group in groups],
        in_specs=[HBM] * 5 + [VMEM] * len(after),
        out_specs=[VMEM] * len(groups),
        scratch_shapes=[
            pltpu.VMEM((pieces, count, slots, piece), act.dtype),
            pltpu.VMEM((rank, feat), wi.dtype),
            pltpu.VMEM((rank, hidden), wo.dtype),
            pltpu.SMEM(lens.shape, lens.dtype),
            pltpu.SemaphoreType.DMA((pieces, len(steps))),
            pltpu.SemaphoreType.DMA((3,)),
        ],
        compiler_params=pltpu.CompilerParams(vmem_limit_bytes=32 << 20),
        cost_estimate=pl.CostEstimate(flops=COST, bytes_accessed=COST // 256, transcendentals=0),
    )(*map(in_hbm, (act, og, wi, wo, lens)), *after)


def unit_kernel(share, rank, size, *refs):
    parts, outs, pairs, held = refs[:-4], refs[-4:-2], refs[-2], refs[-1]
    me = lax.axis_index("tensor")
    rows = rank * rank // 128
    span = rows // size
    dot = functools.partial(lax.dot_general, dimension_numbers=NT, preferred_element_type=jnp.float32)
    for k in range(share):
        full = parts[0][k]
        for part in parts[1:]:
            full = full + part[k]
        high = full.astype(jnp.bfloat16)
        low = (full - high.astype(jnp.float32)).astype(jnp.bfloat16)
        left, right = slice(None, rank), slice(rank, None)
        pairs[k] = dot(high[left], high[right]) + (dot(high[left], low[right]) + dot(low[left], high[right]))
    for k in range(share):
        even = pairs[k, pl.ds(0, rows, stride=2), :]
        odd = pairs[k, pl.ds(1, rows, stride=2), :]
        flat = jnp.concatenate([even, odd], axis=1)
        scale = jnp.sqrt(jnp.sum(flat * flat) / (rank * rank) + 1e-06)
        unit = flat / scale
        for to in range(size):
            held[to, k] = unit[to * span : (to + 1) * span]
    for j in range(size // CORES):
        for core in range(CORES):
            outs[core][j] = held[me ^ core ^ (CORES * j)]


def units(parts, share, rank, size):
    span = rank * rank // 128 // size
    return pl.pallas_call(
        functools.partial(unit_kernel, share, rank, size),
        out_shape=[jax.ShapeDtypeStruct((size // CORES, share, span, 128), jnp.float32)] * CORES,
        in_specs=[VMEM] * len(parts),
        out_specs=[VMEM] * CORES,
        scratch_shapes=[pltpu.VMEM((share, rank, rank), jnp.float32), pltpu.VMEM((size, share, span, 128), jnp.float32)],
        compiler_params=SMALL,
    )(*parts)


def score_kernel(share, far, shifts, own_ref, core_ref, *refs):
    far_refs, test_refs, out, held = refs[: len(far)], refs[len(far) : -2], refs[-2], refs[-1]
    me, dp = lax.axis_index("tensor"), lax.axis_index("dp")
    blocks = [(me, own_ref.at[0]), (me ^ 1, core_ref.at[0])]
    blocks += [(me ^ step ^ core, ref.at[core]) for step, ref in zip(far, far_refs) for core in range(CORES)]
    for owner, ref in blocks:
        for k in range(share):
            held[owner * share + k] = ref[k]
    unit = jnp.concatenate([held[:, c, :] for c in range(held.shape[1])], axis=1).astype(jnp.bfloat16)
    tests = test_refs[0].shape[0]
    for step, test_ref in zip(shifts, test_refs):
        part = lax.dot_general(unit, test_ref[...], NT, preferred_element_type=jnp.float32)
        at = lax.rem(dp - step + len(shifts), len(shifts)) * tests
        out[:, pl.ds(pl.multiple_of(at, 128), tests)] = part


def score(own, core, far_units, test_parts, share, size):
    tests, width = test_parts[0].shape
    return pl.pallas_call(
        functools.partial(score_kernel, share, tuple(far_units), tuple(test_parts)),
        out_shape=jax.ShapeDtypeStruct((share * size, tests * len(test_parts)), jnp.float32),
        in_specs=[VMEM] * (2 + len(far_units) + len(test_parts)),
        out_specs=VMEM,
        scratch_shapes=[pltpu.VMEM((share * size, width // 128, 128), jnp.float32)],
        compiler_params=SMALL,
    )(own, core, *far_units.values(), *test_parts.values())


def shift(value, axis, size, step):
    return lax.ppermute(value, axis, [(i, (i + step) % size) for i in range(size)])


def shards(size, groups, activations, out_grads, proj_in, proj_out, lengths, test_grads):
    rank = proj_in.shape[1]
    share = activations.shape[0] // size
    own_tests = cut_tests(test_grads, size)
    tests = {0: own_tests, 1: shift(own_tests, "dp", groups, 1)}
    if groups == 4:
        tests[2] = shift(tests[1], "dp", groups, 1)
        tests[3] = shift(own_tests, "dp", groups, 3)
    else:
        tests.update({step: shift(own_tests, "dp", groups, step) for step in range(2, groups)})

    far = [CORES * x for x in range(1, size // CORES)]
    arrays = (activations, out_grads, proj_in.T, proj_out.T, lengths)
    far_other, far_own = project(*arrays, [[step ^ 1 for step in far], far], share, False, 4, 512, [own_tests])
    slots = far_other.shape[2]
    far_other = far_other + 0.0 * tests[1][:1, :slots].astype(jnp.float32)
    far_sum = far_own + xor_permute(far_other, "tensor", size, 1)
    sums = [xor_permute(far_sum[i * share : (i + 1) * share], "tensor", size, step) for i, step in enumerate(far)]
    near_other = project(*arrays, [[1]], share, False, 4, 1024, [far_sum, tests[1]])[0]
    arrived = xor_permute(near_other, "tensor", size, 1)
    near_own = project(*arrays, [[0]], share, False, 4, 1024, [near_other])[0]

    own, core = units([near_own, arrived] + sums, share, rank, size)
    core = xor_permute(core, "tensor", size, 1)
    far_units = {
        step: xor_permute(jnp.stack([own[j + 1], core[j + 1]]), "tensor", size, step) for j, step in enumerate(far)
    }
    part = score(own, core, far_units, tests, share, size)
    part = part + xor_permute(part, "tensor", size, 1)
    parts = [part] + [xor_permute(part, "tensor", size, step) for step in far]
    while len(parts) > 1:
        parts = [parts[i] + parts[i + 1] for i in range(0, len(parts), 2)]
    return parts[0]


def solution(mesh):
    placed = (
        P(("groups", "dp"), None, "tensor"),
        P(("groups", "dp"), None, "tensor"),
        P("tensor", None),
        P("tensor", None),
        P(("groups", "dp")),
        P(("groups", "dp"), None),
    )
    return jax.shard_map(
        functools.partial(shards, mesh.shape["tensor"], mesh.shape["dp"]),
        mesh=mesh,
        in_specs=placed,
        out_specs=P(("groups", "dp"), None),
        check_vma=False,
    )
```

```python
import functools

import jax
import jax.numpy as jnp
from jax import lax
from jax.experimental import pallas as pl
from jax.experimental.pallas import tpu as pltpu
from jax.sharding import PartitionSpec as P

CORES = 2
SMALL = pltpu.CompilerParams(vmem_limit_bytes=8 << 20)
NT = (((1,), (1,)), ((), ()))
HBM = pl.BlockSpec(memory_space=pltpu.HBM)
in_hbm = functools.partial(pltpu.with_memory_space_constraint, memory_space=pltpu.HBM)
VMEM = pl.BlockSpec(memory_space=pltpu.VMEM)


def xor_permute(value, axis, size, step):
    return lax.ppermute(value, axis, [(i, i ^ step) for i in range(size)])


def cut_kernel(tests, out, sem):
    width = out.shape[1]
    start = pl.multiple_of(lax.axis_index("tensor") * width, 128)
    copy = pltpu.make_async_copy(tests.at[:, pl.ds(start, width)], out, sem)
    copy.start()
    copy.wait()


def cut_tests(tests, size):
    rows, width = tests.shape
    return pl.pallas_call(
        cut_kernel,
        out_shape=jax.ShapeDtypeStruct((rows, width // size), tests.dtype),
        in_specs=[HBM],
        out_specs=VMEM,
        scratch_shapes=[pltpu.SemaphoreType.DMA],
        compiler_params=SMALL,
    )(in_hbm(tests))


COST = 1 << 32


def project_kernel(steps, share, ahead, piece, after, act, og, wi, wo, lens, *refs):
    refs = refs[after:]
    outs, (buf, wibuf, wobuf, lenbuf, sem, wsem) = refs[:-6], refs[-6:]
    me = lax.axis_index("tensor")
    rank = wibuf.shape[0]
    slots = buf.shape[2]
    count = len(steps) * share
    tokens = count * slots
    small = [
        pltpu.make_async_copy(wi, wibuf, wsem.at[0]),
        pltpu.make_async_copy(wo, wobuf, wsem.at[1]),
        pltpu.make_async_copy(lens, lenbuf, wsem.at[2]),
    ]
    pieces = [(side, at) for side, ref in enumerate((act, og)) for at in range(0, ref.shape[2], piece)]
    copies = []
    for slot, (side, at) in enumerate(pieces):
        width = min(piece, (act, og)[side].shape[2] - at)
        copies.append(
            [
                pltpu.make_async_copy(
                    (act, og)[side].at[pl.ds((me ^ step) * share, share), :, pl.ds(at, width)],
                    buf.at[slot, pl.ds(i * share, share), :, pl.ds(0, width)],
                    sem.at[slot, i],
                )
                for i, step in enumerate(steps)
            ]
        )
    small[0].start()
    for slot, group in enumerate(copies):
        if slot == 1:
            small[1].start()
            small[2].start()
        if slot < ahead:
            for copy in group:
                copy.start()
    sums = [None, None]
    for slot, (side, at) in enumerate(pieces):
        if at == 0:
            small[side].wait()
        for copy in copies[slot]:
            copy.wait()
        if slot + ahead < len(pieces):
            for copy in copies[slot + ahead]:
                copy.start()
        weight = (wibuf, wobuf)[side][:, at : at + piece]
        token = buf[slot].reshape(tokens, piece)[:, : weight.shape[1]]
        part = lax.dot_general(weight, token, NT, preferred_element_type=jnp.float32)
        sums[side] = part if sums[side] is None else sums[side] + part
    small[2].wait()
    col = lax.broadcasted_iota(jnp.int32, (rank, slots), 1)
    places = [out.at[i] for out in outs for i in range(out.shape[0])]
    for slot, out in enumerate(places):
        length = lenbuf[(me ^ steps[slot // share]) * share + slot % share]
        one = sums[0][:, slot * slots : (slot + 1) * slots] * (1.0 / length.astype(jnp.float32))
        out[:rank] = jnp.where(col < length, one, 0.0)
        out[rank:] = sums[1][:, slot * slots : (slot + 1) * slots]


def project(act, og, wi, wo, lens, groups, share, ahead, piece, after=()):
    steps = [step for group in groups for step in group]
    count = len(steps) * share
    slots, feat, hidden = act.shape[1], act.shape[2], og.shape[2]
    rank = wi.shape[0]
    pieces = -(-feat // piece) - (-hidden // piece)
    return pl.pallas_call(
        functools.partial(project_kernel, steps, share, ahead, piece, len(after)),
        out_shape=[jax.ShapeDtypeStruct((len(group) * share, 2 * rank, slots), jnp.float32) for group in groups],
        in_specs=[HBM] * 5 + [VMEM] * len(after),
        out_specs=[VMEM] * len(groups),
        scratch_shapes=[
            pltpu.VMEM((pieces, count, slots, piece), act.dtype),
            pltpu.VMEM((rank, feat), wi.dtype),
            pltpu.VMEM((rank, hidden), wo.dtype),
            pltpu.SMEM(lens.shape, lens.dtype),
            pltpu.SemaphoreType.DMA((pieces, len(steps))),
            pltpu.SemaphoreType.DMA((3,)),
        ],
        compiler_params=pltpu.CompilerParams(vmem_limit_bytes=32 << 20),
        cost_estimate=pl.CostEstimate(flops=COST, bytes_accessed=COST // 256, transcendentals=0),
    )(*map(in_hbm, (act, og, wi, wo, lens)), *after)


def unit_kernel(share, rank, size, *refs):
    parts, outs, pairs, held = refs[:-4], refs[-4:-2], refs[-2], refs[-1]
    me = lax.axis_index("tensor")
    rows = rank * rank // 128
    span = rows // size
    dot = functools.partial(lax.dot_general, dimension_numbers=NT, preferred_element_type=jnp.float32)
    for k in range(share):
        full = parts[0][k]
        for part in parts[1:]:
            full = full + part[k]
        high = full.astype(jnp.bfloat16)
        low = (full - high.astype(jnp.float32)).astype(jnp.bfloat16)
        left, right = slice(None, rank), slice(rank, None)
        pairs[k] = dot(high[left], high[right]) + (dot(high[left], low[right]) + dot(low[left], high[right]))
    for k in range(share):
        even = pairs[k, pl.ds(0, rows, stride=2), :]
        odd = pairs[k, pl.ds(1, rows, stride=2), :]
        flat = jnp.concatenate([even, odd], axis=1)
        scale = jnp.sqrt(jnp.sum(flat * flat) / (rank * rank) + 1e-06)
        unit = flat / scale
        for to in range(size):
            held[to, k] = unit[to * span : (to + 1) * span]
    for j in range(size // CORES):
        for core in range(CORES):
            outs[core][j] = held[me ^ core ^ (CORES * j)]


def units(parts, share, rank, size):
    span = rank * rank // 128 // size
    return pl.pallas_call(
        functools.partial(unit_kernel, share, rank, size),
        out_shape=[jax.ShapeDtypeStruct((size // CORES, share, span, 128), jnp.float32)] * CORES,
        in_specs=[VMEM] * len(parts),
        out_specs=[VMEM] * CORES,
        scratch_shapes=[pltpu.VMEM((share, rank, rank), jnp.float32), pltpu.VMEM((size, share, span, 128), jnp.float32)],
        compiler_params=SMALL,
    )(*parts)


def score_kernel(share, far, shifts, own_ref, core_ref, *refs):
    far_refs, test_refs, out, held = refs[: len(far)], refs[len(far) : -2], refs[-2], refs[-1]
    me, dp = lax.axis_index("tensor"), lax.axis_index("dp")
    blocks = [(me, own_ref.at[0]), (me ^ 1, core_ref.at[0])]
    blocks += [(me ^ step ^ core, ref.at[core]) for step, ref in zip(far, far_refs) for core in range(CORES)]
    for owner, ref in blocks:
        for k in range(share):
            held[owner * share + k] = ref[k]
    unit = jnp.concatenate([held[:, c, :] for c in range(held.shape[1])], axis=1).astype(jnp.bfloat16)
    tests = test_refs[0].shape[0]
    for step, test_ref in zip(shifts, test_refs):
        part = lax.dot_general(unit, test_ref[...], NT, preferred_element_type=jnp.float32)
        at = lax.rem(dp - step + len(shifts), len(shifts)) * tests
        out[:, pl.ds(pl.multiple_of(at, 128), tests)] = part


def score(own, core, far_units, test_parts, share, size):
    tests, width = test_parts[0].shape
    return pl.pallas_call(
        functools.partial(score_kernel, share, tuple(far_units), tuple(test_parts)),
        out_shape=jax.ShapeDtypeStruct((share * size, tests * len(test_parts)), jnp.float32),
        in_specs=[VMEM] * (2 + len(far_units) + len(test_parts)),
        out_specs=VMEM,
        scratch_shapes=[pltpu.VMEM((share * size, width // 128, 128), jnp.float32)],
        compiler_params=SMALL,
    )(own, core, *far_units.values(), *test_parts.values())


def shift(value, axis, size, step):
    return lax.ppermute(value, axis, [(i, (i + step) % size) for i in range(size)])


def shards(size, groups, activations, out_grads, proj_in, proj_out, lengths, test_grads):
    rank = proj_in.shape[1]
    share = activations.shape[0] // size
    own_tests = cut_tests(test_grads, size)
    tests = {0: own_tests, 1: shift(own_tests, "dp", groups, 1)}
    if groups == 4:
        tests[2] = shift(tests[1], "dp", groups, 1)
        tests[3] = shift(own_tests, "dp", groups, 3)
    else:
        tests.update({step: shift(own_tests, "dp", groups, step) for step in range(2, groups)})

    far = [CORES * x for x in range(1, size // CORES)]
    arrays = (activations, out_grads, proj_in.T, proj_out.T, lengths)
    sends = [[step ^ 1 for step in far] + [1], far]
    other, far_own = project(*arrays, sends, share, 3, 512, [own_tests])
    other = other + 0.0 * tests[1][:1, : other.shape[2]].astype(jnp.float32)
    arrived = xor_permute(other, "tensor", size, 1)
    cut = len(far) * share
    far_sum = far_own + arrived[:cut]
    sums = [xor_permute(far_sum[i * share : (i + 1) * share], "tensor", size, step) for i, step in enumerate(far)]
    near_own = project(*arrays, [[0]], share, 4, 1024, [far_sum])[0]

    own, core = units([near_own, arrived[cut:]] + sums, share, rank, size)
    core = xor_permute(core, "tensor", size, 1)
    far_units = {
        step: xor_permute(jnp.stack([own[j + 1], core[j + 1]]), "tensor", size, step) for j, step in enumerate(far)
    }
    part = score(own, core, far_units, tests, share, size)
    part = part + xor_permute(part, "tensor", size, 1)
    parts = [part] + [xor_permute(part, "tensor", size, step) for step in far]
    while len(parts) > 1:
        parts = [parts[i] + parts[i + 1] for i in range(0, len(parts), 2)]
    return parts[0]


def solution(mesh):
    placed = (
        P(("groups", "dp"), None, "tensor"),
        P(("groups", "dp"), None, "tensor"),
        P("tensor", None),
        P("tensor", None),
        P(("groups", "dp")),
        P(("groups", "dp"), None),
    )
    return jax.shard_map(
        functools.partial(shards, mesh.shape["tensor"], mesh.shape["dp"]),
        mesh=mesh,
        in_specs=placed,
        out_specs=P(("groups", "dp"), None),
        check_vma=False,
    )
```

```python
import functools

import jax
import jax.numpy as jnp
from jax import lax
from jax.experimental import pallas as pl
from jax.experimental.pallas import tpu as pltpu
from jax.sharding import PartitionSpec as P

CORES = 2
SMALL = pltpu.CompilerParams(vmem_limit_bytes=8 << 20)
NT = (((1,), (1,)), ((), ()))
HBM = pl.BlockSpec(memory_space=pltpu.HBM)
in_hbm = functools.partial(pltpu.with_memory_space_constraint, memory_space=pltpu.HBM)
VMEM = pl.BlockSpec(memory_space=pltpu.VMEM)


def xor_permute(value, axis, size, step):
    return lax.ppermute(value, axis, [(i, i ^ step) for i in range(size)])


def cut_kernel(tests, out, sem):
    width = out.shape[1]
    start = pl.multiple_of(lax.axis_index("tensor") * width, 128)
    copy = pltpu.make_async_copy(tests.at[:, pl.ds(start, width)], out, sem)
    copy.start()
    copy.wait()


def cut_tests(tests, size):
    rows, width = tests.shape
    return pl.pallas_call(
        cut_kernel,
        out_shape=jax.ShapeDtypeStruct((rows, width // size), tests.dtype),
        in_specs=[HBM],
        out_specs=VMEM,
        scratch_shapes=[pltpu.SemaphoreType.DMA],
        compiler_params=SMALL,
    )(in_hbm(tests))


COST = 1 << 32


def cut(total, piece, last):
    ends = list(range(piece, total - last + 1, piece))
    ends += [total - last] if total - last > 0 and (not ends or ends[-1] < total - last) else []
    ends += [total]
    return [slice(start, end) for start, end in zip([0] + ends[:-1], ends)]


def project_kernel(seqs, share, ahead, pieces, after, act, og, wi, wo, lens, *refs):
    refs = refs[after:]
    outs, (buf, wibuf, wobuf, lenbuf, sem, wsem) = refs[:-6], refs[-6:]
    me = lax.axis_index("tensor")
    rank = wibuf.shape[0]
    count, slots = buf.shape[1:3]
    places = [(me ^ step) * share + k for step, k in seqs]
    small = [
        pltpu.make_async_copy(wi, wibuf, wsem.at[0]),
        pltpu.make_async_copy(wo, wobuf, wsem.at[1]),
        pltpu.make_async_copy(lens, lenbuf, wsem.at[2]),
    ]
    copies = [
        [
            pltpu.make_async_copy(
                (act, og)[side].at[place, :, pl.ds(span.start, span.stop - span.start)],
                buf.at[slot, i, :, pl.ds(0, span.stop - span.start)],
                sem.at[slot, i],
            )
            for i, place in enumerate(places)
        ]
        for slot, (side, span) in enumerate(pieces)
    ]
    small[0].start()
    for slot, group in enumerate(copies[:ahead]):
        for copy in group:
            copy.start()
        if slot == 0:
            small[1].start()
            small[2].start()
    sums = [None, None]
    for slot, (side, span) in enumerate(pieces):
        if span.start == 0:
            small[side].wait()
        for copy in copies[slot]:
            copy.wait()
        for copy in copies[slot + ahead] if slot + ahead < len(copies) else ():
            copy.start()
        token = buf[slot].reshape(count * slots, buf.shape[3])[:, : span.stop - span.start]
        part = lax.dot_general((wibuf, wobuf)[side][:, span], token, NT, preferred_element_type=jnp.float32)
        sums[side] = part if sums[side] is None else sums[side] + part
    small[2].wait()
    col = lax.broadcasted_iota(jnp.int32, (rank, slots), 1)
    rows = [out.at[i] for out in outs for i in range(out.shape[0])]
    for slot, (row, place) in enumerate(zip(rows, places)):
        length = lenbuf[place]
        one = sums[0][:, slot * slots : (slot + 1) * slots] * (1.0 / length.astype(jnp.float32))
        row[:rank] = jnp.where(col < length, one, 0.0)
        row[rank:] = sums[1][:, slot * slots : (slot + 1) * slots]


def project(act, og, wi, wo, lens, groups, share, ahead, piece, after=()):
    seqs = [seq for group in groups for seq in group]
    count = len(seqs)
    slots, feat, hidden = act.shape[1], act.shape[2], og.shape[2]
    rank = wi.shape[0]
    pieces = [(0, span) for span in cut(feat, 512, 512)] + [(1, span) for span in cut(hidden, piece, 256)]
    return pl.pallas_call(
        functools.partial(project_kernel, seqs, share, ahead, pieces, len(after)),
        out_shape=[jax.ShapeDtypeStruct((len(group), 2 * rank, slots), jnp.float32) for group in groups],
        in_specs=[HBM] * 5 + [VMEM] * len(after),
        out_specs=[VMEM] * len(groups),
        scratch_shapes=[
            pltpu.VMEM((len(pieces), count, slots, max(piece, 512)), act.dtype),
            pltpu.VMEM((rank, feat), wi.dtype),
            pltpu.VMEM((rank, hidden), wo.dtype),
            pltpu.SMEM(lens.shape, lens.dtype),
            pltpu.SemaphoreType.DMA((len(pieces), count)),
            pltpu.SemaphoreType.DMA((3,)),
        ],
        compiler_params=pltpu.CompilerParams(vmem_limit_bytes=32 << 20),
        cost_estimate=pl.CostEstimate(flops=COST, bytes_accessed=COST // 256, transcendentals=0),
    )(*map(in_hbm, (act, og, wi, wo, lens)), *after)


def unit_kernel(share, rank, size, *refs):
    singles, parts, outs = refs[:share], refs[share : -2 - size], refs[-2 - size : -2]
    pairs, held = refs[-2:]
    me = lax.axis_index("tensor")
    rows = rank * rank // 128
    span = rows // size
    dot = functools.partial(lax.dot_general, dimension_numbers=NT, preferred_element_type=jnp.float32)
    for k in range(share):
        full = singles[k][0]
        for part in parts:
            full = full + part[k]
        high = full.astype(jnp.bfloat16)
        low = (full - high.astype(jnp.float32)).astype(jnp.bfloat16)
        left, right = slice(None, rank), slice(rank, None)
        pairs[k] = dot(high[left], high[right]) + (dot(high[left], low[right]) + dot(low[left], high[right]))
    for k in range(share):
        even = pairs[k, pl.ds(0, rows, stride=2), :]
        odd = pairs[k, pl.ds(1, rows, stride=2), :]
        flat = jnp.concatenate([even, odd], axis=1)
        scale = jnp.sqrt(jnp.sum(flat * flat) / (rank * rank) + 1e-06)
        unit = flat / scale
        for to in range(size):
            held[to] = unit[to * span : (to + 1) * span]
        for step in range(size):
            outs[step][k] = held[me ^ step]


def units(parts, singles, share, rank, size):
    span = rank * rank // 128 // size
    return pl.pallas_call(
        functools.partial(unit_kernel, share, rank, size),
        out_shape=[jax.ShapeDtypeStruct((share, span, 128), jnp.float32)] * size,
        in_specs=[VMEM] * (share + len(parts)),
        out_specs=[VMEM] * size,
        scratch_shapes=[pltpu.VMEM((share, rank, rank), jnp.float32), pltpu.VMEM((size, span, 128), jnp.float32)],
        compiler_params=SMALL,
    )(*singles, *parts)


def score_kernel(share, size, shifts, *refs):
    unit_refs, test_refs, out, held = refs[:size], refs[size:-2], refs[-2], refs[-1]
    me, dp = lax.axis_index("tensor"), lax.axis_index("dp")
    for step in range(size):
        for k in range(share):
            held[(me ^ step) * share + k] = unit_refs[step][k]
    unit = jnp.concatenate([held[:, c, :] for c in range(held.shape[1])], axis=1).astype(jnp.bfloat16)
    tests = test_refs[0].shape[0]
    for step, test_ref in zip(shifts, test_refs):
        part = lax.dot_general(unit, test_ref[...], NT, preferred_element_type=jnp.float32)
        at = lax.rem(dp - step + len(shifts), len(shifts)) * tests
        out[:, pl.ds(pl.multiple_of(at, 128), tests)] = part


def score(unit_parts, test_parts, share):
    size, groups = len(unit_parts), len(test_parts)
    tests, width = test_parts[0].shape
    shifts = tuple(test_parts)
    return pl.pallas_call(
        functools.partial(score_kernel, share, size, shifts),
        out_shape=jax.ShapeDtypeStruct((share * size, tests * groups), jnp.float32),
        in_specs=[VMEM] * (size + groups),
        out_specs=VMEM,
        scratch_shapes=[pltpu.VMEM((share * size, width // 128, 128), jnp.float32)],
        compiler_params=SMALL,
    )(*unit_parts, *test_parts.values())


def shift(value, axis, size, step):
    return lax.ppermute(value, axis, [(i, (i + step) % size) for i in range(size)])


def shards(size, groups, activations, out_grads, proj_in, proj_out, lengths, test_grads):
    rank = proj_in.shape[1]
    share = activations.shape[0] // size
    own_tests = cut_tests(test_grads, size)
    tests = {0: own_tests, -1: shift(own_tests, "dp", groups, -1)}
    if groups == 4:
        tests[-2] = shift(tests[-1], "dp", groups, -1)
        tests[1] = shift(own_tests, "dp", groups, 1)
    else:
        tests.update({-step: shift(own_tests, "dp", groups, -step) for step in range(2, groups)})

    far = [CORES * x for x in range(1, size // CORES)]
    arrays = (activations, out_grads, proj_in.T, proj_out.T, lengths)
    here = range(share)
    early, late = here[: share // 2], here[share // 2 :]
    sends = [[(step ^ 1, k) for step in far for k in here] + [(1, k) for k in early], [(step, k) for step in far for k in here]]
    other, far_own = project(*arrays, sends, share, 3, 896, [own_tests])
    other = other + 0.0 * tests[-1][:1, : other.shape[2]].astype(jnp.float32)
    arrived = xor_permute(other, "tensor", size, 1)
    split = len(far) * share
    far_sum = far_own + arrived[:split]
    sums = [xor_permute(far_sum[i * share : (i + 1) * share], "tensor", size, step) for i, step in enumerate(far)]
    near_other, near_own = project(*arrays, [[(1, k) for k in late], [(0, k) for k in here]], share, 3, 896, [far_sum])
    last = xor_permute(near_other, "tensor", size, 1)
    singles = [arrived[split + k : split + k + 1] for k in early] + [last[k : k + 1] for k in range(len(late))]

    unit_outs = units([near_own] + sums, singles, share, rank, size)
    unit_parts = [unit_outs[0]] + [xor_permute(unit_outs[step], "tensor", size, step) for step in range(1, size)]
    part = score(unit_parts, tests, share)
    parts = [part] + [xor_permute(part, "tensor", size, step) for step in range(1, size)]
    while len(parts) > 1:
        parts = [parts[i] + parts[i + 1] for i in range(0, len(parts), 2)]
    return parts[0]


def solution(mesh):
    placed = (
        P(("groups", "dp"), None, "tensor"),
        P(("groups", "dp"), None, "tensor"),
        P("tensor", None),
        P("tensor", None),
        P(("groups", "dp")),
        P(("groups", "dp"), None),
    )
    return jax.shard_map(
        functools.partial(shards, mesh.shape["tensor"], mesh.shape["dp"]),
        mesh=mesh,
        in_specs=placed,
        out_specs=P(("groups", "dp"), None),
        check_vma=False,
    )
```

```python
import functools

import jax
import jax.numpy as jnp
from jax import lax
from jax.experimental import pallas as pl
from jax.experimental.pallas import tpu as pltpu
from jax.sharding import PartitionSpec as P

CORES = 2
SMALL = pltpu.CompilerParams(vmem_limit_bytes=8 << 20)
NT = (((1,), (1,)), ((), ()))
HBM = pl.BlockSpec(memory_space=pltpu.HBM)
in_hbm = functools.partial(pltpu.with_memory_space_constraint, memory_space=pltpu.HBM)
VMEM = pl.BlockSpec(memory_space=pltpu.VMEM)


def xor_permute(value, axis, size, step):
    return lax.ppermute(value, axis, [(i, i ^ step) for i in range(size)])


def cut_kernel(tests, out, sem):
    width = out.shape[1]
    start = pl.multiple_of(lax.axis_index("tensor") * width, 128)
    copy = pltpu.make_async_copy(tests.at[:, pl.ds(start, width)], out, sem)
    copy.start()
    copy.wait()


def cut_tests(tests, size):
    rows, width = tests.shape
    return pl.pallas_call(
        cut_kernel,
        out_shape=jax.ShapeDtypeStruct((rows, width // size), tests.dtype),
        in_specs=[HBM],
        out_specs=VMEM,
        scratch_shapes=[pltpu.SemaphoreType.DMA],
        compiler_params=SMALL,
    )(in_hbm(tests))


COST = 1 << 32


def cut(total, piece, last):
    ends = list(range(piece, total - last + 1, piece))
    ends += [total - last] if total - last > 0 and (not ends or ends[-1] < total - last) else []
    ends += [total]
    return [slice(start, end) for start, end in zip([0] + ends[:-1], ends)]


def project_kernel(steps, share, ahead, pieces, after, act, og, wi, wo, lens, *refs):
    refs = refs[after:]
    outs, (buf, wibuf, wobuf, lenbuf, sem, wsem) = refs[:-6], refs[-6:]
    me = lax.axis_index("tensor")
    rank = wibuf.shape[0]
    slots = buf.shape[2]
    count = len(steps) * share
    tokens = count * slots
    small = [
        pltpu.make_async_copy(wi, wibuf, wsem.at[0]),
        pltpu.make_async_copy(wo, wobuf, wsem.at[1]),
        pltpu.make_async_copy(lens, lenbuf, wsem.at[2]),
    ]
    copies = [
        [
            pltpu.make_async_copy(
                (act, og)[side].at[pl.ds((me ^ step) * share, share), :, pl.ds(span.start, span.stop - span.start)],
                buf.at[slot, pl.ds(i * share, share), :, pl.ds(0, span.stop - span.start)],
                sem.at[slot, i],
            )
            for i, step in enumerate(steps)
        ]
        for slot, (side, span) in enumerate(pieces)
    ]
    small[0].start()
    for slot, group in enumerate(copies[:ahead]):
        for copy in group:
            copy.start()
        if slot == 0:
            small[1].start()
            small[2].start()
    sums = [None, None]
    for slot, (side, span) in enumerate(pieces):
        if span.start == 0:
            small[side].wait()
        for copy in copies[slot]:
            copy.wait()
        for copy in copies[slot + ahead] if slot + ahead < len(copies) else ():
            copy.start()
        token = buf[slot].reshape(tokens, buf.shape[3])[:, : span.stop - span.start]
        part = lax.dot_general((wibuf, wobuf)[side][:, span], token, NT, preferred_element_type=jnp.float32)
        sums[side] = part if sums[side] is None else sums[side] + part
    small[2].wait()
    col = lax.broadcasted_iota(jnp.int32, (rank, slots), 1)
    places = [out.at[i] for out in outs for i in range(out.shape[0])]
    for slot, out in enumerate(places):
        length = lenbuf[(me ^ steps[slot // share]) * share + slot % share]
        one = sums[0][:, slot * slots : (slot + 1) * slots] * (1.0 / length.astype(jnp.float32))
        out[:rank] = jnp.where(col < length, one, 0.0)
        out[rank:] = sums[1][:, slot * slots : (slot + 1) * slots]


def project(act, og, wi, wo, lens, groups, share, ahead, piece, after=()):
    steps = [step for group in groups for step in group]
    count = len(steps) * share
    slots, feat, hidden = act.shape[1], act.shape[2], og.shape[2]
    rank = wi.shape[0]
    pieces = [(0, span) for span in cut(feat, piece, piece)] + [(1, span) for span in cut(hidden, piece, 256)]
    return pl.pallas_call(
        functools.partial(project_kernel, steps, share, ahead, pieces, len(after)),
        out_shape=[jax.ShapeDtypeStruct((len(group) * share, 2 * rank, slots), jnp.float32) for group in groups],
        in_specs=[HBM] * 5 + [VMEM] * len(after),
        out_specs=[VMEM] * len(groups),
        scratch_shapes=[
            pltpu.VMEM((len(pieces), count, slots, piece), act.dtype),
            pltpu.VMEM((rank, feat), wi.dtype),
            pltpu.VMEM((rank, hidden), wo.dtype),
            pltpu.SMEM(lens.shape, lens.dtype),
            pltpu.SemaphoreType.DMA((len(pieces), len(steps))),
            pltpu.SemaphoreType.DMA((3,)),
        ],
        compiler_params=pltpu.CompilerParams(vmem_limit_bytes=32 << 20),
        cost_estimate=pl.CostEstimate(flops=COST, bytes_accessed=COST // 256, transcendentals=0),
    )(*map(in_hbm, (act, og, wi, wo, lens)), *after)


def unit_kernel(share, rank, size, *refs):
    parts, outs = refs[: -2 - size], refs[-2 - size : -2]
    pairs, held = refs[-2:]
    me = lax.axis_index("tensor")
    rows = rank * rank // 128
    span = rows // size
    dot = functools.partial(lax.dot_general, dimension_numbers=NT, preferred_element_type=jnp.float32)
    for k in range(share):
        full = parts[0][k]
        for part in parts[1:]:
            full = full + part[k]
        high = full.astype(jnp.bfloat16)
        low = (full - high.astype(jnp.float32)).astype(jnp.bfloat16)
        left, right = slice(None, rank), slice(rank, None)
        pairs[k] = dot(high[left], high[right]) + (dot(high[left], low[right]) + dot(low[left], high[right]))
    for k in range(share):
        even = pairs[k, pl.ds(0, rows, stride=2), :]
        odd = pairs[k, pl.ds(1, rows, stride=2), :]
        flat = jnp.concatenate([even, odd], axis=1)
        scale = jnp.sqrt(jnp.sum(flat * flat) / (rank * rank) + 1e-06)
        unit = flat / scale
        for to in range(size):
            held[to] = unit[to * span : (to + 1) * span]
        for step in range(size):
            outs[step][k] = held[me ^ step]


def units(parts, share, rank, size):
    span = rank * rank // 128 // size
    return pl.pallas_call(
        functools.partial(unit_kernel, share, rank, size),
        out_shape=[jax.ShapeDtypeStruct((share, span, 128), jnp.float32)] * size,
        in_specs=[VMEM] * len(parts),
        out_specs=[VMEM] * size,
        scratch_shapes=[pltpu.VMEM((share, rank, rank), jnp.float32), pltpu.VMEM((size, span, 128), jnp.float32)],
        compiler_params=SMALL,
    )(*parts)


def score_kernel(share, size, shifts, *refs):
    unit_refs, test_refs, out, held = refs[:size], refs[size:-2], refs[-2], refs[-1]
    me, dp = lax.axis_index("tensor"), lax.axis_index("dp")
    for step in range(size):
        for k in range(share):
            held[(me ^ step) * share + k] = unit_refs[step][k]
    unit = jnp.concatenate([held[:, c, :] for c in range(held.shape[1])], axis=1).astype(jnp.bfloat16)
    tests = test_refs[0].shape[0]
    for step, test_ref in zip(shifts, test_refs):
        part = lax.dot_general(unit, test_ref[...], NT, preferred_element_type=jnp.float32)
        at = lax.rem(dp - step + len(shifts), len(shifts)) * tests
        out[:, pl.ds(pl.multiple_of(at, 128), tests)] = part


def score(unit_parts, test_parts, share):
    size, groups = len(unit_parts), len(test_parts)
    tests, width = test_parts[0].shape
    shifts = tuple(test_parts)
    return pl.pallas_call(
        functools.partial(score_kernel, share, size, shifts),
        out_shape=jax.ShapeDtypeStruct((share * size, tests * groups), jnp.float32),
        in_specs=[VMEM] * (size + groups),
        out_specs=VMEM,
        scratch_shapes=[pltpu.VMEM((share * size, width // 128, 128), jnp.float32)],
        compiler_params=SMALL,
    )(*unit_parts, *test_parts.values())


def shift(value, axis, size, step):
    return lax.ppermute(value, axis, [(i, (i + step) % size) for i in range(size)])


def shards(size, groups, activations, out_grads, proj_in, proj_out, lengths, test_grads):
    rank = proj_in.shape[1]
    share = activations.shape[0] // size
    own_tests = cut_tests(test_grads, size)
    tests = {0: own_tests, 1: shift(own_tests, "dp", groups, 1)}
    if groups == 4:
        tests[2] = shift(tests[1], "dp", groups, 1)
        tests[3] = shift(own_tests, "dp", groups, 3)
    else:
        tests.update({step: shift(own_tests, "dp", groups, step) for step in range(2, groups)})

    far = [CORES * x for x in range(1, size // CORES)]
    arrays = (activations, out_grads, proj_in.T, proj_out.T, lengths)
    sends = [[step ^ 1 for step in far] + [1], far]
    other, far_own = project(*arrays, sends, share, 2, 512, [own_tests])
    other = other + 0.0 * tests[1][:1, : other.shape[2]].astype(jnp.float32)
    arrived = xor_permute(other, "tensor", size, 1)
    cut_at = len(far) * share
    far_sum = far_own + arrived[:cut_at]
    sums = [xor_permute(far_sum[i * share : (i + 1) * share], "tensor", size, step) for i, step in enumerate(far)]
    near_own = project(*arrays, [[0]], share, 4, 512, [far_sum])[0]

    unit_outs = units([near_own, arrived[cut_at:]] + sums, share, rank, size)
    unit_parts = [unit_outs[0]] + [xor_permute(unit_outs[step], "tensor", size, step) for step in range(1, size)]
    part = score(unit_parts, tests, share)
    parts = [part] + [xor_permute(part, "tensor", size, step) for step in range(1, size)]
    while len(parts) > 1:
        parts = [parts[i] + parts[i + 1] for i in range(0, len(parts), 2)]
    return parts[0]


def solution(mesh):
    placed = (
        P(("groups", "dp"), None, "tensor"),
        P(("groups", "dp"), None, "tensor"),
        P("tensor", None),
        P("tensor", None),
        P(("groups", "dp")),
        P(("groups", "dp"), None),
    )
    return jax.shard_map(
        functools.partial(shards, mesh.shape["tensor"], mesh.shape["dp"]),
        mesh=mesh,
        in_specs=placed,
        out_specs=P(("groups", "dp"), None),
        check_vma=False,
    )
```

```python
import functools

import jax
import jax.numpy as jnp
from jax import lax
from jax.experimental import pallas as pl
from jax.experimental.pallas import tpu as pltpu
from jax.sharding import PartitionSpec as P

CORES = 2
SMALL = pltpu.CompilerParams(vmem_limit_bytes=8 << 20)
NT = (((1,), (1,)), ((), ()))
HBM = pl.BlockSpec(memory_space=pltpu.HBM)
in_hbm = functools.partial(pltpu.with_memory_space_constraint, memory_space=pltpu.HBM)
VMEM = pl.BlockSpec(memory_space=pltpu.VMEM)


def xor_permute(value, axis, size, step):
    return lax.ppermute(value, axis, [(i, i ^ step) for i in range(size)])


def cut_kernel(tests, out, sem):
    width = out.shape[1]
    start = pl.multiple_of(lax.axis_index("tensor") * width, 128)
    copy = pltpu.make_async_copy(tests.at[:, pl.ds(start, width)], out, sem)
    copy.start()
    copy.wait()


def cut_tests(tests, size):
    rows, width = tests.shape
    return pl.pallas_call(
        cut_kernel,
        out_shape=jax.ShapeDtypeStruct((rows, width // size), tests.dtype),
        in_specs=[HBM],
        out_specs=VMEM,
        scratch_shapes=[pltpu.SemaphoreType.DMA],
        compiler_params=SMALL,
    )(in_hbm(tests))


COST = 1 << 32


def cut(total, widths):
    slices = []
    while not slices or slices[-1].stop < total:
        start = slices[-1].stop if slices else 0
        slices.append(slice(start, min(start + widths[min(len(slices), len(widths) - 1)], total)))
    return slices


def project_kernel(steps, share, ahead, pieces, after, act, og, wi, wo, lens, *refs):
    refs = refs[after:]
    outs, (buf, wibuf, wobuf, lenbuf, sem, wsem) = refs[:-6], refs[-6:]
    me = lax.axis_index("tensor")
    rank = wibuf.shape[0]
    slots = buf.shape[2]
    count = len(steps) * share
    tokens = count * slots
    small = [
        pltpu.make_async_copy(wi, wibuf, wsem.at[0]),
        pltpu.make_async_copy(wo, wobuf, wsem.at[1]),
        pltpu.make_async_copy(lens, lenbuf, wsem.at[2]),
    ]
    copies = [
        [
            pltpu.make_async_copy(
                (act, og)[side].at[pl.ds((me ^ step) * share, share), :, pl.ds(span.start, span.stop - span.start)],
                buf.at[slot, pl.ds(i * share, share), :, pl.ds(0, span.stop - span.start)],
                sem.at[slot, i],
            )
            for i, step in enumerate(steps)
        ]
        for slot, (side, span) in enumerate(pieces)
    ]
    small[0].start()
    for slot, group in enumerate(copies[:ahead]):
        for copy in group:
            copy.start()
        if slot == 0:
            small[1].start()
            small[2].start()
    sums = [None, None]
    for slot, (side, span) in enumerate(pieces):
        if span.start == 0:
            small[side].wait()
        for copy in copies[slot]:
            copy.wait()
        for copy in copies[slot + ahead] if slot + ahead < len(copies) else ():
            copy.start()
        token = buf[slot].reshape(tokens, buf.shape[3])[:, : span.stop - span.start]
        part = lax.dot_general((wibuf, wobuf)[side][:, span], token, NT, preferred_element_type=jnp.float32)
        sums[side] = part if sums[side] is None else sums[side] + part
    small[2].wait()
    col = lax.broadcasted_iota(jnp.int32, (rank, slots), 1)
    places = [out.at[i] for out in outs for i in range(out.shape[0])]
    for slot, out in enumerate(places):
        length = lenbuf[(me ^ steps[slot // share]) * share + slot % share]
        one = sums[0][:, slot * slots : (slot + 1) * slots] * (1.0 / length.astype(jnp.float32))
        out[:rank] = jnp.where(col < length, one, 0.0)
        out[rank:] = sums[1][:, slot * slots : (slot + 1) * slots]


def project(act, og, wi, wo, lens, groups, share, ahead, widths, after=()):
    steps = [step for group in groups for step in group]
    count = len(steps) * share
    slots, feat, hidden = act.shape[1], act.shape[2], og.shape[2]
    rank = wi.shape[0]
    pieces = [(0, span) for span in cut(feat, widths)] + [(1, span) for span in cut(hidden, [512])]
    piece = max(span.stop - span.start for _, span in pieces)
    return pl.pallas_call(
        functools.partial(project_kernel, steps, share, ahead, pieces, len(after)),
        out_shape=[jax.ShapeDtypeStruct((len(group) * share, 2 * rank, slots), jnp.float32) for group in groups],
        in_specs=[HBM] * 5 + [VMEM] * len(after),
        out_specs=[VMEM] * len(groups),
        scratch_shapes=[
            pltpu.VMEM((len(pieces), count, slots, piece), act.dtype),
            pltpu.VMEM((rank, feat), wi.dtype),
            pltpu.VMEM((rank, hidden), wo.dtype),
            pltpu.SMEM(lens.shape, lens.dtype),
            pltpu.SemaphoreType.DMA((len(pieces), len(steps))),
            pltpu.SemaphoreType.DMA((3,)),
        ],
        compiler_params=pltpu.CompilerParams(vmem_limit_bytes=32 << 20),
        cost_estimate=pl.CostEstimate(flops=COST, bytes_accessed=COST // 256, transcendentals=0),
    )(*map(in_hbm, (act, og, wi, wo, lens)), *after)


def unit_kernel(share, rank, size, *refs):
    parts, outs = refs[: -2 - size], refs[-2 - size : -2]
    pairs, held = refs[-2:]
    me = lax.axis_index("tensor")
    rows = rank * rank // 128
    span = rows // size
    dot = functools.partial(lax.dot_general, dimension_numbers=NT, preferred_element_type=jnp.float32)
    for k in range(share):
        full = parts[0][k]
        for part in parts[1:]:
            full = full + part[k]
        high = full.astype(jnp.bfloat16)
        low = (full - high.astype(jnp.float32)).astype(jnp.bfloat16)
        left, right = slice(None, rank), slice(rank, None)
        pairs[k] = dot(high[left], high[right]) + (dot(high[left], low[right]) + dot(low[left], high[right]))
    for k in range(share):
        even = pairs[k, pl.ds(0, rows, stride=2), :]
        odd = pairs[k, pl.ds(1, rows, stride=2), :]
        flat = jnp.concatenate([even, odd], axis=1)
        scale = jnp.sqrt(jnp.sum(flat * flat) / (rank * rank) + 1e-06)
        unit = flat / scale
        for to in range(size):
            held[to] = unit[to * span : (to + 1) * span]
        for step in range(size):
            outs[step][k] = held[me ^ step]


def units(parts, share, rank, size):
    span = rank * rank // 128 // size
    return pl.pallas_call(
        functools.partial(unit_kernel, share, rank, size),
        out_shape=[jax.ShapeDtypeStruct((share, span, 128), jnp.float32)] * size,
        in_specs=[VMEM] * len(parts),
        out_specs=[VMEM] * size,
        scratch_shapes=[pltpu.VMEM((share, rank, rank), jnp.float32), pltpu.VMEM((size, span, 128), jnp.float32)],
        compiler_params=SMALL,
    )(*parts)


def score_kernel(share, size, groups, origins, *refs):
    unit_refs, test_refs, out, held = refs[:size], refs[size:-2], refs[-2], refs[-1]
    me, dp = lax.axis_index("tensor"), lax.axis_index("dp")
    for step in range(size):
        for k in range(share):
            held[(me ^ step) * share + k] = unit_refs[step][k]
    unit = jnp.concatenate([held[:, c, :] for c in range(held.shape[1])], axis=1).astype(jnp.bfloat16)
    tests = test_refs[0].shape[0]
    out[...] = jnp.zeros_like(out)
    for (factor, offset), test_ref in zip(origins, test_refs):
        part = lax.dot_general(unit, test_ref[...], NT, preferred_element_type=jnp.float32)
        at = lax.rem(factor * dp + offset + groups, groups) * tests
        out[:, pl.ds(pl.multiple_of(at, 128), tests)] += part


def score(unit_parts, test_parts, share, groups):
    size = len(unit_parts)
    tests, width = test_parts[0][0].shape
    origins = [origin for _, *origin in test_parts]
    return pl.pallas_call(
        functools.partial(score_kernel, share, size, groups, origins),
        out_shape=jax.ShapeDtypeStruct((share * size, tests * groups), jnp.float32),
        in_specs=[VMEM] * (size + len(test_parts)),
        out_specs=VMEM,
        scratch_shapes=[pltpu.VMEM((share * size, width // 128, 128), jnp.float32)],
        compiler_params=SMALL,
    )(*unit_parts, *(shard for shard, *_ in test_parts))


def gather_tests(own, groups):
    if groups != 4:
        shards = [lax.ppermute(own, "dp", [(i, (i + step) % groups) for i in range(groups)]) for step in range(1, groups)]
        return [(own, 1, 0)] + [(shard, 1, -step) for step, shard in enumerate(shards, 1)], shards[:1]
    below = lax.ppermute(own, "dp", [(0, 1), (1, 2), (2, 3)])
    above = lax.ppermute(own, "dp", [(1, 0), (2, 1), (3, 2)])
    lower = lax.axis_index("dp") == 1
    outer, inner = jnp.where(lower, below, above), jnp.where(lower, above, below)
    ends = lax.ppermute(inner, "dp", [(1, 0), (2, 3)])
    middle = lax.ppermute(outer, "dp", [(1, 2), (2, 1)])
    across = lax.ppermute(outer, "dp", [(1, 3), (2, 0)])
    return [(own, 1, 0), (below, 1, -1), (above, 1, 1), (ends, 1, 2), (middle, 1, 2), (across, -1, 3)], [below, above]


def shards(size, groups, activations, out_grads, proj_in, proj_out, lengths, test_grads):
    rank = proj_in.shape[1]
    share = activations.shape[0] // size
    own_tests = cut_tests(test_grads, size)
    tests, first = gather_tests(own_tests, groups)

    far = [CORES * x for x in range(1, size // CORES)]
    arrays = (activations, out_grads, proj_in.T, proj_out.T, lengths)
    sends = [[step ^ 1 for step in far] + [1], far]
    other, far_own = project(*arrays, sends, share, 3, [128, 256, 640], [own_tests])
    for shard in first:
        other = other + 0.0 * shard[:1, : other.shape[2]].astype(jnp.float32)
    arrived = xor_permute(other, "tensor", size, 1)
    cut_at = len(far) * share
    far_sum = far_own + arrived[:cut_at]
    sums = [xor_permute(far_sum[i * share : (i + 1) * share], "tensor", size, step) for i, step in enumerate(far)]
    near_own = project(*arrays, [[0]], share, 7, [128, 256, 256, 384], [far_sum])[0]

    unit_outs = units([near_own, arrived[cut_at:]] + sums, share, rank, size)
    unit_parts = [unit_outs[0]] + [xor_permute(unit_outs[step], "tensor", size, step) for step in range(1, size)]
    part = score(unit_parts, tests, share, groups)
    parts = [part] + [xor_permute(part, "tensor", size, step) for step in range(1, size)]
    while len(parts) > 1:
        parts = [parts[i] + parts[i + 1] for i in range(0, len(parts), 2)]
    return parts[0]


def solution(mesh):
    placed = (
        P(("groups", "dp"), None, "tensor"),
        P(("groups", "dp"), None, "tensor"),
        P("tensor", None),
        P("tensor", None),
        P(("groups", "dp")),
        P(("groups", "dp"), None),
    )
    return jax.shard_map(
        functools.partial(shards, mesh.shape["tensor"], mesh.shape["dp"]),
        mesh=mesh,
        in_specs=placed,
        out_specs=P(("groups", "dp"), None),
        check_vma=False,
    )
```

```python
import functools

import jax
import jax.numpy as jnp
from jax import lax
from jax.experimental import pallas as pl
from jax.experimental.pallas import tpu as pltpu
from jax.sharding import PartitionSpec as P

CORES = 2
SMALL = pltpu.CompilerParams(vmem_limit_bytes=8 << 20)
NT = (((1,), (1,)), ((), ()))
HBM = pl.BlockSpec(memory_space=pltpu.HBM)
in_hbm = functools.partial(pltpu.with_memory_space_constraint, memory_space=pltpu.HBM)
VMEM = pl.BlockSpec(memory_space=pltpu.VMEM)


def xor_permute(value, axis, size, step):
    return lax.ppermute(value, axis, [(i, i ^ step) for i in range(size)])


def cut_kernel(tests, out, sem):
    width = out.shape[1]
    start = pl.multiple_of(lax.axis_index("tensor") * width, 128)
    copy = pltpu.make_async_copy(tests.at[:, pl.ds(start, width)], out, sem)
    copy.start()
    copy.wait()


def cut_tests(tests, size):
    rows, width = tests.shape
    return pl.pallas_call(
        cut_kernel,
        out_shape=jax.ShapeDtypeStruct((rows, width // size), tests.dtype),
        in_specs=[HBM],
        out_specs=VMEM,
        scratch_shapes=[pltpu.SemaphoreType.DMA],
        compiler_params=SMALL,
    )(in_hbm(tests))


COST = 1 << 32
PIECE = 512


def project_kernel(steps, share, ahead, pieces, after, act, og, wi, wo, lens, *refs):
    refs = refs[after:]
    outs, (buf, wibuf, wobuf, wide, lenbuf, sem, wsem) = refs[:-7], refs[-7:]
    me = lax.axis_index("tensor")
    rank, feat = wibuf.shape
    slots, piece = buf.shape[2:]
    small = [
        pltpu.make_async_copy(wi, wibuf, wsem.at[0]),
        pltpu.make_async_copy(wo, wobuf, wsem.at[1]),
        pltpu.make_async_copy(lens, lenbuf, wsem.at[2]),
    ]
    copies = [
        [
            pltpu.make_async_copy(
                (act, og)[side].at[pl.ds((me ^ step) * share, share), :, pl.ds(at, width)],
                buf.at[slot, pl.ds(i * share, share), :, pl.ds(0, width)],
                sem.at[slot, i],
            )
            for i, step in enumerate(steps)
        ]
        for slot, (side, at, width) in enumerate(pieces)
    ]
    for copy in small:
        copy.start()
    for group in copies[:ahead]:
        for copy in group:
            copy.start()
    for copy in small:
        copy.wait()
    for side, at, width in pieces:
        weight = (wibuf, wobuf)[side][:, at : at + width]
        none = jnp.zeros_like(weight)
        both = jnp.concatenate([none, weight] if side else [weight, none], axis=0)
        wide[side * feat + at : side * feat + at + width] = both.T
    sums = [None] * len(steps)
    for slot, (side, at, width) in enumerate(pieces):
        for copy in copies[slot]:
            copy.wait()
        for copy in copies[slot + ahead] if slot + ahead < len(copies) else ():
            copy.start()
        weight = wide[side * feat + at : side * feat + at + width]
        for i in range(len(steps)):
            token = buf[slot, i * share : (i + 1) * share].reshape(share * slots, piece)[:, :width]
            part = jnp.dot(token, weight, preferred_element_type=jnp.float32)
            sums[i] = part if sums[i] is None else sums[i] + part
    row = lax.broadcasted_iota(jnp.int32, (slots, 2 * rank), 0)
    lane = lax.broadcasted_iota(jnp.int32, (slots, 2 * rank), 1)
    places = [out.at[i] for out in outs for i in range(out.shape[0])]
    for slot, out in enumerate(places):
        i, k = divmod(slot, share)
        length = lenbuf[(me ^ steps[i]) * share + k]
        scale = jnp.where(lane < rank, 1.0 / length.astype(jnp.float32), 1.0)
        out[...] = jnp.where(row < length, sums[i][k * slots : (k + 1) * slots] * scale, 0.0)


def project(act, og, wi, wo, lens, groups, share, ahead, after=()):
    steps = [step for group in groups for step in group]
    count = len(steps) * share
    slots, feat, hidden = act.shape[1], act.shape[2], og.shape[2]
    rank = wi.shape[0]
    pieces = [
        (side, at, min(PIECE, total - at)) for side, total in enumerate((feat, hidden)) for at in range(0, total, PIECE)
    ]
    return pl.pallas_call(
        functools.partial(project_kernel, steps, share, ahead, pieces, len(after)),
        out_shape=[jax.ShapeDtypeStruct((len(group) * share, slots, 2 * rank), jnp.float32) for group in groups],
        in_specs=[HBM] * 5 + [VMEM] * len(after),
        out_specs=[VMEM] * len(groups),
        scratch_shapes=[
            pltpu.VMEM((len(pieces), count, slots, PIECE), act.dtype),
            pltpu.VMEM((rank, feat), wi.dtype),
            pltpu.VMEM((rank, hidden), wo.dtype),
            pltpu.VMEM((feat + hidden, 2 * rank), wo.dtype),
            pltpu.SMEM(lens.shape, lens.dtype),
            pltpu.SemaphoreType.DMA((len(pieces), len(steps))),
            pltpu.SemaphoreType.DMA((3,)),
        ],
        compiler_params=pltpu.CompilerParams(vmem_limit_bytes=32 << 20),
        cost_estimate=pl.CostEstimate(flops=COST, bytes_accessed=COST // 256, transcendentals=0),
    )(*map(in_hbm, (act, og, wi, wo, lens)), *after)


def unit_kernel(share, rank, size, *refs):
    parts, outs = refs[: -2 - size], refs[-2 - size : -2]
    pairs, held = refs[-2:]
    me = lax.axis_index("tensor")
    rows = rank * rank // 128
    span = rows // size
    dot = functools.partial(lax.dot_general, dimension_numbers=NT, preferred_element_type=jnp.float32)
    for k in range(share):
        full = parts[0][k]
        for part in parts[1:]:
            full = full + part[k]
        full = full.T
        high = full.astype(jnp.bfloat16)
        low = (full - high.astype(jnp.float32)).astype(jnp.bfloat16)
        left, right = slice(None, rank), slice(rank, None)
        pairs[k] = dot(high[left], high[right]) + (dot(high[left], low[right]) + dot(low[left], high[right]))
    for k in range(share):
        even = pairs[k, pl.ds(0, rows, stride=2), :]
        odd = pairs[k, pl.ds(1, rows, stride=2), :]
        flat = jnp.concatenate([even, odd], axis=1)
        scale = jnp.sqrt(jnp.sum(flat * flat) / (rank * rank) + 1e-06)
        unit = flat / scale
        for to in range(size):
            held[to] = unit[to * span : (to + 1) * span]
        for step in range(size):
            outs[step][k] = held[me ^ step]


def units(parts, share, rank, size):
    span = rank * rank // 128 // size
    return pl.pallas_call(
        functools.partial(unit_kernel, share, rank, size),
        out_shape=[jax.ShapeDtypeStruct((share, span, 128), jnp.float32)] * size,
        in_specs=[VMEM] * len(parts),
        out_specs=[VMEM] * size,
        scratch_shapes=[pltpu.VMEM((share, rank, rank), jnp.float32), pltpu.VMEM((size, span, 128), jnp.float32)],
        compiler_params=SMALL,
    )(*parts)


def score_kernel(share, size, shifts, *refs):
    unit_refs, test_refs, out, held = refs[:size], refs[size:-2], refs[-2], refs[-1]
    me, dp = lax.axis_index("tensor"), lax.axis_index("dp")
    for step in range(size):
        for k in range(share):
            held[(me ^ step) * share + k] = unit_refs[step][k]
    unit = jnp.concatenate([held[:, c, :] for c in range(held.shape[1])], axis=1).astype(jnp.bfloat16)
    tests = test_refs[0].shape[0]
    for step, test_ref in zip(shifts, test_refs):
        part = lax.dot_general(unit, test_ref[...], NT, preferred_element_type=jnp.float32)
        at = lax.rem(dp - step + len(shifts), len(shifts)) * tests
        out[:, pl.ds(pl.multiple_of(at, 128), tests)] = part


def score(unit_parts, test_parts, share):
    size, groups = len(unit_parts), len(test_parts)
    tests, width = test_parts[0].shape
    shifts = tuple(test_parts)
    return pl.pallas_call(
        functools.partial(score_kernel, share, size, shifts),
        out_shape=jax.ShapeDtypeStruct((share * size, tests * groups), jnp.float32),
        in_specs=[VMEM] * (size + groups),
        out_specs=VMEM,
        scratch_shapes=[pltpu.VMEM((share * size, width // 128, 128), jnp.float32)],
        compiler_params=SMALL,
    )(*unit_parts, *test_parts.values())


def shift(value, axis, size, step):
    return lax.ppermute(value, axis, [(i, (i + step) % size) for i in range(size)])


def shards(size, groups, activations, out_grads, proj_in, proj_out, lengths, test_grads):
    rank = proj_in.shape[1]
    share = activations.shape[0] // size
    own_tests = cut_tests(test_grads, size)
    tests = {0: own_tests, 1: shift(own_tests, "dp", groups, 1)}
    if groups == 4:
        tests[2] = shift(tests[1], "dp", groups, 1)
        tests[3] = shift(own_tests, "dp", groups, 3)
    else:
        tests.update({step: shift(own_tests, "dp", groups, step) for step in range(2, groups)})

    far = [CORES * x for x in range(1, size // CORES)]
    arrays = (activations, out_grads, proj_in.T, proj_out.T, lengths)
    sends = [[step ^ 1 for step in far] + [1], far]
    other, far_own = project(*arrays, sends, share, 3, [own_tests])
    other = other + 0.0 * tests[1][:1, : other.shape[2]].astype(jnp.float32)
    arrived = xor_permute(other, "tensor", size, 1)
    cut_at = len(far) * share
    far_sum = far_own + arrived[:cut_at]
    sums = [xor_permute(far_sum[i * share : (i + 1) * share], "tensor", size, step) for i, step in enumerate(far)]
    near_own = project(*arrays, [[0]], share, 6, [far_sum])[0]

    unit_outs = units([near_own, arrived[cut_at:]] + sums, share, rank, size)
    unit_parts = [unit_outs[0]] + [xor_permute(unit_outs[step], "tensor", size, step) for step in range(1, size)]
    part = score(unit_parts, tests, share)
    parts = [part] + [xor_permute(part, "tensor", size, step) for step in range(1, size)]
    while len(parts) > 1:
        parts = [parts[i] + parts[i + 1] for i in range(0, len(parts), 2)]
    return parts[0]


def solution(mesh):
    placed = (
        P(("groups", "dp"), None, "tensor"),
        P(("groups", "dp"), None, "tensor"),
        P("tensor", None),
        P("tensor", None),
        P(("groups", "dp")),
        P(("groups", "dp"), None),
    )
    return jax.shard_map(
        functools.partial(shards, mesh.shape["tensor"], mesh.shape["dp"]),
        mesh=mesh,
        in_specs=placed,
        out_specs=P(("groups", "dp"), None),
        check_vma=False,
    )
```

```python
import functools

import jax
import jax.numpy as jnp
from jax import lax
from jax.experimental import pallas as pl
from jax.experimental.pallas import tpu as pltpu
from jax.sharding import PartitionSpec as P

CORES = 2
SMALL = pltpu.CompilerParams(vmem_limit_bytes=8 << 20)
NT = (((1,), (1,)), ((), ()))
HBM = pl.BlockSpec(memory_space=pltpu.HBM)
in_hbm = functools.partial(pltpu.with_memory_space_constraint, memory_space=pltpu.HBM)
VMEM = pl.BlockSpec(memory_space=pltpu.VMEM)


def xor_permute(value, axis, size, step):
    return lax.ppermute(value, axis, [(i, i ^ step) for i in range(size)])


def cut_kernel(tests, out, sem):
    width = out.shape[1]
    start = pl.multiple_of(lax.axis_index("tensor") * width, 128)
    copy = pltpu.make_async_copy(tests.at[:, pl.ds(start, width)], out, sem)
    copy.start()
    copy.wait()


def cut_tests(tests, size):
    rows, width = tests.shape
    return pl.pallas_call(
        cut_kernel,
        out_shape=jax.ShapeDtypeStruct((rows, width // size), tests.dtype),
        in_specs=[HBM],
        out_specs=VMEM,
        scratch_shapes=[pltpu.SemaphoreType.DMA],
        compiler_params=SMALL,
    )(in_hbm(tests))


COST = 1 << 32


def project_kernel(steps, share, ahead, piece, after, act, og, wi, wo, lens, *refs):
    refs = refs[after:]
    outs, (buf, wibuf, wobuf, lenbuf, sem, wsem) = refs[:-6], refs[-6:]
    me = lax.axis_index("tensor")
    rank = wibuf.shape[0]
    slots = buf.shape[2]
    count = len(steps) * share
    tokens = count * slots
    small = [
        pltpu.make_async_copy(wi, wibuf, wsem.at[0]),
        pltpu.make_async_copy(wo, wobuf, wsem.at[1]),
        pltpu.make_async_copy(lens, lenbuf, wsem.at[2]),
    ]
    pieces = [(side, at) for side, ref in enumerate((act, og)) for at in range(0, ref.shape[2], piece)]
    copies = []
    for slot, (side, at) in enumerate(pieces):
        width = min(piece, (act, og)[side].shape[2] - at)
        copies.append(
            [
                pltpu.make_async_copy(
                    (act, og)[side].at[pl.ds((me ^ step) * share, share), :, pl.ds(at, width)],
                    buf.at[slot, pl.ds(i * share, share), :, pl.ds(0, width)],
                    sem.at[slot, i],
                )
                for i, step in enumerate(steps)
            ]
        )
    small[0].start()
    for slot, group in enumerate(copies):
        if slot == 1:
            small[1].start()
            small[2].start()
        if slot < ahead:
            for copy in group:
                copy.start()
    sums = [None, None]
    for slot, (side, at) in enumerate(pieces):
        if at == 0:
            small[side].wait()
        for copy in copies[slot]:
            copy.wait()
        if slot + ahead < len(pieces):
            for copy in copies[slot + ahead]:
                copy.start()
        weight = (wibuf, wobuf)[side][:, at : at + piece]
        token = buf[slot].reshape(tokens, piece)[:, : weight.shape[1]]
        part = lax.dot_general(weight, token, NT, preferred_element_type=jnp.float32)
        sums[side] = part if sums[side] is None else sums[side] + part
    small[2].wait()
    col = lax.broadcasted_iota(jnp.int32, (rank, slots), 1)
    places = [out.at[i] for out in outs for i in range(out.shape[0])]
    for slot, out in enumerate(places):
        length = lenbuf[(me ^ steps[slot // share]) * share + slot % share]
        one = sums[0][:, slot * slots : (slot + 1) * slots] * (1.0 / length.astype(jnp.float32))
        out[:rank] = jnp.where(col < length, one, 0.0)
        out[rank:] = sums[1][:, slot * slots : (slot + 1) * slots]


def project(act, og, wi, wo, lens, groups, share, ahead, piece, after=()):
    steps = [step for group in groups for step in group]
    count = len(steps) * share
    slots, feat, hidden = act.shape[1], act.shape[2], og.shape[2]
    rank = wi.shape[0]
    pieces = -(-feat // piece) - (-hidden // piece)
    return pl.pallas_call(
        functools.partial(project_kernel, steps, share, ahead, piece, len(after)),
        out_shape=[jax.ShapeDtypeStruct((len(group) * share, 2 * rank, slots), jnp.float32) for group in groups],
        in_specs=[HBM] * 5 + [VMEM] * len(after),
        out_specs=[VMEM] * len(groups),
        scratch_shapes=[
            pltpu.VMEM((pieces, count, slots, piece), act.dtype),
            pltpu.VMEM((rank, feat), wi.dtype),
            pltpu.VMEM((rank, hidden), wo.dtype),
            pltpu.SMEM(lens.shape, lens.dtype),
            pltpu.SemaphoreType.DMA((pieces, len(steps))),
            pltpu.SemaphoreType.DMA((3,)),
        ],
        compiler_params=pltpu.CompilerParams(vmem_limit_bytes=32 << 20),
        cost_estimate=pl.CostEstimate(flops=COST, bytes_accessed=COST // 256, transcendentals=0),
    )(*map(in_hbm, (act, og, wi, wo, lens)), *after)


def unit_kernel(share, rank, size, *refs):
    parts, outs = refs[: -2 - size], refs[-2 - size : -2]
    pairs, held = refs[-2:]
    me = lax.axis_index("tensor")
    rows = rank * rank // 128
    span = rows // size
    dot = functools.partial(lax.dot_general, dimension_numbers=NT, preferred_element_type=jnp.float32)
    for k in range(share):
        full = parts[0][k]
        for part in parts[1:]:
            full = full + part[k]
        high = full.astype(jnp.bfloat16)
        low = (full - high.astype(jnp.float32)).astype(jnp.bfloat16)
        left, right = slice(None, rank), slice(rank, None)
        pairs[k] = dot(high[left], high[right]) + (dot(high[left], low[right]) + dot(low[left], high[right]))
    for k in range(share):
        even = pairs[k, pl.ds(0, rows, stride=2), :]
        odd = pairs[k, pl.ds(1, rows, stride=2), :]
        flat = jnp.concatenate([even, odd], axis=1)
        scale = jnp.sqrt(jnp.sum(flat * flat) / (rank * rank) + 1e-06)
        unit = flat / scale
        for to in range(size):
            held[to] = unit[to * span : (to + 1) * span]
        for step in range(size):
            outs[step][k] = held[me ^ step]


def units(parts, share, rank, size):
    span = rank * rank // 128 // size
    return pl.pallas_call(
        functools.partial(unit_kernel, share, rank, size),
        out_shape=[jax.ShapeDtypeStruct((share, span, 128), jnp.float32)] * size,
        in_specs=[VMEM] * len(parts),
        out_specs=[VMEM] * size,
        scratch_shapes=[pltpu.VMEM((share, rank, rank), jnp.float32), pltpu.VMEM((size, span, 128), jnp.float32)],
        compiler_params=SMALL,
    )(*parts)


def score_kernel(share, size, shifts, *refs):
    unit_refs, test_refs, out, held = refs[:size], refs[size:-2], refs[-2], refs[-1]
    me, dp = lax.axis_index("tensor"), lax.axis_index("dp")
    for step in range(size):
        for k in range(share):
            held[(me ^ step) * share + k] = unit_refs[step][k]
    unit = jnp.concatenate([held[:, c, :] for c in range(held.shape[1])], axis=1).astype(jnp.bfloat16)
    tests = test_refs[0].shape[0]
    for step, test_ref in zip(shifts, test_refs):
        part = lax.dot_general(unit, test_ref[...], NT, preferred_element_type=jnp.float32)
        at = lax.rem(dp - step + len(shifts), len(shifts)) * tests
        out[:, pl.ds(pl.multiple_of(at, 128), tests)] = part


def score(unit_parts, test_parts, share):
    size, groups = len(unit_parts), len(test_parts)
    tests, width = test_parts[0].shape
    shifts = tuple(test_parts)
    return pl.pallas_call(
        functools.partial(score_kernel, share, size, shifts),
        out_shape=jax.ShapeDtypeStruct((share * size, tests * groups), jnp.float32),
        in_specs=[VMEM] * (size + groups),
        out_specs=VMEM,
        scratch_shapes=[pltpu.VMEM((share * size, width // 128, 128), jnp.float32)],
        compiler_params=SMALL,
    )(*unit_parts, *test_parts.values())


def shift(value, axis, size, step):
    return lax.ppermute(value, axis, [(i, (i + step) % size) for i in range(size)])


def shards(size, groups, activations, out_grads, proj_in, proj_out, lengths, test_grads):
    rank = proj_in.shape[1]
    share = activations.shape[0] // size
    own_tests = cut_tests(test_grads, size)
    tests = {0: own_tests, 1: shift(own_tests, "dp", groups, 1)}
    if groups == 4:
        tests[2] = shift(tests[1], "dp", groups, 1)
        tests[3] = shift(own_tests, "dp", groups, 3)
    else:
        tests.update({step: shift(own_tests, "dp", groups, step) for step in range(2, groups)})

    far = [CORES * x for x in range(1, size // CORES)]
    arrays = (activations, out_grads, proj_in.T, proj_out.T, lengths)
    far_other, far_own = project(*arrays, [[step ^ 1 for step in far], far], share, 4, 512, [own_tests])
    far_sum = far_own + xor_permute(far_other, "tensor", size, 1)
    sums = [xor_permute(far_sum[i * share : (i + 1) * share], "tensor", size, step) for i, step in enumerate(far)]
    here = xor_permute(tests[1][:16, :128], "tensor", size, 1)
    near_other, near_own = project(*arrays, [[1], [0]], share, 4, 512, [far_sum, here])
    arrived = jnp.concatenate([xor_permute(near_other[k : k + 1], "tensor", size, 1) for k in range(share)])

    unit_outs = units([near_own, arrived] + sums, share, rank, size)
    unit_parts = [unit_outs[0]] + [xor_permute(unit_outs[step], "tensor", size, step) for step in range(1, size)]
    part = score(unit_parts, tests, share)
    parts = [part] + [xor_permute(part, "tensor", size, step) for step in range(1, size)]
    while len(parts) > 1:
        parts = [parts[i] + parts[i + 1] for i in range(0, len(parts), 2)]
    return parts[0]


def solution(mesh):
    placed = (
        P(("groups", "dp"), None, "tensor"),
        P(("groups", "dp"), None, "tensor"),
        P("tensor", None),
        P("tensor", None),
        P(("groups", "dp")),
        P(("groups", "dp"), None),
    )
    return jax.shard_map(
        functools.partial(shards, mesh.shape["tensor"], mesh.shape["dp"]),
        mesh=mesh,
        in_specs=placed,
        out_specs=P(("groups", "dp"), None),
        check_vma=False,
    )
```

```python
import functools

import jax
import jax.numpy as jnp
from jax import lax
from jax.experimental import pallas as pl
from jax.experimental.pallas import tpu as pltpu
from jax.sharding import PartitionSpec as P

CORES = 2
SMALL = pltpu.CompilerParams(vmem_limit_bytes=8 << 20)
NT = (((1,), (1,)), ((), ()))
HBM = pl.BlockSpec(memory_space=pltpu.HBM)
in_hbm = functools.partial(pltpu.with_memory_space_constraint, memory_space=pltpu.HBM)
VMEM = pl.BlockSpec(memory_space=pltpu.VMEM)


def xor_permute(value, axis, size, step):
    return lax.ppermute(value, axis, [(i, i ^ step) for i in range(size)])


def cut_kernel(tests, out, sem):
    width = out.shape[1]
    start = pl.multiple_of(lax.axis_index("tensor") * width, 128)
    copy = pltpu.make_async_copy(tests.at[:, pl.ds(start, width)], out, sem)
    copy.start()
    copy.wait()


def cut_tests(tests, size):
    rows, width = tests.shape
    return pl.pallas_call(
        cut_kernel,
        out_shape=jax.ShapeDtypeStruct((rows, width // size), tests.dtype),
        in_specs=[HBM],
        out_specs=VMEM,
        scratch_shapes=[pltpu.SemaphoreType.DMA],
        compiler_params=SMALL,
    )(in_hbm(tests))


COST = 1 << 32


def project_kernel(steps, share, ahead, piece, after, act, og, wi, wo, lens, *refs):
    refs = refs[after:]
    outs, (buf, wibuf, wobuf, lenbuf, sem, wsem) = refs[:-6], refs[-6:]
    me = lax.axis_index("tensor")
    rank = wibuf.shape[0]
    slots = buf.shape[2]
    count = len(steps) * share
    tokens = count * slots
    small = [
        pltpu.make_async_copy(wi, wibuf, wsem.at[0]),
        pltpu.make_async_copy(wo, wobuf, wsem.at[1]),
        pltpu.make_async_copy(lens, lenbuf, wsem.at[2]),
    ]
    pieces = [(side, at) for side, ref in enumerate((act, og)) for at in range(0, ref.shape[2], piece)]
    copies = []
    for slot, (side, at) in enumerate(pieces):
        width = min(piece, (act, og)[side].shape[2] - at)
        copies.append(
            [
                pltpu.make_async_copy(
                    (act, og)[side].at[pl.ds((me ^ step) * share, share), :, pl.ds(at, width)],
                    buf.at[slot, pl.ds(i * share, share), :, pl.ds(0, width)],
                    sem.at[slot, i],
                )
                for i, step in enumerate(steps)
            ]
        )
    small[0].start()
    for slot, group in enumerate(copies):
        if slot == 1:
            small[1].start()
            small[2].start()
        if slot < ahead:
            for copy in group:
                copy.start()
    sums = [None, None]
    for slot, (side, at) in enumerate(pieces):
        if at == 0:
            small[side].wait()
        for copy in copies[slot]:
            copy.wait()
        if slot + ahead < len(pieces):
            for copy in copies[slot + ahead]:
                copy.start()
        weight = (wibuf, wobuf)[side][:, at : at + piece]
        token = buf[slot].reshape(tokens, piece)[:, : weight.shape[1]]
        part = lax.dot_general(weight, token, NT, preferred_element_type=jnp.float32)
        sums[side] = part if sums[side] is None else sums[side] + part
    small[2].wait()
    col = lax.broadcasted_iota(jnp.int32, (rank, slots), 1)
    places = [out.at[i] for out in outs for i in range(out.shape[0])]
    for slot, out in enumerate(places):
        length = lenbuf[(me ^ steps[slot // share]) * share + slot % share]
        one = sums[0][:, slot * slots : (slot + 1) * slots] * (1.0 / length.astype(jnp.float32))
        out[:rank] = jnp.where(col < length, one, 0.0)
        out[rank:] = sums[1][:, slot * slots : (slot + 1) * slots]


def project(act, og, wi, wo, lens, groups, share, ahead, piece, after=()):
    steps = [step for group in groups for step in group]
    count = len(steps) * share
    slots, feat, hidden = act.shape[1], act.shape[2], og.shape[2]
    rank = wi.shape[0]
    pieces = -(-feat // piece) - (-hidden // piece)
    return pl.pallas_call(
        functools.partial(project_kernel, steps, share, ahead, piece, len(after)),
        out_shape=[jax.ShapeDtypeStruct((len(group) * share, 2 * rank, slots), jnp.float32) for group in groups],
        in_specs=[HBM] * 5 + [VMEM] * len(after),
        out_specs=[VMEM] * len(groups),
        scratch_shapes=[
            pltpu.VMEM((pieces, count, slots, piece), act.dtype),
            pltpu.VMEM((rank, feat), wi.dtype),
            pltpu.VMEM((rank, hidden), wo.dtype),
            pltpu.SMEM(lens.shape, lens.dtype),
            pltpu.SemaphoreType.DMA((pieces, len(steps))),
            pltpu.SemaphoreType.DMA((3,)),
        ],
        compiler_params=pltpu.CompilerParams(vmem_limit_bytes=32 << 20),
        cost_estimate=pl.CostEstimate(flops=COST, bytes_accessed=COST // 256, transcendentals=0),
    )(*map(in_hbm, (act, og, wi, wo, lens)), *after)


def unit_kernel(share, rank, size, *refs):
    parts, outs = refs[: -2 - size], refs[-2 - size : -2]
    pairs, held = refs[-2:]
    me = lax.axis_index("tensor")
    rows = rank * rank // 128
    span = rows // size
    dot = functools.partial(lax.dot_general, dimension_numbers=NT, preferred_element_type=jnp.float32)
    for k in range(share):
        full = parts[0][k]
        for part in parts[1:]:
            full = full + part[k]
        high = full.astype(jnp.bfloat16)
        low = (full - high.astype(jnp.float32)).astype(jnp.bfloat16)
        left, right = slice(None, rank), slice(rank, None)
        pairs[k] = dot(high[left], high[right]) + (dot(high[left], low[right]) + dot(low[left], high[right]))
    for k in range(share):
        even = pairs[k, pl.ds(0, rows, stride=2), :]
        odd = pairs[k, pl.ds(1, rows, stride=2), :]
        flat = jnp.concatenate([even, odd], axis=1)
        scale = jnp.sqrt(jnp.sum(flat * flat) / (rank * rank) + 1e-06)
        unit = flat / scale
        for to in range(size):
            held[to] = unit[to * span : (to + 1) * span]
        for step in range(size):
            outs[step][k] = held[me ^ step]


def units(parts, share, rank, size):
    span = rank * rank // 128 // size
    return pl.pallas_call(
        functools.partial(unit_kernel, share, rank, size),
        out_shape=[jax.ShapeDtypeStruct((share, span, 128), jnp.float32)] * size,
        in_specs=[VMEM] * len(parts),
        out_specs=[VMEM] * size,
        scratch_shapes=[pltpu.VMEM((share, rank, rank), jnp.float32), pltpu.VMEM((size, span, 128), jnp.float32)],
        compiler_params=SMALL,
    )(*parts)


def score_kernel(share, size, origins, *refs):
    unit_refs, test_refs, out, held = refs[:size], refs[size:-2], refs[-2], refs[-1]
    me, dp = lax.axis_index("tensor"), lax.axis_index("dp")
    for step in range(size):
        for k in range(share):
            held[(me ^ step) * share + k] = unit_refs[step][k]
    unit = jnp.concatenate([held[:, c, :] for c in range(held.shape[1])], axis=1).astype(jnp.bfloat16)
    tests = test_refs[0].shape[0]
    for (factor, offset, modulus), test_ref in zip(origins, test_refs):
        part = lax.dot_general(unit, test_ref[...], NT, preferred_element_type=jnp.float32)
        at = lax.rem(factor * dp + offset, modulus) * tests
        out[:, pl.ds(pl.multiple_of(at, 128), tests)] = part


def score(unit_parts, test_parts, share):
    size, groups = len(unit_parts), len(test_parts)
    tests, width = test_parts[0][0].shape
    origins = [origin for _, *origin in test_parts]
    return pl.pallas_call(
        functools.partial(score_kernel, share, size, origins),
        out_shape=jax.ShapeDtypeStruct((share * size, tests * groups), jnp.float32),
        in_specs=[VMEM] * (size + groups),
        out_specs=VMEM,
        scratch_shapes=[pltpu.VMEM((share * size, width // 128, 128), jnp.float32)],
        compiler_params=SMALL,
    )(*unit_parts, *(shard for shard, *_ in test_parts))


def gather_tests(own, groups):
    ring = [0, 1, 3, 2] if groups == 4 else list(range(groups))

    def shift(value, step):
        return lax.ppermute(value, "dp", [(ring[i], ring[(i + step) % groups]) for i in range(groups)])

    if groups == 4:
        first = shift(own, 1)
        return [(own, 1, 0, 4), (first, -2, 12, 5), (shift(own, -1), 2, 1, 5), (shift(first, 1), -1, 3, 4)]
    return [(own, 1, 0, groups)] + [(shift(own, step), 1, groups - step, groups) for step in range(1, groups)]


def shards(size, groups, activations, out_grads, proj_in, proj_out, lengths, test_grads):
    rank = proj_in.shape[1]
    share = activations.shape[0] // size
    own_tests = cut_tests(test_grads, size)
    tests = gather_tests(own_tests, groups)

    far = [CORES * x for x in range(1, size // CORES)]
    arrays = (activations, out_grads, proj_in.T, proj_out.T, lengths)
    far_other, far_own = project(*arrays, [[step ^ 1 for step in far], far], share, 4, 512, [own_tests])
    far_sum = far_own + xor_permute(far_other, "tensor", size, 1)
    sums = [xor_permute(far_sum[i * share : (i + 1) * share], "tensor", size, step) for i, step in enumerate(far)]
    here = xor_permute(tests[1][0][:16, :128], "tensor", size, 1)
    near_other, near_own = project(*arrays, [[1], [0]], share, 4, 512, [far_sum, here])
    arrived = jnp.concatenate([xor_permute(near_other[k : k + 1], "tensor", size, 1) for k in range(share)])

    unit_outs = units([near_own, arrived] + sums, share, rank, size)
    unit_parts = [unit_outs[0]] + [xor_permute(unit_outs[step], "tensor", size, step) for step in range(1, size)]
    part = score(unit_parts, tests, share)
    parts = [part] + [xor_permute(part, "tensor", size, step) for step in range(1, size)]
    while len(parts) > 1:
        parts = [parts[i] + parts[i + 1] for i in range(0, len(parts), 2)]
    return parts[0]


def solution(mesh):
    placed = (
        P(("groups", "dp"), None, "tensor"),
        P(("groups", "dp"), None, "tensor"),
        P("tensor", None),
        P("tensor", None),
        P(("groups", "dp")),
        P(("groups", "dp"), None),
    )
    return jax.shard_map(
        functools.partial(shards, mesh.shape["tensor"], mesh.shape["dp"]),
        mesh=mesh,
        in_specs=placed,
        out_specs=P(("groups", "dp"), None),
        check_vma=False,
    )
```

```python
import functools

import jax
import jax.numpy as jnp
from jax import lax
from jax.experimental import pallas as pl
from jax.experimental.pallas import tpu as pltpu
from jax.sharding import PartitionSpec as P

CORES = 2
SMALL = pltpu.CompilerParams(vmem_limit_bytes=8 << 20)
NT = (((1,), (1,)), ((), ()))
HBM = pl.BlockSpec(memory_space=pltpu.HBM)
in_hbm = functools.partial(pltpu.with_memory_space_constraint, memory_space=pltpu.HBM)
VMEM = pl.BlockSpec(memory_space=pltpu.VMEM)


def xor_permute(value, axis, size, step):
    return lax.ppermute(value, axis, [(i, i ^ step) for i in range(size)])


def cut_kernel(tests, out, sem):
    width = out.shape[1]
    start = pl.multiple_of(lax.axis_index("tensor") * width, 128)
    copy = pltpu.make_async_copy(tests.at[:, pl.ds(start, width)], out, sem)
    copy.start()
    copy.wait()


def cut_tests(tests, size):
    rows, width = tests.shape
    return pl.pallas_call(
        cut_kernel,
        out_shape=jax.ShapeDtypeStruct((rows, width // size), tests.dtype),
        in_specs=[HBM],
        out_specs=VMEM,
        scratch_shapes=[pltpu.SemaphoreType.DMA],
        compiler_params=SMALL,
    )(in_hbm(tests))


COST = 1 << 32
LATER = 1<<10


def project_kernel(steps, share, ahead, piece, after, act, og, wi, wo, lens, *refs):
    refs = refs[after:]
    outs, (buf, wibuf, wobuf, lenbuf, sem, wsem) = refs[:-6], refs[-6:]
    me = lax.axis_index("tensor")
    rank = wibuf.shape[0]
    slots = buf.shape[2]
    count = len(steps) * share
    tokens = count * slots
    small = [
        pltpu.make_async_copy(wi, wibuf, wsem.at[0]),
        pltpu.make_async_copy(wo, wobuf, wsem.at[1]),
        pltpu.make_async_copy(lens, lenbuf, wsem.at[2]),
    ]
    pieces = [(side, at) for side, ref in enumerate((act, og)) for at in range(0, ref.shape[2], piece)]
    copies = []
    for slot, (side, at) in enumerate(pieces):
        width = min(piece, (act, og)[side].shape[2] - at)
        copies.append(
            [
                pltpu.make_async_copy(
                    (act, og)[side].at[pl.ds((me ^ step) * share, share), :, pl.ds(at, width)],
                    buf.at[slot, pl.ds(i * share, share), :, pl.ds(0, width)],
                    sem.at[slot, i],
                )
                for i, step in enumerate(steps)
            ]
        )
    small[0].start()
    for slot, group in enumerate(copies):
        if slot == 1:
            small[1].start()
            small[2].start()
        if slot < ahead:
            for copy in group:
                copy.start()
    sums = [None, None]
    for slot, (side, at) in enumerate(pieces):
        if at == 0:
            small[side].wait()
        for copy in copies[slot]:
            copy.wait()
        if slot + ahead < len(pieces):
            for copy in copies[slot + ahead]:
                copy.start()
        weight = (wibuf, wobuf)[side][:, at : at + piece]
        token = buf[slot].reshape(tokens, piece)[:, : weight.shape[1]]
        part = lax.dot_general(weight, token, NT, preferred_element_type=jnp.float32)
        sums[side] = part if sums[side] is None else sums[side] + part
    small[2].wait()
    col = lax.broadcasted_iota(jnp.int32, (rank, slots), 1)
    places = [out.at[i] for out in outs for i in range(out.shape[0])]
    for slot, out in enumerate(places):
        length = lenbuf[(me ^ steps[slot // share]) * share + slot % share]
        one = sums[0][:, slot * slots : (slot + 1) * slots] * (1.0 / length.astype(jnp.float32))
        out[:rank] = jnp.where(col < length, one, 0.0)
        out[rank:] = sums[1][:, slot * slots : (slot + 1) * slots]


def project(act, og, wi, wo, lens, groups, share, ahead, piece, cost, after=()):
    steps = [step for group in groups for step in group]
    count = len(steps) * share
    slots, feat, hidden = act.shape[1], act.shape[2], og.shape[2]
    rank = wi.shape[0]
    pieces = -(-feat // piece) - (-hidden // piece)
    return pl.pallas_call(
        functools.partial(project_kernel, steps, share, ahead, piece, len(after)),
        out_shape=[jax.ShapeDtypeStruct((len(group) * share, 2 * rank, slots), jnp.float32) for group in groups],
        in_specs=[HBM] * 5 + [VMEM] * len(after),
        out_specs=[VMEM] * len(groups),
        scratch_shapes=[
            pltpu.VMEM((pieces, count, slots, piece), act.dtype),
            pltpu.VMEM((rank, feat), wi.dtype),
            pltpu.VMEM((rank, hidden), wo.dtype),
            pltpu.SMEM(lens.shape, lens.dtype),
            pltpu.SemaphoreType.DMA((pieces, len(steps))),
            pltpu.SemaphoreType.DMA((3,)),
        ],
        compiler_params=pltpu.CompilerParams(vmem_limit_bytes=32 << 20),
        cost_estimate=pl.CostEstimate(flops=cost, bytes_accessed=cost // 256, transcendentals=0),
    )(*map(in_hbm, (act, og, wi, wo, lens)), *after)


def unit_kernel(share, rank, size, *refs):
    parts, outs = refs[: -2 - size], refs[-2 - size : -2]
    pairs, held = refs[-2:]
    me = lax.axis_index("tensor")
    rows = rank * rank // 128
    span = rows // size
    dot = functools.partial(lax.dot_general, dimension_numbers=NT, preferred_element_type=jnp.float32)
    for k in range(share):
        full = parts[0][k]
        for part in parts[1:]:
            full = full + part[k]
        high = full.astype(jnp.bfloat16)
        low = (full - high.astype(jnp.float32)).astype(jnp.bfloat16)
        left, right = slice(None, rank), slice(rank, None)
        pairs[k] = dot(high[left], high[right]) + (dot(high[left], low[right]) + dot(low[left], high[right]))
    for k in range(share):
        even = pairs[k, pl.ds(0, rows, stride=2), :]
        odd = pairs[k, pl.ds(1, rows, stride=2), :]
        flat = jnp.concatenate([even, odd], axis=1)
        scale = jnp.sqrt(jnp.sum(flat * flat) / (rank * rank) + 1e-06)
        unit = flat / scale
        for to in range(size):
            held[to] = unit[to * span : (to + 1) * span]
        for step in range(size):
            outs[step][k] = held[me ^ step]


def units(parts, share, rank, size):
    span = rank * rank // 128 // size
    return pl.pallas_call(
        functools.partial(unit_kernel, share, rank, size),
        out_shape=[jax.ShapeDtypeStruct((share, span, 128), jnp.float32)] * size,
        in_specs=[VMEM] * len(parts),
        out_specs=[VMEM] * size,
        scratch_shapes=[pltpu.VMEM((share, rank, rank), jnp.float32), pltpu.VMEM((size, span, 128), jnp.float32)],
        compiler_params=SMALL,
    )(*parts)


def score_kernel(share, size, origins, *refs):
    unit_refs, test_refs, out, held = refs[:size], refs[size:-2], refs[-2], refs[-1]
    me, dp = lax.axis_index("tensor"), lax.axis_index("dp")
    for step in range(size):
        for k in range(share):
            held[(me ^ step) * share + k] = unit_refs[step][k]
    unit = jnp.concatenate([held[:, c, :] for c in range(held.shape[1])], axis=1).astype(jnp.bfloat16)
    tests = test_refs[0].shape[0]
    for (factor, offset, modulus), test_ref in zip(origins, test_refs):
        part = lax.dot_general(unit, test_ref[...], NT, preferred_element_type=jnp.float32)
        at = lax.rem(factor * dp + offset, modulus) * tests
        out[:, pl.ds(pl.multiple_of(at, 128), tests)] = part


def score(unit_parts, test_parts, share):
    size, groups = len(unit_parts), len(test_parts)
    tests, width = test_parts[0][0].shape
    origins = [origin for _, *origin in test_parts]
    return pl.pallas_call(
        functools.partial(score_kernel, share, size, origins),
        out_shape=jax.ShapeDtypeStruct((share * size, tests * groups), jnp.float32),
        in_specs=[VMEM] * (size + groups),
        out_specs=VMEM,
        scratch_shapes=[pltpu.VMEM((share * size, width // 128, 128), jnp.float32)],
        compiler_params=SMALL,
    )(*unit_parts, *(shard for shard, *_ in test_parts))


def gather_tests(own, groups):
    ring = [0, 1, 3, 2] if groups == 4 else list(range(groups))

    def shift(value, step):
        return lax.ppermute(value, "dp", [(ring[i], ring[(i + step) % groups]) for i in range(groups)])

    if groups == 4:
        first = shift(own, 1)
        return [(own, 1, 0, 4), (first, -2, 12, 5), (shift(own, -1), 2, 1, 5), (shift(first, 1), -1, 3, 4)]
    return [(own, 1, 0, groups)] + [(shift(own, step), 1, groups - step, groups) for step in range(1, groups)]


def shards(size, groups, activations, out_grads, proj_in, proj_out, lengths, test_grads):
    rank = proj_in.shape[1]
    share = activations.shape[0] // size
    own_tests = cut_tests(test_grads, size)
    tests = gather_tests(own_tests, groups)

    far = [CORES * x for x in range(1, size // CORES)]
    arrays = (activations, out_grads, proj_in.T, proj_out.T, lengths)
    far_other, far_own = project(*arrays, [[step ^ 1 for step in far], far], share, 4, 512, COST, [own_tests])
    far_sum = far_own + xor_permute(far_other, "tensor", size, 1)
    sums = [xor_permute(far_sum[i * share : (i + 1) * share], "tensor", size, step) for i, step in enumerate(far)]
    here = xor_permute(tests[1][0][:16, :128], "tensor", size, 1)
    near_other, near_own = project(*arrays, [[1], [0]], share, 4, 512, LATER, [far_sum, here])
    late = tests[2][0][: near_other.shape[1], : near_other.shape[2]].astype(jnp.float32)
    pieces = [near_other[k : k + 1] for k in range(share)]
    pieces[0] = pieces[0] + 0.0 * late[None]
    arrived = jnp.concatenate([xor_permute(one, "tensor", size, 1) for one in pieces])

    unit_outs = units([near_own, arrived] + sums, share, rank, size)
    unit_parts = [unit_outs[0]] + [xor_permute(unit_outs[step], "tensor", size, step) for step in range(1, size)]
    part = score(unit_parts, tests, share)
    parts = [part] + [xor_permute(part, "tensor", size, step) for step in range(1, size)]
    while len(parts) > 1:
        parts = [parts[i] + parts[i + 1] for i in range(0, len(parts), 2)]
    return parts[0]


def solution(mesh):
    placed = (
        P(("groups", "dp"), None, "tensor"),
        P(("groups", "dp"), None, "tensor"),
        P("tensor", None),
        P("tensor", None),
        P(("groups", "dp")),
        P(("groups", "dp"), None),
    )
    return jax.shard_map(
        functools.partial(shards, mesh.shape["tensor"], mesh.shape["dp"]),
        mesh=mesh,
        in_specs=placed,
        out_specs=P(("groups", "dp"), None),
        check_vma=False,
    )
```

```python
import functools

import jax
import jax.numpy as jnp
from jax import lax
from jax.experimental import pallas as pl
from jax.experimental.pallas import tpu as pltpu
from jax.sharding import PartitionSpec as P

CORES = 2
SMALL = pltpu.CompilerParams(vmem_limit_bytes=8 << 20)
NT = (((1,), (1,)), ((), ()))
HBM = pl.BlockSpec(memory_space=pltpu.HBM)
in_hbm = functools.partial(pltpu.with_memory_space_constraint, memory_space=pltpu.HBM)
VMEM = pl.BlockSpec(memory_space=pltpu.VMEM)


def xor_permute(value, axis, size, step):
    return lax.ppermute(value, axis, [(i, i ^ step) for i in range(size)])


def cut_kernel(tests, out, sem):
    width = out.shape[1]
    start = pl.multiple_of(lax.axis_index("tensor") * width, 128)
    copy = pltpu.make_async_copy(tests.at[:, pl.ds(start, width)], out, sem)
    copy.start()
    copy.wait()


def cut_tests(tests, size):
    rows, width = tests.shape
    return pl.pallas_call(
        cut_kernel,
        out_shape=jax.ShapeDtypeStruct((rows, width // size), tests.dtype),
        in_specs=[HBM],
        out_specs=VMEM,
        scratch_shapes=[pltpu.SemaphoreType.DMA],
        compiler_params=SMALL,
    )(in_hbm(tests))


COST = 1 << 32
LATER = 1<<10


def project_kernel(blocks, share, ahead, piece, after, act, og, wi, wo, lens, *refs):
    refs = refs[after:]
    outs, (buf, wibuf, wobuf, lenbuf, sem, wsem) = refs[:-6], refs[-6:]
    me = lax.axis_index("tensor")
    rank = wibuf.shape[0]
    count, slots = buf.shape[1:3]
    tokens = count * slots
    starts = [(me ^ step) * share + first for step, first, _ in blocks]
    ends = [sum(size for *_, size in blocks[: i + 1]) for i in range(len(blocks))]
    small = [
        pltpu.make_async_copy(wi, wibuf, wsem.at[0]),
        pltpu.make_async_copy(wo, wobuf, wsem.at[1]),
        pltpu.make_async_copy(lens, lenbuf, wsem.at[2]),
    ]
    pieces = [(side, at) for side, ref in enumerate((act, og)) for at in range(0, ref.shape[2], piece)]
    copies = []
    for slot, (side, at) in enumerate(pieces):
        width = min(piece, (act, og)[side].shape[2] - at)
        copies.append(
            [
                pltpu.make_async_copy(
                    (act, og)[side].at[pl.ds(start, size), :, pl.ds(at, width)],
                    buf.at[slot, pl.ds(end - size, size), :, pl.ds(0, width)],
                    sem.at[slot, i],
                )
                for i, (start, end, (*_, size)) in enumerate(zip(starts, ends, blocks))
            ]
        )
    small[0].start()
    for slot, group in enumerate(copies):
        if slot == 1:
            small[1].start()
            small[2].start()
        if slot < ahead:
            for copy in group:
                copy.start()
    sums = [None, None]
    for slot, (side, at) in enumerate(pieces):
        if at == 0:
            small[side].wait()
        for copy in copies[slot]:
            copy.wait()
        if slot + ahead < len(pieces):
            for copy in copies[slot + ahead]:
                copy.start()
        weight = (wibuf, wobuf)[side][:, at : at + piece]
        token = buf[slot].reshape(tokens, piece)[:, : weight.shape[1]]
        part = lax.dot_general(weight, token, NT, preferred_element_type=jnp.float32)
        sums[side] = part if sums[side] is None else sums[side] + part
    small[2].wait()
    col = lax.broadcasted_iota(jnp.int32, (rank, slots), 1)
    places = [out.at[i] for out in outs for i in range(out.shape[0])]
    seqs = [start + k for start, (*_, size) in zip(starts, blocks) for k in range(size)]
    for slot, (out, seq) in enumerate(zip(places, seqs)):
        length = lenbuf[seq]
        one = sums[0][:, slot * slots : (slot + 1) * slots] * (1.0 / length.astype(jnp.float32))
        out[:rank] = jnp.where(col < length, one, 0.0)
        out[rank:] = sums[1][:, slot * slots : (slot + 1) * slots]


def project(act, og, wi, wo, lens, groups, share, ahead, piece, cost, after=()):
    blocks = [block for group in groups for block in group]
    counts = [sum(size for *_, size in group) for group in groups]
    count = sum(counts)
    slots, feat, hidden = act.shape[1], act.shape[2], og.shape[2]
    rank = wi.shape[0]
    pieces = -(-feat // piece) - (-hidden // piece)
    return pl.pallas_call(
        functools.partial(project_kernel, blocks, share, ahead, piece, len(after)),
        out_shape=[jax.ShapeDtypeStruct((size, 2 * rank, slots), jnp.float32) for size in counts],
        in_specs=[HBM] * 5 + [VMEM] * len(after),
        out_specs=[VMEM] * len(groups),
        scratch_shapes=[
            pltpu.VMEM((pieces, count, slots, piece), act.dtype),
            pltpu.VMEM((rank, feat), wi.dtype),
            pltpu.VMEM((rank, hidden), wo.dtype),
            pltpu.SMEM(lens.shape, lens.dtype),
            pltpu.SemaphoreType.DMA((pieces, len(blocks))),
            pltpu.SemaphoreType.DMA((3,)),
        ],
        compiler_params=pltpu.CompilerParams(vmem_limit_bytes=32 << 20),
        cost_estimate=pl.CostEstimate(flops=cost, bytes_accessed=cost // 256, transcendentals=0),
    )(*map(in_hbm, (act, og, wi, wo, lens)), *after)


def unit_kernel(share, rank, size, *refs):
    parts, outs = refs[: -2 - size], refs[-2 - size : -2]
    pairs, held = refs[-2:]
    me = lax.axis_index("tensor")
    rows = rank * rank // 128
    span = rows // size
    dot = functools.partial(lax.dot_general, dimension_numbers=NT, preferred_element_type=jnp.float32)
    for k in range(share):
        full = parts[0][k]
        for part in parts[1:]:
            full = full + part[k]
        high = full.astype(jnp.bfloat16)
        low = (full - high.astype(jnp.float32)).astype(jnp.bfloat16)
        left, right = slice(None, rank), slice(rank, None)
        pairs[k] = dot(high[left], high[right]) + (dot(high[left], low[right]) + dot(low[left], high[right]))
    for k in range(share):
        even = pairs[k, pl.ds(0, rows, stride=2), :]
        odd = pairs[k, pl.ds(1, rows, stride=2), :]
        flat = jnp.concatenate([even, odd], axis=1)
        scale = jnp.sqrt(jnp.sum(flat * flat) / (rank * rank) + 1e-06)
        unit = flat / scale
        for to in range(size):
            held[to] = unit[to * span : (to + 1) * span]
        for step in range(size):
            outs[step][k] = held[me ^ step]


def units(parts, share, rank, size):
    span = rank * rank // 128 // size
    return pl.pallas_call(
        functools.partial(unit_kernel, share, rank, size),
        out_shape=[jax.ShapeDtypeStruct((share, span, 128), jnp.float32)] * size,
        in_specs=[VMEM] * len(parts),
        out_specs=[VMEM] * size,
        scratch_shapes=[pltpu.VMEM((share, rank, rank), jnp.float32), pltpu.VMEM((size, span, 128), jnp.float32)],
        compiler_params=SMALL,
    )(*parts)


def score_kernel(share, size, origins, *refs):
    unit_refs, test_refs, out, held = refs[:size], refs[size:-2], refs[-2], refs[-1]
    me, dp = lax.axis_index("tensor"), lax.axis_index("dp")
    for step in range(size):
        for k in range(share):
            held[(me ^ step) * share + k] = unit_refs[step][k]
    unit = jnp.concatenate([held[:, c, :] for c in range(held.shape[1])], axis=1).astype(jnp.bfloat16)
    tests = test_refs[0].shape[0]
    for (factor, offset, modulus), test_ref in zip(origins, test_refs):
        part = lax.dot_general(unit, test_ref[...], NT, preferred_element_type=jnp.float32)
        at = lax.rem(factor * dp + offset, modulus) * tests
        out[:, pl.ds(pl.multiple_of(at, 128), tests)] = part


def score(unit_parts, test_parts, share):
    size, groups = len(unit_parts), len(test_parts)
    tests, width = test_parts[0][0].shape
    origins = [origin for _, *origin in test_parts]
    return pl.pallas_call(
        functools.partial(score_kernel, share, size, origins),
        out_shape=jax.ShapeDtypeStruct((share * size, tests * groups), jnp.float32),
        in_specs=[VMEM] * (size + groups),
        out_specs=VMEM,
        scratch_shapes=[pltpu.VMEM((share * size, width // 128, 128), jnp.float32)],
        compiler_params=SMALL,
    )(*unit_parts, *(shard for shard, *_ in test_parts))


def gather_tests(own, groups):
    ring = [0, 1, 3, 2] if groups == 4 else list(range(groups))

    def shift(value, step):
        return lax.ppermute(value, "dp", [(ring[i], ring[(i + step) % groups]) for i in range(groups)])

    if groups == 4:
        first = shift(own, 1)
        return [(own, 1, 0, 4), (first, -2, 12, 5), (shift(own, -1), 2, 1, 5), (shift(first, 1), -1, 3, 4)]
    return [(own, 1, 0, groups)] + [(shift(own, step), 1, groups - step, groups) for step in range(1, groups)]


def shards(size, groups, activations, out_grads, proj_in, proj_out, lengths, test_grads):
    rank = proj_in.shape[1]
    share = activations.shape[0] // size
    own_tests = cut_tests(test_grads, size)
    tests = gather_tests(own_tests, groups)

    far = [CORES * x for x in range(1, size // CORES)]
    arrays = (activations, out_grads, proj_in.T, proj_out.T, lengths)
    early = share // 2
    sends = [[(step ^ 1, 0, share) for step in far], [(step, 0, share) for step in far]]
    far_other, far_own, *near_first = project(
        *arrays, sends + [[(1, 0, early)]] * bool(early), share, 4, 512, COST, [own_tests]
    )
    far_sum = far_own + xor_permute(far_other, "tensor", size, 1)
    sums = [xor_permute(far_sum[i * share : (i + 1) * share], "tensor", size, step) for i, step in enumerate(far)]
    here = xor_permute(tests[1][0][:16, :128], "tensor", size, 1)
    groups_left = [[(1, early, share - early)], [(0, 0, share)]]
    near_other, near_own = project(*arrays, groups_left, share, 5, 512, LATER, [far_sum, here])
    late = tests[2][0][: near_other.shape[1], : near_other.shape[2]].astype(jnp.float32)
    pieces = [near_other[k : k + 1] for k in range(share - early)]
    pieces[0] = pieces[0] + 0.0 * late[None]
    arrived = jnp.concatenate([xor_permute(one, "tensor", size, 1) for one in near_first + pieces])

    unit_outs = units([near_own, arrived] + sums, share, rank, size)
    unit_parts = [unit_outs[0]] + [xor_permute(unit_outs[step], "tensor", size, step) for step in range(1, size)]
    part = score(unit_parts, tests, share)
    parts = [part] + [xor_permute(part, "tensor", size, step) for step in range(1, size)]
    while len(parts) > 1:
        parts = [parts[i] + parts[i + 1] for i in range(0, len(parts), 2)]
    return parts[0]


def solution(mesh):
    placed = (
        P(("groups", "dp"), None, "tensor"),
        P(("groups", "dp"), None, "tensor"),
        P("tensor", None),
        P("tensor", None),
        P(("groups", "dp")),
        P(("groups", "dp"), None),
    )
    return jax.shard_map(
        functools.partial(shards, mesh.shape["tensor"], mesh.shape["dp"]),
        mesh=mesh,
        in_specs=placed,
        out_specs=P(("groups", "dp"), None),
        check_vma=False,
    )
```

```python
import functools

import jax
import jax.numpy as jnp
from jax import lax
from jax.experimental import pallas as pl
from jax.experimental.pallas import tpu as pltpu
from jax.sharding import PartitionSpec as P

CORES = 2
SMALL = pltpu.CompilerParams(vmem_limit_bytes=8 << 20)
NT = (((1,), (1,)), ((), ()))
HBM = pl.BlockSpec(memory_space=pltpu.HBM)
in_hbm = functools.partial(pltpu.with_memory_space_constraint, memory_space=pltpu.HBM)
VMEM = pl.BlockSpec(memory_space=pltpu.VMEM)


def xor_permute(value, axis, size, step):
    return lax.ppermute(value, axis, [(i, i ^ step) for i in range(size)])


def first_kernel(tests, wi, wo, own, wide, wibuf, wobuf, sem):
    width = own.shape[1]
    start = pl.multiple_of(lax.axis_index("tensor") * width, 128)
    copies = [
        pltpu.make_async_copy(wi, wibuf, sem.at[0]),
        pltpu.make_async_copy(wo, wobuf, sem.at[1]),
        pltpu.make_async_copy(tests.at[:, pl.ds(start, width)], own, sem.at[2]),
    ]
    for copy in copies:
        copy.start()
    feat = wibuf.shape[1]
    for side, buf in enumerate((wibuf, wobuf)):
        copies[side].wait()
        for at in range(0, buf.shape[1], 256):
            weight = buf[:, at : at + 256]
            none = jnp.zeros_like(weight)
            both = jnp.concatenate([none, weight] if side else [weight, none], axis=0)
            wide[side * feat + at : side * feat + at + weight.shape[1]] = both.T
    copies[2].wait()


def first(tests, wi, wo, size):
    rows, width = tests.shape
    rank, feat = wi.shape
    return pl.pallas_call(
        first_kernel,
        out_shape=[
            jax.ShapeDtypeStruct((rows, width // size), tests.dtype),
            jax.ShapeDtypeStruct((feat + wo.shape[1], 2 * rank), wi.dtype),
        ],
        in_specs=[HBM] * 3,
        out_specs=[VMEM] * 2,
        scratch_shapes=[pltpu.VMEM(wi.shape, wi.dtype), pltpu.VMEM(wo.shape, wo.dtype), pltpu.SemaphoreType.DMA((3,))],
        compiler_params=SMALL,
    )(in_hbm(tests), in_hbm(wi), in_hbm(wo))


COST = 1 << 32
LATER = 1<<10


def project_kernel(steps, share, ahead, piece, after, act, og, lens, wide, *refs):
    refs = refs[after:]
    outs, (buf, lenbuf, sem, lensem) = refs[:-4], refs[-4:]
    me = lax.axis_index("tensor")
    rank = wide.shape[1] // 2
    slots, feat = act.shape[1:]
    lencopy = pltpu.make_async_copy(lens, lenbuf, lensem)
    pieces = [
        (side, at, min(piece, ref.shape[2] - at)) for side, ref in enumerate((act, og)) for at in range(0, ref.shape[2], piece)
    ]
    copies = [
        [
            pltpu.make_async_copy(
                (act, og)[side].at[pl.ds((me ^ step) * share, share), :, pl.ds(at, width)],
                buf.at[slot, pl.ds(i * share, share), :, pl.ds(0, width)],
                sem.at[slot, i],
            )
            for i, step in enumerate(steps)
        ]
        for slot, (side, at, width) in enumerate(pieces)
    ]
    for group in copies[:ahead]:
        for copy in group:
            copy.start()
    lencopy.start()
    sums = [None] * len(steps)
    for slot, (side, at, width) in enumerate(pieces):
        for copy in copies[slot]:
            copy.wait()
        for copy in copies[slot + ahead] if slot + ahead < len(copies) else ():
            copy.start()
        weight = wide[side * feat + at : side * feat + at + width]
        for i in range(len(steps)):
            token = buf[slot, i * share : (i + 1) * share].reshape(share * slots, piece)[:, :width]
            part = jnp.dot(token, weight, preferred_element_type=jnp.float32)
            sums[i] = part if sums[i] is None else sums[i] + part
    lencopy.wait()
    col = lax.broadcasted_iota(jnp.int32, (rank, slots), 1)
    places = [out.at[i] for out in outs for i in range(out.shape[0])]
    for slot, out in enumerate(places):
        i, k = divmod(slot, share)
        length = lenbuf[(me ^ steps[i]) * share + k]
        both = sums[i][k * slots : (k + 1) * slots].T
        out[:rank] = jnp.where(col < length, both[:rank] * (1.0 / length.astype(jnp.float32)), 0.0)
        out[rank:] = both[rank:]


def project(act, og, lens, wide, groups, share, ahead, piece, cost, after=()):
    steps = [step for group in groups for step in group]
    count = len(steps) * share
    slots, feat, hidden = act.shape[1], act.shape[2], og.shape[2]
    pieces = -(-feat // piece) - (-hidden // piece)
    return pl.pallas_call(
        functools.partial(project_kernel, steps, share, ahead, piece, len(after)),
        out_shape=[jax.ShapeDtypeStruct((len(group) * share, wide.shape[1], slots), jnp.float32) for group in groups],
        in_specs=[HBM] * 3 + [VMEM] * (1 + len(after)),
        out_specs=[VMEM] * len(groups),
        scratch_shapes=[
            pltpu.VMEM((pieces, count, slots, piece), act.dtype),
            pltpu.SMEM(lens.shape, lens.dtype),
            pltpu.SemaphoreType.DMA((pieces, len(steps))),
            pltpu.SemaphoreType.DMA,
        ],
        compiler_params=pltpu.CompilerParams(vmem_limit_bytes=32 << 20),
        cost_estimate=pl.CostEstimate(flops=cost, bytes_accessed=cost // 256, transcendentals=0),
    )(*map(in_hbm, (act, og, lens)), wide, *after)


def unit_kernel(share, rank, size, *refs):
    parts, outs = refs[: -2 - size], refs[-2 - size : -2]
    pairs, held = refs[-2:]
    me = lax.axis_index("tensor")
    rows = rank * rank // 128
    span = rows // size
    dot = functools.partial(lax.dot_general, dimension_numbers=NT, preferred_element_type=jnp.float32)
    for k in range(share):
        full = parts[0][k]
        for part in parts[1:]:
            full = full + part[k]
        high = full.astype(jnp.bfloat16)
        low = (full - high.astype(jnp.float32)).astype(jnp.bfloat16)
        left, right = slice(None, rank), slice(rank, None)
        pairs[k] = dot(high[left], high[right]) + (dot(high[left], low[right]) + dot(low[left], high[right]))
    for k in range(share):
        even = pairs[k, pl.ds(0, rows, stride=2), :]
        odd = pairs[k, pl.ds(1, rows, stride=2), :]
        flat = jnp.concatenate([even, odd], axis=1)
        scale = jnp.sqrt(jnp.sum(flat * flat) / (rank * rank) + 1e-06)
        unit = flat / scale
        for to in range(size):
            held[to] = unit[to * span : (to + 1) * span]
        for step in range(size):
            outs[step][k] = held[me ^ step]


def units(parts, share, rank, size):
    span = rank * rank // 128 // size
    return pl.pallas_call(
        functools.partial(unit_kernel, share, rank, size),
        out_shape=[jax.ShapeDtypeStruct((share, span, 128), jnp.float32)] * size,
        in_specs=[VMEM] * len(parts),
        out_specs=[VMEM] * size,
        scratch_shapes=[pltpu.VMEM((share, rank, rank), jnp.float32), pltpu.VMEM((size, span, 128), jnp.float32)],
        compiler_params=SMALL,
    )(*parts)


def score_kernel(share, size, origins, *refs):
    unit_refs, test_refs, out, held = refs[:size], refs[size:-2], refs[-2], refs[-1]
    me, dp = lax.axis_index("tensor"), lax.axis_index("dp")
    for step in range(size):
        for k in range(share):
            held[(me ^ step) * share + k] = unit_refs[step][k]
    unit = jnp.concatenate([held[:, c, :] for c in range(held.shape[1])], axis=1).astype(jnp.bfloat16)
    tests = test_refs[0].shape[0]
    for (factor, offset, modulus), test_ref in zip(origins, test_refs):
        part = lax.dot_general(unit, test_ref[...], NT, preferred_element_type=jnp.float32)
        at = lax.rem(factor * dp + offset, modulus) * tests
        out[:, pl.ds(pl.multiple_of(at, 128), tests)] = part


def score(unit_parts, test_parts, share):
    size, groups = len(unit_parts), len(test_parts)
    tests, width = test_parts[0][0].shape
    origins = [origin for _, *origin in test_parts]
    return pl.pallas_call(
        functools.partial(score_kernel, share, size, origins),
        out_shape=jax.ShapeDtypeStruct((share * size, tests * groups), jnp.float32),
        in_specs=[VMEM] * (size + groups),
        out_specs=VMEM,
        scratch_shapes=[pltpu.VMEM((share * size, width // 128, 128), jnp.float32)],
        compiler_params=SMALL,
    )(*unit_parts, *(shard for shard, *_ in test_parts))


def gather_tests(own, groups):
    ring = [0, 1, 3, 2] if groups == 4 else list(range(groups))

    def shift(value, step):
        return lax.ppermute(value, "dp", [(ring[i], ring[(i + step) % groups]) for i in range(groups)])

    if groups == 4:
        first = shift(own, 1)
        return [(own, 1, 0, 4), (first, -2, 12, 5), (shift(own, -1), 2, 1, 5), (shift(first, 1), -1, 3, 4)]
    return [(own, 1, 0, groups)] + [(shift(own, step), 1, groups - step, groups) for step in range(1, groups)]


def shards(size, groups, activations, out_grads, proj_in, proj_out, lengths, test_grads):
    rank = proj_in.shape[1]
    share = activations.shape[0] // size
    own_tests, wide = first(test_grads, proj_in.T, proj_out.T, size)
    tests = gather_tests(own_tests, groups)

    far = [CORES * x for x in range(1, size // CORES)]
    arrays = (activations, out_grads, lengths, wide)
    far_other, far_own = project(*arrays, [[step ^ 1 for step in far], far], share, 4, 512, COST, [own_tests])
    far_sum = far_own + xor_permute(far_other, "tensor", size, 1)
    sums = [xor_permute(far_sum[i * share : (i + 1) * share], "tensor", size, step) for i, step in enumerate(far)]
    here = xor_permute(tests[1][0][:16, :128], "tensor", size, 1)
    near_other, near_own = project(*arrays, [[1], [0]], share, 4, 512, LATER, [far_sum, here])
    late = tests[2][0][: near_other.shape[1], : near_other.shape[2]].astype(jnp.float32)
    pieces = [near_other[k : k + 1] for k in range(share)]
    pieces[0] = pieces[0] + 0.0 * late[None]
    arrived = jnp.concatenate([xor_permute(one, "tensor", size, 1) for one in pieces])

    unit_outs = units([near_own, arrived] + sums, share, rank, size)
    unit_parts = [unit_outs[0]] + [xor_permute(unit_outs[step], "tensor", size, step) for step in range(1, size)]
    part = score(unit_parts, tests, share)
    parts = [part] + [xor_permute(part, "tensor", size, step) for step in range(1, size)]
    while len(parts) > 1:
        parts = [parts[i] + parts[i + 1] for i in range(0, len(parts), 2)]
    return parts[0]


def solution(mesh):
    placed = (
        P(("groups", "dp"), None, "tensor"),
        P(("groups", "dp"), None, "tensor"),
        P("tensor", None),
        P("tensor", None),
        P(("groups", "dp")),
        P(("groups", "dp"), None),
    )
    return jax.shard_map(
        functools.partial(shards, mesh.shape["tensor"], mesh.shape["dp"]),
        mesh=mesh,
        in_specs=placed,
        out_specs=P(("groups", "dp"), None),
        check_vma=False,
    )
```

```python
import functools

import jax
import jax.numpy as jnp
from jax import lax
from jax.experimental import pallas as pl
from jax.experimental.pallas import tpu as pltpu
from jax.sharding import PartitionSpec as P

CORES = 2
SMALL = pltpu.CompilerParams(vmem_limit_bytes=8 << 20)
NT = (((1,), (1,)), ((), ()))
HBM = pl.BlockSpec(memory_space=pltpu.HBM)
in_hbm = functools.partial(pltpu.with_memory_space_constraint, memory_space=pltpu.HBM)
VMEM = pl.BlockSpec(memory_space=pltpu.VMEM)


def xor_permute(value, axis, size, step):
    return lax.ppermute(value, axis, [(i, i ^ step) for i in range(size)])


def cut_kernel(tests, out, sem):
    width = out.shape[1]
    start = pl.multiple_of(lax.axis_index("tensor") * width, 128)
    copy = pltpu.make_async_copy(tests.at[:, pl.ds(start, width)], out, sem)
    copy.start()
    copy.wait()


def cut_tests(tests, size):
    rows, width = tests.shape
    return pl.pallas_call(
        cut_kernel,
        out_shape=jax.ShapeDtypeStruct((rows, width // size), tests.dtype),
        in_specs=[HBM],
        out_specs=VMEM,
        scratch_shapes=[pltpu.SemaphoreType.DMA],
        compiler_params=SMALL,
    )(in_hbm(tests))


COST = 1 << 32
LATER = 1<<10


def project_kernel(steps, share, ahead, piece, after, act, og, wi, wo, lens, *refs):
    refs = refs[after:]
    outs, (buf, wibuf, wobuf, lenbuf, sem, wsem) = refs[:-6], refs[-6:]
    me = lax.axis_index("tensor")
    rank = wibuf.shape[0]
    slots = buf.shape[2]
    count = len(steps) * share
    tokens = count * slots
    small = [
        pltpu.make_async_copy(wi, wibuf, wsem.at[0]),
        pltpu.make_async_copy(wo, wobuf, wsem.at[1]),
        pltpu.make_async_copy(lens, lenbuf, wsem.at[2]),
    ]
    pieces = [(side, at) for side, ref in enumerate((act, og)) for at in range(0, ref.shape[2], piece)]
    copies = []
    for slot, (side, at) in enumerate(pieces):
        width = min(piece, (act, og)[side].shape[2] - at)
        copies.append(
            [
                pltpu.make_async_copy(
                    (act, og)[side].at[pl.ds((me ^ step) * share, share), :, pl.ds(at, width)],
                    buf.at[slot, pl.ds(i * share, share), :, pl.ds(0, width)],
                    sem.at[slot, i],
                )
                for i, step in enumerate(steps)
            ]
        )
    small[0].start()
    for slot, group in enumerate(copies):
        if slot == 1:
            small[1].start()
            small[2].start()
        if slot < ahead:
            for copy in group:
                copy.start()
    sums = [None, None]
    for slot, (side, at) in enumerate(pieces):
        if at == 0:
            small[side].wait()
        for copy in copies[slot]:
            copy.wait()
        if slot + ahead < len(pieces):
            for copy in copies[slot + ahead]:
                copy.start()
        weight = (wibuf, wobuf)[side][:, at : at + piece]
        token = buf[slot].reshape(tokens, piece)[:, : weight.shape[1]]
        part = lax.dot_general(weight, token, NT, preferred_element_type=jnp.float32)
        sums[side] = part if sums[side] is None else sums[side] + part
    small[2].wait()
    col = lax.broadcasted_iota(jnp.int32, (rank, slots), 1)
    places = [out.at[i] for out in outs for i in range(out.shape[0])]
    for slot, out in enumerate(places):
        length = lenbuf[(me ^ steps[slot // share]) * share + slot % share]
        one = sums[0][:, slot * slots : (slot + 1) * slots] * (1.0 / length.astype(jnp.float32))
        out[:rank] = jnp.where(col < length, one, 0.0)
        out[rank:] = sums[1][:, slot * slots : (slot + 1) * slots]


def project(act, og, wi, wo, lens, groups, share, ahead, piece, cost, after=()):
    steps = [step for group in groups for step in group]
    count = len(steps) * share
    slots, feat, hidden = act.shape[1], act.shape[2], og.shape[2]
    rank = wi.shape[0]
    pieces = -(-feat // piece) - (-hidden // piece)
    return pl.pallas_call(
        functools.partial(project_kernel, steps, share, ahead, piece, len(after)),
        out_shape=[jax.ShapeDtypeStruct((len(group) * share, 2 * rank, slots), jnp.float32) for group in groups],
        in_specs=[HBM] * 5 + [VMEM] * len(after),
        out_specs=[VMEM] * len(groups),
        scratch_shapes=[
            pltpu.VMEM((pieces, count, slots, piece), act.dtype),
            pltpu.VMEM((rank, feat), wi.dtype),
            pltpu.VMEM((rank, hidden), wo.dtype),
            pltpu.SMEM(lens.shape, lens.dtype),
            pltpu.SemaphoreType.DMA((pieces, len(steps))),
            pltpu.SemaphoreType.DMA((3,)),
        ],
        compiler_params=pltpu.CompilerParams(vmem_limit_bytes=32 << 20),
        cost_estimate=pl.CostEstimate(flops=cost, bytes_accessed=cost // 256, transcendentals=0),
    )(*map(in_hbm, (act, og, wi, wo, lens)), *after)


def unit_kernel(share, rank, size, *refs):
    parts, outs = refs[: -2 - size], refs[-2 - size : -2]
    pairs, held = refs[-2:]
    me = lax.axis_index("tensor")
    rows = rank * rank // 128
    span = rows // size
    dot = functools.partial(lax.dot_general, dimension_numbers=NT, preferred_element_type=jnp.float32)
    for k in range(share):
        full = parts[0][k]
        for part in parts[1:]:
            full = full + part[k]
        high = full.astype(jnp.bfloat16)
        low = (full - high.astype(jnp.float32)).astype(jnp.bfloat16)
        left, right = slice(None, rank), slice(rank, None)
        pairs[k] = dot(high[left], high[right]) + (dot(high[left], low[right]) + dot(low[left], high[right]))
    for k in range(share):
        even = pairs[k, pl.ds(0, rows, stride=2), :]
        odd = pairs[k, pl.ds(1, rows, stride=2), :]
        flat = jnp.concatenate([even, odd], axis=1)
        scale = jnp.sqrt(jnp.sum(flat * flat) / (rank * rank) + 1e-06)
        unit = flat / scale
        for to in range(size):
            held[to] = unit[to * span : (to + 1) * span]
        for step in range(size):
            outs[step][k] = held[me ^ step]


def units(parts, share, rank, size):
    span = rank * rank // 128 // size
    return pl.pallas_call(
        functools.partial(unit_kernel, share, rank, size),
        out_shape=[jax.ShapeDtypeStruct((share, span, 128), jnp.float32)] * size,
        in_specs=[VMEM] * len(parts),
        out_specs=[VMEM] * size,
        scratch_shapes=[pltpu.VMEM((share, rank, rank), jnp.float32), pltpu.VMEM((size, span, 128), jnp.float32)],
        compiler_params=SMALL,
    )(*parts)


def score_kernel(share, size, origins, *refs):
    unit_refs, test_refs, out, held = refs[:size], refs[size:-2], refs[-2], refs[-1]
    me, dp = lax.axis_index("tensor"), lax.axis_index("dp")
    for step in range(size):
        for k in range(share):
            held[(me ^ step) * share + k] = unit_refs[step][k]
    unit = jnp.concatenate([held[:, c, :] for c in range(held.shape[1])], axis=1).astype(jnp.bfloat16)
    tests = test_refs[0].shape[0]
    for (factor, offset, modulus), test_ref in zip(origins, test_refs):
        part = lax.dot_general(unit, test_ref[...], NT, preferred_element_type=jnp.float32)
        at = lax.rem(factor * dp + offset, modulus) * tests
        out[:, pl.ds(pl.multiple_of(at, 128), tests)] = part


def score(unit_parts, test_parts, share):
    size, groups = len(unit_parts), len(test_parts)
    tests, width = test_parts[0][0].shape
    origins = [origin for _, *origin in test_parts]
    return pl.pallas_call(
        functools.partial(score_kernel, share, size, origins),
        out_shape=jax.ShapeDtypeStruct((share * size, tests * groups), jnp.float32),
        in_specs=[VMEM] * (size + groups),
        out_specs=VMEM,
        scratch_shapes=[pltpu.VMEM((share * size, width // 128, 128), jnp.float32)],
        compiler_params=SMALL,
    )(*unit_parts, *(shard for shard, *_ in test_parts))


def gather_tests(own, groups):
    ring = [0, 2, 3, 1] if groups == 4 else list(range(groups))

    def shift(value, step):
        return lax.ppermute(value, "dp", [(ring[i], ring[(i + step) % groups]) for i in range(groups)])

    if groups == 4:
        first = shift(own, 1)
        return [(own, 1, 0, 4), (first, 2, 1, 5), (shift(own, -1), -2, 12, 5), (shift(first, 1), -1, 3, 4)]
    return [(own, 1, 0, groups)] + [(shift(own, step), 1, groups - step, groups) for step in range(1, groups)]


def shards(size, groups, activations, out_grads, proj_in, proj_out, lengths, test_grads):
    rank = proj_in.shape[1]
    share = activations.shape[0] // size
    own_tests = cut_tests(test_grads, size)
    tests = gather_tests(own_tests, groups)

    far = [CORES * x for x in range(1, size // CORES)]
    arrays = (activations, out_grads, proj_in.T, proj_out.T, lengths)
    far_other, far_own = project(*arrays, [[step ^ 1 for step in far], far], share, 4, 512, COST, [own_tests])
    far_sum = far_own + xor_permute(far_other, "tensor", size, 1)
    sums = [xor_permute(far_sum[i * share : (i + 1) * share], "tensor", size, step) for i, step in enumerate(far)]
    here = xor_permute(tests[1][0][:16, :128], "tensor", size, 1)
    near_other, near_own = project(*arrays, [[1], [0]], share, 4, 512, LATER, [far_sum, here])
    late = tests[2][0][: near_other.shape[1], : near_other.shape[2]].astype(jnp.float32)
    pieces = [near_other[k : k + 1] for k in range(share)]
    pieces[0] = pieces[0] + 0.0 * late[None]
    arrived = jnp.concatenate([xor_permute(one, "tensor", size, 1) for one in pieces])

    unit_outs = units([near_own, arrived] + sums, share, rank, size)
    unit_parts = [unit_outs[0]] + [xor_permute(unit_outs[step], "tensor", size, step) for step in range(1, size)]
    part = score(unit_parts, tests, share)
    parts = [part] + [xor_permute(part, "tensor", size, step) for step in range(1, size)]
    while len(parts) > 1:
        parts = [parts[i] + parts[i + 1] for i in range(0, len(parts), 2)]
    return parts[0]


def solution(mesh):
    placed = (
        P(("groups", "dp"), None, "tensor"),
        P(("groups", "dp"), None, "tensor"),
        P("tensor", None),
        P("tensor", None),
        P(("groups", "dp")),
        P(("groups", "dp"), None),
    )
    return jax.shard_map(
        functools.partial(shards, mesh.shape["tensor"], mesh.shape["dp"]),
        mesh=mesh,
        in_specs=placed,
        out_specs=P(("groups", "dp"), None),
        check_vma=False,
    )
```

```python
import functools

import jax
import jax.numpy as jnp
from jax import lax
from jax.experimental import pallas as pl
from jax.experimental.pallas import tpu as pltpu
from jax.sharding import PartitionSpec as P

CORES = 2
SMALL = pltpu.CompilerParams(vmem_limit_bytes=8 << 20)
NT = (((1,), (1,)), ((), ()))
HBM = pl.BlockSpec(memory_space=pltpu.HBM)
in_hbm = functools.partial(pltpu.with_memory_space_constraint, memory_space=pltpu.HBM)
VMEM = pl.BlockSpec(memory_space=pltpu.VMEM)


def xor_permute(value, axis, size, step):
    return lax.ppermute(value, axis, [(i, i ^ step) for i in range(size)])


def cut_kernel(tests, out, sem):
    width = out.shape[1]
    start = pl.multiple_of(lax.axis_index("tensor") * width, 128)
    copy = pltpu.make_async_copy(tests.at[:, pl.ds(start, width)], out, sem)
    copy.start()
    copy.wait()


def cut_tests(tests, size):
    rows, width = tests.shape
    return pl.pallas_call(
        cut_kernel,
        out_shape=jax.ShapeDtypeStruct((rows, width // size), tests.dtype),
        in_specs=[HBM],
        out_specs=VMEM,
        scratch_shapes=[pltpu.SemaphoreType.DMA],
        compiler_params=SMALL,
    )(in_hbm(tests))


COST = 1 << 32
LATER = 1<<10


def project_kernel(steps, share, ahead, piece, after, act, og, wi, wo, lens, *refs):
    refs = refs[after:]
    outs, (buf, wibuf, wobuf, lenbuf, sem, wsem) = refs[:-6], refs[-6:]
    me = lax.axis_index("tensor")
    rank = wibuf.shape[0]
    slots = buf.shape[2]
    count = len(steps) * share
    tokens = count * slots
    small = [
        pltpu.make_async_copy(wi, wibuf, wsem.at[0]),
        pltpu.make_async_copy(wo, wobuf, wsem.at[1]),
        pltpu.make_async_copy(lens, lenbuf, wsem.at[2]),
    ]
    pieces = [(side, at) for side, ref in enumerate((act, og)) for at in range(0, ref.shape[2], piece)]
    copies = []
    for slot, (side, at) in enumerate(pieces):
        width = min(piece, (act, og)[side].shape[2] - at)
        copies.append(
            [
                pltpu.make_async_copy(
                    (act, og)[side].at[pl.ds((me ^ step) * share, share), :, pl.ds(at, width)],
                    buf.at[slot, pl.ds(i * share, share), :, pl.ds(0, width)],
                    sem.at[slot, i],
                )
                for i, step in enumerate(steps)
            ]
        )
    small[0].start()
    for slot, group in enumerate(copies):
        if slot == 1:
            small[1].start()
            small[2].start()
        if slot < ahead:
            for copy in group:
                copy.start()
    sums = [None, None]
    for slot, (side, at) in enumerate(pieces):
        if at == 0:
            small[side].wait()
        for copy in copies[slot]:
            copy.wait()
        if slot + ahead < len(pieces):
            for copy in copies[slot + ahead]:
                copy.start()
        weight = (wibuf, wobuf)[side][:, at : at + piece]
        token = buf[slot].reshape(tokens, piece)[:, : weight.shape[1]]
        part = lax.dot_general(weight, token, NT, preferred_element_type=jnp.float32)
        sums[side] = part if sums[side] is None else sums[side] + part
    small[2].wait()
    col = lax.broadcasted_iota(jnp.int32, (rank, slots), 1)
    places = [out.at[i] for out in outs for i in range(out.shape[0])]
    for slot, out in enumerate(places):
        length = lenbuf[(me ^ steps[slot // share]) * share + slot % share]
        one = sums[0][:, slot * slots : (slot + 1) * slots] * (1.0 / length.astype(jnp.float32))
        out[:rank] = jnp.where(col < length, one, 0.0)
        out[rank:] = sums[1][:, slot * slots : (slot + 1) * slots]


def project(act, og, wi, wo, lens, groups, share, ahead, piece, cost, after=()):
    steps = [step for group in groups for step in group]
    count = len(steps) * share
    slots, feat, hidden = act.shape[1], act.shape[2], og.shape[2]
    rank = wi.shape[0]
    pieces = -(-feat // piece) - (-hidden // piece)
    return pl.pallas_call(
        functools.partial(project_kernel, steps, share, ahead, piece, len(after)),
        out_shape=[jax.ShapeDtypeStruct((len(group) * share, 2 * rank, slots), jnp.float32) for group in groups],
        in_specs=[HBM] * 5 + [VMEM] * len(after),
        out_specs=[VMEM] * len(groups),
        scratch_shapes=[
            pltpu.VMEM((pieces, count, slots, piece), act.dtype),
            pltpu.VMEM((rank, feat), wi.dtype),
            pltpu.VMEM((rank, hidden), wo.dtype),
            pltpu.SMEM(lens.shape, lens.dtype),
            pltpu.SemaphoreType.DMA((pieces, len(steps))),
            pltpu.SemaphoreType.DMA((3,)),
        ],
        compiler_params=pltpu.CompilerParams(vmem_limit_bytes=32 << 20),
        cost_estimate=pl.CostEstimate(flops=cost, bytes_accessed=cost // 256, transcendentals=0),
    )(*map(in_hbm, (act, og, wi, wo, lens)), *after)


def unit_kernel(share, rank, size, *refs):
    parts, outs = refs[: -2 - size], refs[-2 - size : -2]
    pairs, held = refs[-2:]
    me = lax.axis_index("tensor")
    rows = rank * rank // 128
    span = rows // size
    dot = functools.partial(lax.dot_general, dimension_numbers=NT, preferred_element_type=jnp.float32)
    for k in range(share):
        full = parts[0][k]
        for part in parts[1:]:
            full = full + part[k]
        high = full.astype(jnp.bfloat16)
        low = (full - high.astype(jnp.float32)).astype(jnp.bfloat16)
        left, right = slice(None, rank), slice(rank, None)
        pairs[k] = dot(high[left], high[right]) + (dot(high[left], low[right]) + dot(low[left], high[right]))
    for k in range(share):
        even = pairs[k, pl.ds(0, rows, stride=2), :]
        odd = pairs[k, pl.ds(1, rows, stride=2), :]
        flat = jnp.concatenate([even, odd], axis=1)
        scale = jnp.sqrt(jnp.sum(flat * flat) / (rank * rank) + 1e-06)
        unit = flat / scale
        for to in range(size):
            held[to] = unit[to * span : (to + 1) * span]
        for step in range(size):
            outs[step][k] = held[me ^ step]


def units(parts, share, rank, size):
    span = rank * rank // 128 // size
    return pl.pallas_call(
        functools.partial(unit_kernel, share, rank, size),
        out_shape=[jax.ShapeDtypeStruct((share, span, 128), jnp.float32)] * size,
        in_specs=[VMEM] * len(parts),
        out_specs=[VMEM] * size,
        scratch_shapes=[pltpu.VMEM((share, rank, rank), jnp.float32), pltpu.VMEM((size, span, 128), jnp.float32)],
        compiler_params=SMALL,
    )(*parts)


def score_kernel(share, size, origins, *refs):
    unit_refs, test_refs, out, held = refs[:size], refs[size:-2], refs[-2], refs[-1]
    me, dp = lax.axis_index("tensor"), lax.axis_index("dp")
    for step in range(size):
        for k in range(share):
            held[(me ^ step) * share + k] = unit_refs[step][k]
    unit = jnp.concatenate([held[:, c, :] for c in range(held.shape[1])], axis=1).astype(jnp.bfloat16)
    tests = test_refs[0].shape[0]
    for (factor, offset, modulus), test_ref in zip(origins, test_refs):
        part = lax.dot_general(unit, test_ref[...], NT, preferred_element_type=jnp.float32)
        at = lax.rem(factor * dp + offset, modulus) * tests
        out[:, pl.ds(pl.multiple_of(at, 128), tests)] = part


def score(unit_parts, test_parts, share):
    size, groups = len(unit_parts), len(test_parts)
    tests, width = test_parts[0][0].shape
    origins = [origin for _, *origin in test_parts]
    return pl.pallas_call(
        functools.partial(score_kernel, share, size, origins),
        out_shape=jax.ShapeDtypeStruct((share * size, tests * groups), jnp.float32),
        in_specs=[VMEM] * (size + groups),
        out_specs=VMEM,
        scratch_shapes=[pltpu.VMEM((share * size, width // 128, 128), jnp.float32)],
        compiler_params=SMALL,
    )(*unit_parts, *(shard for shard, *_ in test_parts))


def gather_tests(own, groups):
    def shift(value, step):
        return lax.ppermute(value, "dp", [(i, (i + step) % groups) for i in range(groups)])

    if groups == 4:
        first = shift(own, 1)
        return [(own, 1, 0, 4), (first, 1, 3, 4), (shift(own, -1), 1, 1, 4), (shift(first, 1), 1, 2, 4)]
    return [(own, 1, 0, groups)] + [(shift(own, step), 1, groups - step, groups) for step in range(1, groups)]


def shards(size, groups, activations, out_grads, proj_in, proj_out, lengths, test_grads):
    rank = proj_in.shape[1]
    share = activations.shape[0] // size
    own_tests = cut_tests(test_grads, size)
    tests = gather_tests(own_tests, groups)

    far = [CORES * x for x in range(1, size // CORES)]
    arrays = (activations, out_grads, proj_in.T, proj_out.T, lengths)
    far_other, far_own = project(*arrays, [[step ^ 1 for step in far], far], share, 4, 512, COST, [own_tests])
    far_sum = far_own + xor_permute(far_other, "tensor", size, 1)
    sums = [xor_permute(far_sum[i * share : (i + 1) * share], "tensor", size, step) for i, step in enumerate(far)]
    here = xor_permute(tests[1][0][:16, :128], "tensor", size, 1)
    near_other, near_own = project(*arrays, [[1], [0]], share, 4, 512, LATER, [far_sum, here])
    late = tests[2][0][: near_other.shape[1], : near_other.shape[2]].astype(jnp.float32)
    pieces = [near_other[k : k + 1] for k in range(share)]
    pieces[0] = pieces[0] + 0.0 * late[None]
    arrived = jnp.concatenate([xor_permute(one, "tensor", size, 1) for one in pieces])

    unit_outs = units([near_own, arrived] + sums, share, rank, size)
    unit_parts = [unit_outs[0]] + [xor_permute(unit_outs[step], "tensor", size, step) for step in range(1, size)]
    part = score(unit_parts, tests, share)
    parts = [part] + [xor_permute(part, "tensor", size, step) for step in range(1, size)]
    while len(parts) > 1:
        parts = [parts[i] + parts[i + 1] for i in range(0, len(parts), 2)]
    return parts[0]


def solution(mesh):
    placed = (
        P(("groups", "dp"), None, "tensor"),
        P(("groups", "dp"), None, "tensor"),
        P("tensor", None),
        P("tensor", None),
        P(("groups", "dp")),
        P(("groups", "dp"), None),
    )
    return jax.shard_map(
        functools.partial(shards, mesh.shape["tensor"], mesh.shape["dp"]),
        mesh=mesh,
        in_specs=placed,
        out_specs=P(("groups", "dp"), None),
        check_vma=False,
    )
```

```python
import functools

import jax
import jax.numpy as jnp
from jax import lax
from jax.experimental import pallas as pl
from jax.experimental.pallas import tpu as pltpu
from jax.sharding import PartitionSpec as P

CORES = 2
SMALL = pltpu.CompilerParams(vmem_limit_bytes=8 << 20)
NT = (((1,), (1,)), ((), ()))
HBM = pl.BlockSpec(memory_space=pltpu.HBM)
in_hbm = functools.partial(pltpu.with_memory_space_constraint, memory_space=pltpu.HBM)
VMEM = pl.BlockSpec(memory_space=pltpu.VMEM)


def xor_permute(value, axis, size, step):
    return lax.ppermute(value, axis, [(i, i ^ step) for i in range(size)])


def cut_kernel(tests, out, sem):
    width = out.shape[1]
    start = pl.multiple_of(lax.axis_index("tensor") * width, 128)
    copy = pltpu.make_async_copy(tests.at[:, pl.ds(start, width)], out, sem)
    copy.start()
    copy.wait()


def cut_tests(tests, size):
    rows, width = tests.shape
    return pl.pallas_call(
        cut_kernel,
        out_shape=jax.ShapeDtypeStruct((rows, width // size), tests.dtype),
        in_specs=[HBM],
        out_specs=VMEM,
        scratch_shapes=[pltpu.SemaphoreType.DMA],
        compiler_params=SMALL,
    )(in_hbm(tests))


COST = 1 << 32
LATER = 1<<10


def project_kernel(steps, share, ahead, piece, after, act, og, wi, wo, lens, *refs):
    refs = refs[after:]
    outs, (buf, wibuf, wobuf, lenbuf, sem, wsem) = refs[:-6], refs[-6:]
    me = lax.axis_index("tensor")
    rank = wibuf.shape[0]
    slots = buf.shape[2]
    count = len(steps) * share
    tokens = count * slots
    small = [
        pltpu.make_async_copy(wi, wibuf, wsem.at[0]),
        pltpu.make_async_copy(wo, wobuf, wsem.at[1]),
        pltpu.make_async_copy(lens, lenbuf, wsem.at[2]),
    ]
    pieces = [(side, at) for side, ref in enumerate((act, og)) for at in range(0, ref.shape[2], piece)]
    copies = []
    for slot, (side, at) in enumerate(pieces):
        width = min(piece, (act, og)[side].shape[2] - at)
        copies.append(
            [
                pltpu.make_async_copy(
                    (act, og)[side].at[pl.ds((me ^ step) * share, share), :, pl.ds(at, width)],
                    buf.at[slot, pl.ds(i * share, share), :, pl.ds(0, width)],
                    sem.at[slot, i],
                )
                for i, step in enumerate(steps)
            ]
        )
    small[0].start()
    for slot, group in enumerate(copies):
        if slot == 1:
            small[1].start()
            small[2].start()
        if slot < ahead:
            for copy in group:
                copy.start()
    sums = [None, None]
    for slot, (side, at) in enumerate(pieces):
        if at == 0:
            small[side].wait()
        for copy in copies[slot]:
            copy.wait()
        if slot + ahead < len(pieces):
            for copy in copies[slot + ahead]:
                copy.start()
        weight = (wibuf, wobuf)[side][:, at : at + piece]
        token = buf[slot].reshape(tokens, piece)[:, : weight.shape[1]]
        part = lax.dot_general(weight, token, NT, preferred_element_type=jnp.float32)
        sums[side] = part if sums[side] is None else sums[side] + part
    small[2].wait()
    col = lax.broadcasted_iota(jnp.int32, (rank, slots), 1)
    places = [out.at[i] for out in outs for i in range(out.shape[0])]
    for slot, out in enumerate(places):
        length = lenbuf[(me ^ steps[slot // share]) * share + slot % share]
        one = sums[0][:, slot * slots : (slot + 1) * slots] * (1.0 / length.astype(jnp.float32))
        out[:rank] = jnp.where(col < length, one, 0.0)
        out[rank:] = sums[1][:, slot * slots : (slot + 1) * slots]


def project(act, og, wi, wo, lens, groups, share, ahead, piece, cost, after=()):
    steps = [step for group in groups for step in group]
    count = len(steps) * share
    slots, feat, hidden = act.shape[1], act.shape[2], og.shape[2]
    rank = wi.shape[0]
    pieces = -(-feat // piece) - (-hidden // piece)
    return pl.pallas_call(
        functools.partial(project_kernel, steps, share, ahead, piece, len(after)),
        out_shape=[jax.ShapeDtypeStruct((len(group) * share, 2 * rank, slots), jnp.float32) for group in groups],
        in_specs=[HBM] * 5 + [VMEM] * len(after),
        out_specs=[VMEM] * len(groups),
        scratch_shapes=[
            pltpu.VMEM((pieces, count, slots, piece), act.dtype),
            pltpu.VMEM((rank, feat), wi.dtype),
            pltpu.VMEM((rank, hidden), wo.dtype),
            pltpu.SMEM(lens.shape, lens.dtype),
            pltpu.SemaphoreType.DMA((pieces, len(steps))),
            pltpu.SemaphoreType.DMA((3,)),
        ],
        compiler_params=pltpu.CompilerParams(vmem_limit_bytes=32 << 20),
        cost_estimate=pl.CostEstimate(flops=cost, bytes_accessed=cost // 256, transcendentals=0),
    )(*map(in_hbm, (act, og, wi, wo, lens)), *after)


def unit_kernel(share, rank, size, *refs):
    parts, outs = refs[: -2 - size], refs[-2 - size : -2]
    pairs, held = refs[-2:]
    me = lax.axis_index("tensor")
    rows = rank * rank // 128
    span = rows // size
    dot = functools.partial(lax.dot_general, dimension_numbers=NT, preferred_element_type=jnp.float32)
    for k in range(share):
        full = parts[0][k]
        for part in parts[1:]:
            full = full + part[k]
        high = full.astype(jnp.bfloat16)
        low = (full - high.astype(jnp.float32)).astype(jnp.bfloat16)
        left, right = slice(None, rank), slice(rank, None)
        pairs[k] = dot(high[left], high[right]) + (dot(high[left], low[right]) + dot(low[left], high[right]))
    for k in range(share):
        even = pairs[k, pl.ds(0, rows, stride=2), :]
        odd = pairs[k, pl.ds(1, rows, stride=2), :]
        flat = jnp.concatenate([even, odd], axis=1)
        scale = jnp.sqrt(jnp.sum(flat * flat) / (rank * rank) + 1e-06)
        unit = flat / scale
        for to in range(size):
            held[to] = unit[to * span : (to + 1) * span]
        for step in range(size):
            outs[step][k] = held[me ^ step]


def units(parts, share, rank, size):
    span = rank * rank // 128 // size
    return pl.pallas_call(
        functools.partial(unit_kernel, share, rank, size),
        out_shape=[jax.ShapeDtypeStruct((share, span, 128), jnp.float32)] * size,
        in_specs=[VMEM] * len(parts),
        out_specs=[VMEM] * size,
        scratch_shapes=[pltpu.VMEM((share, rank, rank), jnp.float32), pltpu.VMEM((size, span, 128), jnp.float32)],
        compiler_params=SMALL,
    )(*parts)


def score_kernel(share, size, origins, *refs):
    unit_refs, test_refs, out, held = refs[:size], refs[size:-2], refs[-2], refs[-1]
    me, dp = lax.axis_index("tensor"), lax.axis_index("dp")
    for step in range(size):
        for k in range(share):
            held[(me ^ step) * share + k] = unit_refs[step][k]
    unit = jnp.concatenate([held[:, c, :] for c in range(held.shape[1])], axis=1).astype(jnp.bfloat16)
    tests = test_refs[0].shape[0]
    for (factor, offset, modulus), test_ref in zip(origins, test_refs):
        part = lax.dot_general(unit, test_ref[...], NT, preferred_element_type=jnp.float32)
        at = lax.rem(factor * dp + offset, modulus) * tests
        out[:, pl.ds(pl.multiple_of(at, 128), tests)] = part


def score(unit_parts, test_parts, share):
    size, groups = len(unit_parts), len(test_parts)
    tests, width = test_parts[0][0].shape
    origins = [origin for _, *origin in test_parts]
    return pl.pallas_call(
        functools.partial(score_kernel, share, size, origins),
        out_shape=jax.ShapeDtypeStruct((share * size, tests * groups), jnp.float32),
        in_specs=[VMEM] * (size + groups),
        out_specs=VMEM,
        scratch_shapes=[pltpu.VMEM((share * size, width // 128, 128), jnp.float32)],
        compiler_params=SMALL,
    )(*unit_parts, *(shard for shard, *_ in test_parts))


def gather_tests(own, groups):
    def shift(value, step):
        return lax.ppermute(value, "dp", [(i, (i + step) % groups) for i in range(groups)])

    if groups == 4:
        first = shift(own, -1)
        return [(own, 1, 0, 4), (first, 1, 1, 4), (shift(own, 1), 1, 3, 4), (shift(first, -1), 1, 2, 4)]
    return [(own, 1, 0, groups)] + [(shift(own, step), 1, groups - step, groups) for step in range(1, groups)]


def shards(size, groups, activations, out_grads, proj_in, proj_out, lengths, test_grads):
    rank = proj_in.shape[1]
    share = activations.shape[0] // size
    own_tests = cut_tests(test_grads, size)
    tests = gather_tests(own_tests, groups)

    far = [CORES * x for x in range(1, size // CORES)]
    arrays = (activations, out_grads, proj_in.T, proj_out.T, lengths)
    far_other, far_own = project(*arrays, [[step ^ 1 for step in far], far], share, 4, 512, COST, [own_tests])
    far_sum = far_own + xor_permute(far_other, "tensor", size, 1)
    sums = [xor_permute(far_sum[i * share : (i + 1) * share], "tensor", size, step) for i, step in enumerate(far)]
    here = xor_permute(tests[1][0][:16, :128], "tensor", size, 1)
    near_other, near_own = project(*arrays, [[1], [0]], share, 4, 512, LATER, [far_sum, here])
    late = tests[2][0][: near_other.shape[1], : near_other.shape[2]].astype(jnp.float32)
    pieces = [near_other[k : k + 1] for k in range(share)]
    pieces[0] = pieces[0] + 0.0 * late[None]
    arrived = jnp.concatenate([xor_permute(one, "tensor", size, 1) for one in pieces])

    unit_outs = units([near_own, arrived] + sums, share, rank, size)
    unit_parts = [unit_outs[0]] + [xor_permute(unit_outs[step], "tensor", size, step) for step in range(1, size)]
    part = score(unit_parts, tests, share)
    parts = [part] + [xor_permute(part, "tensor", size, step) for step in range(1, size)]
    while len(parts) > 1:
        parts = [parts[i] + parts[i + 1] for i in range(0, len(parts), 2)]
    return parts[0]


def solution(mesh):
    placed = (
        P(("groups", "dp"), None, "tensor"),
        P(("groups", "dp"), None, "tensor"),
        P("tensor", None),
        P("tensor", None),
        P(("groups", "dp")),
        P(("groups", "dp"), None),
    )
    return jax.shard_map(
        functools.partial(shards, mesh.shape["tensor"], mesh.shape["dp"]),
        mesh=mesh,
        in_specs=placed,
        out_specs=P(("groups", "dp"), None),
        check_vma=False,
    )
```

```python
import functools

import jax
import jax.numpy as jnp
from jax import lax
from jax.experimental import pallas as pl
from jax.experimental.pallas import tpu as pltpu
from jax.sharding import PartitionSpec as P

CORES = 2
SMALL = pltpu.CompilerParams(vmem_limit_bytes=8 << 20)
NT = (((1,), (1,)), ((), ()))
HBM = pl.BlockSpec(memory_space=pltpu.HBM)
in_hbm = functools.partial(pltpu.with_memory_space_constraint, memory_space=pltpu.HBM)
VMEM = pl.BlockSpec(memory_space=pltpu.VMEM)


def xor_permute(value, axis, size, step):
    return lax.ppermute(value, axis, [(i, i ^ step) for i in range(size)])


def first_kernel(tests, wi, wo, own, wide, wibuf, wobuf, sem):
    width = own.shape[1]
    start = pl.multiple_of(lax.axis_index("tensor") * width, 128)
    copies = [
        pltpu.make_async_copy(wi, wibuf, sem.at[0]),
        pltpu.make_async_copy(wo, wobuf, sem.at[1]),
        pltpu.make_async_copy(tests.at[:, pl.ds(start, width)], own, sem.at[2]),
    ]
    for copy in copies:
        copy.start()
    feat = wibuf.shape[1]
    for side, buf in enumerate((wibuf, wobuf)):
        copies[side].wait()
        for at in range(0, buf.shape[1], 256):
            weight = buf[:, at : at + 256]
            none = jnp.zeros_like(weight)
            both = jnp.concatenate([none, weight] if side else [weight, none], axis=0)
            wide[side * feat + at : side * feat + at + weight.shape[1]] = both.T
    copies[2].wait()


def first(tests, wi, wo, size):
    rows, width = tests.shape
    rank, feat = wi.shape
    return pl.pallas_call(
        first_kernel,
        out_shape=[
            jax.ShapeDtypeStruct((rows, width // size), tests.dtype),
            jax.ShapeDtypeStruct((feat + wo.shape[1], 2 * rank), wi.dtype),
        ],
        in_specs=[HBM] * 3,
        out_specs=[VMEM] * 2,
        scratch_shapes=[pltpu.VMEM(wi.shape, wi.dtype), pltpu.VMEM(wo.shape, wo.dtype), pltpu.SemaphoreType.DMA((3,))],
        compiler_params=SMALL,
    )(in_hbm(tests), in_hbm(wi), in_hbm(wo))


COST = 1 << 32
LATER = 1<<10


def project_kernel(steps, share, ahead, piece, height, after, act, og, lens, wide, *refs):
    refs = refs[after:]
    outs, (buf, lenbuf, sem, lensem) = refs[:-4], refs[-4:]
    me = lax.axis_index("tensor")
    rank = wide.shape[1] // 2
    slots, feat = act.shape[1:]
    lencopy = pltpu.make_async_copy(lens, lenbuf, lensem)
    pieces = [
        (side, at, min(piece, ref.shape[2] - at)) for side, ref in enumerate((act, og)) for at in range(0, ref.shape[2], piece)
    ]
    copies = [
        [
            pltpu.make_async_copy(
                (act, og)[side].at[pl.ds((me ^ step) * share, share), :, pl.ds(at, width)],
                buf.at[slot, pl.ds(i * share, share), :, pl.ds(0, width)],
                sem.at[slot, i],
            )
            for i, step in enumerate(steps)
        ]
        for slot, (side, at, width) in enumerate(pieces)
    ]
    for group in copies[:ahead]:
        for copy in group:
            copy.start()
    lencopy.start()
    count = len(steps) * share
    sums = [None] * (count // height)
    for slot, (side, at, width) in enumerate(pieces):
        for copy in copies[slot]:
            copy.wait()
        for copy in copies[slot + ahead] if slot + ahead < len(copies) else ():
            copy.start()
        weight = wide[side * feat + at : side * feat + at + width]
        for i in range(len(sums)):
            token = buf[slot, i * height : (i + 1) * height].reshape(height * slots, piece)[:, :width]
            part = jnp.dot(token, weight, preferred_element_type=jnp.float32)
            sums[i] = part if sums[i] is None else sums[i] + part
    lencopy.wait()
    col = lax.broadcasted_iota(jnp.int32, (rank, slots), 1)
    places = [out.at[i] for out in outs for i in range(out.shape[0])]
    for slot, out in enumerate(places):
        length = lenbuf[(me ^ steps[slot // share]) * share + slot % share]
        i, k = divmod(slot, height)
        both = sums[i][k * slots : (k + 1) * slots].T
        out[:rank] = jnp.where(col < length, both[:rank] * (1.0 / length.astype(jnp.float32)), 0.0)
        out[rank:] = both[rank:]


def project(act, og, lens, wide, groups, share, ahead, piece, height, cost, after=()):
    steps = [step for group in groups for step in group]
    count = len(steps) * share
    slots, feat, hidden = act.shape[1], act.shape[2], og.shape[2]
    pieces = -(-feat // piece) - (-hidden // piece)
    return pl.pallas_call(
        functools.partial(project_kernel, steps, share, ahead, piece, height, len(after)),
        out_shape=[jax.ShapeDtypeStruct((len(group) * share, wide.shape[1], slots), jnp.float32) for group in groups],
        in_specs=[HBM] * 3 + [VMEM] * (1 + len(after)),
        out_specs=[VMEM] * len(groups),
        scratch_shapes=[
            pltpu.VMEM((pieces, count, slots, piece), act.dtype),
            pltpu.SMEM(lens.shape, lens.dtype),
            pltpu.SemaphoreType.DMA((pieces, len(steps))),
            pltpu.SemaphoreType.DMA,
        ],
        compiler_params=pltpu.CompilerParams(vmem_limit_bytes=32 << 20),
        cost_estimate=pl.CostEstimate(flops=cost, bytes_accessed=cost // 256, transcendentals=0),
    )(*map(in_hbm, (act, og, lens)), wide, *after)


def unit_kernel(share, rank, size, *refs):
    parts, outs = refs[: -2 - size], refs[-2 - size : -2]
    pairs, held = refs[-2:]
    me = lax.axis_index("tensor")
    rows = rank * rank // 128
    span = rows // size
    dot = functools.partial(lax.dot_general, dimension_numbers=NT, preferred_element_type=jnp.float32)
    for k in range(share):
        full = parts[0][k]
        for part in parts[1:]:
            full = full + part[k]
        high = full.astype(jnp.bfloat16)
        low = (full - high.astype(jnp.float32)).astype(jnp.bfloat16)
        left, right = slice(None, rank), slice(rank, None)
        pairs[k] = dot(high[left], high[right]) + (dot(high[left], low[right]) + dot(low[left], high[right]))
    for k in range(share):
        even = pairs[k, pl.ds(0, rows, stride=2), :]
        odd = pairs[k, pl.ds(1, rows, stride=2), :]
        flat = jnp.concatenate([even, odd], axis=1)
        scale = jnp.sqrt(jnp.sum(flat * flat) / (rank * rank) + 1e-06)
        unit = flat / scale
        for to in range(size):
            held[to] = unit[to * span : (to + 1) * span]
        for step in range(size):
            outs[step][k] = held[me ^ step]


def units(parts, share, rank, size):
    span = rank * rank // 128 // size
    return pl.pallas_call(
        functools.partial(unit_kernel, share, rank, size),
        out_shape=[jax.ShapeDtypeStruct((share, span, 128), jnp.float32)] * size,
        in_specs=[VMEM] * len(parts),
        out_specs=[VMEM] * size,
        scratch_shapes=[pltpu.VMEM((share, rank, rank), jnp.float32), pltpu.VMEM((size, span, 128), jnp.float32)],
        compiler_params=SMALL,
    )(*parts)


def score_kernel(share, size, origins, *refs):
    unit_refs, test_refs, out, held = refs[:size], refs[size:-2], refs[-2], refs[-1]
    me, dp = lax.axis_index("tensor"), lax.axis_index("dp")
    for step in range(size):
        for k in range(share):
            held[(me ^ step) * share + k] = unit_refs[step][k]
    unit = jnp.concatenate([held[:, c, :] for c in range(held.shape[1])], axis=1).astype(jnp.bfloat16)
    tests = test_refs[0].shape[0]
    for (factor, offset, modulus), test_ref in zip(origins, test_refs):
        part = lax.dot_general(unit, test_ref[...], NT, preferred_element_type=jnp.float32)
        at = lax.rem(factor * dp + offset, modulus) * tests
        out[:, pl.ds(pl.multiple_of(at, 128), tests)] = part


def score(unit_parts, test_parts, share):
    size, groups = len(unit_parts), len(test_parts)
    tests, width = test_parts[0][0].shape
    origins = [origin for _, *origin in test_parts]
    return pl.pallas_call(
        functools.partial(score_kernel, share, size, origins),
        out_shape=jax.ShapeDtypeStruct((share * size, tests * groups), jnp.float32),
        in_specs=[VMEM] * (size + groups),
        out_specs=VMEM,
        scratch_shapes=[pltpu.VMEM((share * size, width // 128, 128), jnp.float32)],
        compiler_params=SMALL,
    )(*unit_parts, *(shard for shard, *_ in test_parts))


def gather_tests(own, groups):
    def shift(value, step):
        return lax.ppermute(value, "dp", [(i, (i + step) % groups) for i in range(groups)])

    if groups == 4:
        first = shift(own, 1)
        return [(own, 1, 0, 4), (first, 1, 3, 4), (shift(own, -1), 1, 1, 4), (shift(first, 1), 1, 2, 4)]
    return [(own, 1, 0, groups)] + [(shift(own, step), 1, groups - step, groups) for step in range(1, groups)]


def shards(size, groups, activations, out_grads, proj_in, proj_out, lengths, test_grads):
    rank = proj_in.shape[1]
    share = activations.shape[0] // size
    own_tests, wide = first(test_grads, proj_in.T, proj_out.T, size)
    tests = gather_tests(own_tests, groups)

    far = [CORES * x for x in range(1, size // CORES)]
    arrays = (activations, out_grads, lengths, wide)
    far_other, far_own = project(*arrays, [[step ^ 1 for step in far], far], share, 4, 512, 1, COST, [own_tests])
    far_sum = far_own + xor_permute(far_other, "tensor", size, 1)
    sums = [xor_permute(far_sum[i * share : (i + 1) * share], "tensor", size, step) for i, step in enumerate(far)]
    here = xor_permute(tests[1][0][:16, :128], "tensor", size, 1)
    near_other, near_own = project(*arrays, [[1], [0]], share, 4, 512, 2 * share, LATER, [far_sum, here])
    late = tests[2][0][: near_other.shape[1], : near_other.shape[2]].astype(jnp.float32)
    pieces = [near_other[k : k + 1] for k in range(share)]
    pieces[0] = pieces[0] + 0.0 * late[None]
    arrived = jnp.concatenate([xor_permute(one, "tensor", size, 1) for one in pieces])

    unit_outs = units([near_own, arrived] + sums, share, rank, size)
    unit_parts = [unit_outs[0]] + [xor_permute(unit_outs[step], "tensor", size, step) for step in range(1, size)]
    part = score(unit_parts, tests, share)
    parts = [part] + [xor_permute(part, "tensor", size, step) for step in range(1, size)]
    while len(parts) > 1:
        parts = [parts[i] + parts[i + 1] for i in range(0, len(parts), 2)]
    return parts[0]


def solution(mesh):
    placed = (
        P(("groups", "dp"), None, "tensor"),
        P(("groups", "dp"), None, "tensor"),
        P("tensor", None),
        P("tensor", None),
        P(("groups", "dp")),
        P(("groups", "dp"), None),
    )
    return jax.shard_map(
        functools.partial(shards, mesh.shape["tensor"], mesh.shape["dp"]),
        mesh=mesh,
        in_specs=placed,
        out_specs=P(("groups", "dp"), None),
        check_vma=False,
    )
```

```python
import functools

import jax
import jax.numpy as jnp
from jax import lax
from jax.experimental import pallas as pl
from jax.experimental.pallas import tpu as pltpu
from jax.sharding import PartitionSpec as P

CORES = 2
SMALL = pltpu.CompilerParams(vmem_limit_bytes=8 << 20)
NT = (((1,), (1,)), ((), ()))
HBM = pl.BlockSpec(memory_space=pltpu.HBM)
in_hbm = functools.partial(pltpu.with_memory_space_constraint, memory_space=pltpu.HBM)
VMEM = pl.BlockSpec(memory_space=pltpu.VMEM)


def xor_permute(value, axis, size, step):
    return lax.ppermute(value, axis, [(i, i ^ step) for i in range(size)])


def cut_kernel(tests, out, sem):
    width = out.shape[1]
    start = pl.multiple_of(lax.axis_index("tensor") * width, 128)
    copy = pltpu.make_async_copy(tests.at[:, pl.ds(start, width)], out, sem)
    copy.start()
    copy.wait()


def cut_tests(tests, size):
    rows, width = tests.shape
    return pl.pallas_call(
        cut_kernel,
        out_shape=jax.ShapeDtypeStruct((rows, width // size), tests.dtype),
        in_specs=[HBM],
        out_specs=VMEM,
        scratch_shapes=[pltpu.SemaphoreType.DMA],
        compiler_params=SMALL,
    )(in_hbm(tests))


AHEAD = 4
COST = 1 << 32
LATER = 1<<10


def project_kernel(steps, share, piece, fresh, after, act, og, lens, *refs):
    if fresh:
        (wi, wo), refs = refs[:2], refs[2 + after :]
        outs, (wide, buf, lenbuf, sem, lensem, wibuf, wobuf, wsem) = refs[:-8], refs[-8:]
    else:
        wide, refs = refs[0], refs[1 + after :]
        outs, (buf, lenbuf, sem, lensem) = refs[:-4], refs[-4:]
    me = lax.axis_index("tensor")
    rank = wide.shape[1] // 2
    slots, feat = act.shape[1:]
    count = len(steps) * share
    pieces = [
        (side, at, min(piece, ref.shape[2] - at)) for side, ref in enumerate((act, og)) for at in range(0, ref.shape[2], piece)
    ]
    copies = [
        [
            pltpu.make_async_copy(
                (act, og)[side].at[pl.ds((me ^ step) * share, share), :, pl.ds(at, width)],
                buf.at[slot, pl.ds(i * share, share), :, pl.ds(0, width)],
                sem.at[slot, i],
            )
            for i, step in enumerate(steps)
        ]
        for slot, (side, at, width) in enumerate(pieces)
    ]
    lencopy = pltpu.make_async_copy(lens, lenbuf, lensem)
    if fresh:
        weights = [pltpu.make_async_copy(wi, wibuf, wsem.at[0]), pltpu.make_async_copy(wo, wobuf, wsem.at[1])]
        weights[0].start()
        weights[1].start()
    for group in copies[:AHEAD]:
        for copy in group:
            copy.start()
    lencopy.start()
    sums = [None, None]
    for slot, (side, at, width) in enumerate(pieces):
        rows = slice(side * feat + at, side * feat + at + width)
        if fresh:
            if at == 0:
                weights[side].wait()
            weight = (wibuf, wobuf)[side][:, at : at + width]
            none = jnp.zeros_like(weight)
            wide[rows] = jnp.concatenate([none, weight] if side else [weight, none], axis=0).T
        for copy in copies[slot]:
            copy.wait()
        for copy in copies[slot + AHEAD] if slot + AHEAD < len(copies) else ():
            copy.start()
        weight = wide[rows]
        token = buf[slot].reshape(count * slots, piece)
        for half, start in enumerate(range(0, width, piece // 2)):
            stop = min(start + piece // 2, width)
            part = jnp.dot(token[:, start:stop], weight[start:stop], preferred_element_type=jnp.float32)
            sums[half] = part if sums[half] is None else sums[half] + part
    total = sums[0] + sums[1]
    lencopy.wait()
    col = lax.broadcasted_iota(jnp.int32, (rank, slots), 1)
    places = [out.at[i] for out in outs for i in range(out.shape[0])]
    for slot, out in enumerate(places):
        length = lenbuf[(me ^ steps[slot // share]) * share + slot % share]
        both = total[slot * slots : (slot + 1) * slots].T
        out[:rank] = jnp.where(col < length, both[:rank] * (1.0 / length.astype(jnp.float32)), 0.0)
        out[rank:] = both[rank:]


def project(act, og, lens, weights, groups, share, piece, cost, after=()):
    steps = [step for group in groups for step in group]
    count = len(steps) * share
    slots, feat, hidden = act.shape[1], act.shape[2], og.shape[2]
    pieces = -(-feat // piece) - (-hidden // piece)
    fresh = len(weights) == 2
    columns = 2 * weights[0].shape[0] if fresh else weights[0].shape[1]
    shapes = [jax.ShapeDtypeStruct((len(group) * share, columns, slots), jnp.float32) for group in groups]
    scratch = [
        pltpu.VMEM((pieces, count, slots, piece), act.dtype),
        pltpu.SMEM(lens.shape, lens.dtype),
        pltpu.SemaphoreType.DMA((pieces, len(steps))),
        pltpu.SemaphoreType.DMA,
    ]
    if fresh:
        shapes += [jax.ShapeDtypeStruct((feat + hidden, columns), act.dtype)]
        scratch += [pltpu.VMEM(one.shape, one.dtype) for one in weights] + [pltpu.SemaphoreType.DMA((2,))]
    return pl.pallas_call(
        functools.partial(project_kernel, steps, share, piece, fresh, len(after)),
        out_shape=shapes,
        in_specs=[HBM] * 3 + [HBM if fresh else VMEM] * len(weights) + [VMEM] * len(after),
        out_specs=[VMEM] * len(shapes),
        scratch_shapes=scratch,
        compiler_params=pltpu.CompilerParams(vmem_limit_bytes=32 << 20),
        cost_estimate=pl.CostEstimate(flops=cost, bytes_accessed=cost // 256, transcendentals=0),
    )(*map(in_hbm, (act, og, lens)), *(map(in_hbm, weights) if fresh else weights), *after)


def unit_kernel(share, rank, size, *refs):
    parts, outs = refs[: -2 - size], refs[-2 - size : -2]
    pairs, held = refs[-2:]
    me = lax.axis_index("tensor")
    rows = rank * rank // 128
    span = rows // size
    dot = functools.partial(lax.dot_general, dimension_numbers=NT, preferred_element_type=jnp.float32)
    for k in range(share):
        full = parts[0][k]
        for part in parts[1:]:
            full = full + part[k]
        high = full.astype(jnp.bfloat16)
        low = (full - high.astype(jnp.float32)).astype(jnp.bfloat16)
        left, right = slice(None, rank), slice(rank, None)
        pairs[k] = dot(high[left], high[right]) + (dot(high[left], low[right]) + dot(low[left], high[right]))
    for k in range(share):
        even = pairs[k, pl.ds(0, rows, stride=2), :]
        odd = pairs[k, pl.ds(1, rows, stride=2), :]
        flat = jnp.concatenate([even, odd], axis=1)
        scale = jnp.sqrt(jnp.sum(flat * flat) / (rank * rank) + 1e-06)
        unit = flat / scale
        for to in range(size):
            held[to] = unit[to * span : (to + 1) * span]
        for step in range(size):
            outs[step][k] = held[me ^ step]


def units(parts, share, rank, size):
    span = rank * rank // 128 // size
    return pl.pallas_call(
        functools.partial(unit_kernel, share, rank, size),
        out_shape=[jax.ShapeDtypeStruct((share, span, 128), jnp.float32)] * size,
        in_specs=[VMEM] * len(parts),
        out_specs=[VMEM] * size,
        scratch_shapes=[pltpu.VMEM((share, rank, rank), jnp.float32), pltpu.VMEM((size, span, 128), jnp.float32)],
        compiler_params=SMALL,
    )(*parts)


def score_kernel(share, size, origins, *refs):
    unit_refs, test_refs, out, held = refs[:size], refs[size:-2], refs[-2], refs[-1]
    me, dp = lax.axis_index("tensor"), lax.axis_index("dp")
    for step in range(size):
        for k in range(share):
            held[(me ^ step) * share + k] = unit_refs[step][k]
    unit = jnp.concatenate([held[:, c, :] for c in range(held.shape[1])], axis=1).astype(jnp.bfloat16)
    tests = test_refs[0].shape[0]
    for (factor, offset, modulus), test_ref in zip(origins, test_refs):
        part = lax.dot_general(unit, test_ref[...], NT, preferred_element_type=jnp.float32)
        at = lax.rem(factor * dp + offset, modulus) * tests
        out[:, pl.ds(pl.multiple_of(at, 128), tests)] = part


def score(unit_parts, test_parts, share):
    size, groups = len(unit_parts), len(test_parts)
    tests, width = test_parts[0][0].shape
    origins = [origin for _, *origin in test_parts]
    return pl.pallas_call(
        functools.partial(score_kernel, share, size, origins),
        out_shape=jax.ShapeDtypeStruct((share * size, tests * groups), jnp.float32),
        in_specs=[VMEM] * (size + groups),
        out_specs=VMEM,
        scratch_shapes=[pltpu.VMEM((share * size, width // 128, 128), jnp.float32)],
        compiler_params=SMALL,
    )(*unit_parts, *(shard for shard, *_ in test_parts))


def gather_tests(own, groups):
    def shift(value, step):
        return lax.ppermute(value, "dp", [(i, (i + step) % groups) for i in range(groups)])

    if groups == 4:
        first = shift(own, 1)
        return [(own, 1, 0, 4), (first, 1, 3, 4), (shift(own, -1), 1, 1, 4), (shift(first, 1), 1, 2, 4)]
    return [(own, 1, 0, groups)] + [(shift(own, step), 1, groups - step, groups) for step in range(1, groups)]


def shards(size, groups, activations, out_grads, proj_in, proj_out, lengths, test_grads):
    rank = proj_in.shape[1]
    share = activations.shape[0] // size
    own_tests = cut_tests(test_grads, size)
    tests = gather_tests(own_tests, groups)

    far = [CORES * x for x in range(1, size // CORES)]
    arrays = (activations, out_grads, lengths)
    sends = [[step ^ 1 for step in far], far]
    far_other, far_own, wide = project(*arrays, [proj_in.T, proj_out.T], sends, share, 512, COST, [own_tests])
    far_sum = far_own + xor_permute(far_other, "tensor", size, 1)
    sums = [xor_permute(far_sum[i * share : (i + 1) * share], "tensor", size, step) for i, step in enumerate(far)]
    here = xor_permute(tests[1][0][:16, :128], "tensor", size, 1)
    near_other, near_own = project(*arrays, [wide], [[1], [0]], share, 512, LATER, [far_sum, here])
    late = tests[2][0][: near_other.shape[1], : near_other.shape[2]].astype(jnp.float32)
    pieces = [near_other[k : k + 1] for k in range(share)]
    pieces[0] = pieces[0] + 0.0 * late[None]
    arrived = jnp.concatenate([xor_permute(one, "tensor", size, 1) for one in pieces])

    unit_outs = units([near_own, arrived] + sums, share, rank, size)
    unit_parts = [unit_outs[0]] + [xor_permute(unit_outs[step], "tensor", size, step) for step in range(1, size)]
    part = score(unit_parts, tests, share)
    parts = [part] + [xor_permute(part, "tensor", size, step) for step in range(1, size)]
    while len(parts) > 1:
        parts = [parts[i] + parts[i + 1] for i in range(0, len(parts), 2)]
    return parts[0]


def solution(mesh):
    placed = (
        P(("groups", "dp"), None, "tensor"),
        P(("groups", "dp"), None, "tensor"),
        P("tensor", None),
        P("tensor", None),
        P(("groups", "dp")),
        P(("groups", "dp"), None),
    )
    return jax.shard_map(
        functools.partial(shards, mesh.shape["tensor"], mesh.shape["dp"]),
        mesh=mesh,
        in_specs=placed,
        out_specs=P(("groups", "dp"), None),
        check_vma=False,
    )
```

```python
import functools

import jax
import jax.numpy as jnp
from jax import lax
from jax.experimental import pallas as pl
from jax.experimental.pallas import tpu as pltpu
from jax.sharding import PartitionSpec as P

CORES = 2
SMALL = pltpu.CompilerParams(vmem_limit_bytes=8 << 20)
NT = (((1,), (1,)), ((), ()))
HBM = pl.BlockSpec(memory_space=pltpu.HBM)
in_hbm = functools.partial(pltpu.with_memory_space_constraint, memory_space=pltpu.HBM)
VMEM = pl.BlockSpec(memory_space=pltpu.VMEM)


def xor_permute(value, axis, size, step):
    return lax.ppermute(value, axis, [(i, i ^ step) for i in range(size)])


def cut_kernel(tests, out, sem):
    width = out.shape[1]
    start = pl.multiple_of(lax.axis_index("tensor") * width, 128)
    copy = pltpu.make_async_copy(tests.at[:, pl.ds(start, width)], out, sem)
    copy.start()
    copy.wait()


def cut_tests(tests, size):
    rows, width = tests.shape
    return pl.pallas_call(
        cut_kernel,
        out_shape=jax.ShapeDtypeStruct((rows, width // size), tests.dtype),
        in_specs=[HBM],
        out_specs=VMEM,
        scratch_shapes=[pltpu.SemaphoreType.DMA],
        compiler_params=SMALL,
    )(in_hbm(tests))


COST = 1 << 32
LATER = 1<<10


def project_kernel(steps, share, ahead, pieces, after, act, og, wi, wo, lens, *refs):
    refs = refs[after:]
    outs, (buf, wibuf, wobuf, lenbuf, sem, wsem) = refs[:-6], refs[-6:]
    me = lax.axis_index("tensor")
    rank = wibuf.shape[0]
    slots = buf.shape[2]
    count = len(steps) * share
    tokens = count * slots
    small = [
        pltpu.make_async_copy(wi, wibuf, wsem.at[0]),
        pltpu.make_async_copy(wo, wobuf, wsem.at[1]),
        pltpu.make_async_copy(lens, lenbuf, wsem.at[2]),
    ]
    copies = []
    for slot, (side, at, width) in enumerate(pieces):
        copies.append(
            [
                pltpu.make_async_copy(
                    (act, og)[side].at[pl.ds((me ^ step) * share, share), :, pl.ds(at, width)],
                    buf.at[slot, pl.ds(i * share, share), :, pl.ds(0, width)],
                    sem.at[slot, i],
                )
                for i, step in enumerate(steps)
            ]
        )
    small[0].start()
    for slot, group in enumerate(copies):
        if slot == 1:
            small[1].start()
            small[2].start()
        if slot < ahead:
            for copy in group:
                copy.start()
    sums = [None, None]
    for slot, (side, at, width) in enumerate(pieces):
        if at == 0:
            small[side].wait()
        for copy in copies[slot]:
            copy.wait()
        if slot + ahead < len(pieces):
            for copy in copies[slot + ahead]:
                copy.start()
        weight = (wibuf, wobuf)[side][:, at : at + width]
        token = buf[slot].reshape(tokens, buf.shape[3])[:, :width]
        part = lax.dot_general(weight, token, NT, preferred_element_type=jnp.float32)
        sums[side] = part if sums[side] is None else sums[side] + part
    small[2].wait()
    col = lax.broadcasted_iota(jnp.int32, (rank, slots), 1)
    places = [out.at[i] for out in outs for i in range(out.shape[0])]
    for slot, out in enumerate(places):
        length = lenbuf[(me ^ steps[slot // share]) * share + slot % share]
        one = sums[0][:, slot * slots : (slot + 1) * slots] * (1.0 / length.astype(jnp.float32))
        out[:rank] = jnp.where(col < length, one, 0.0)
        out[rank:] = sums[1][:, slot * slots : (slot + 1) * slots]


def project(act, og, wi, wo, lens, groups, share, ahead, piece, cost, after=()):
    steps = [step for group in groups for step in group]
    count = len(steps) * share
    slots, feat, hidden = act.shape[1], act.shape[2], og.shape[2]
    rank = wi.shape[0]
    pieces = [(0, at, 256) for at in range(0, min(512, feat), 256)]
    pieces += [(0, at, min(piece, feat - at)) for at in range(512, feat, piece)]
    pieces += [(1, at, min(piece, hidden - at)) for at in range(0, hidden, piece)]
    return pl.pallas_call(
        functools.partial(project_kernel, steps, share, ahead, pieces, len(after)),
        out_shape=[jax.ShapeDtypeStruct((len(group) * share, 2 * rank, slots), jnp.float32) for group in groups],
        in_specs=[HBM] * 5 + [VMEM] * len(after),
        out_specs=[VMEM] * len(groups),
        scratch_shapes=[
            pltpu.VMEM((len(pieces), count, slots, piece), act.dtype),
            pltpu.VMEM((rank, feat), wi.dtype),
            pltpu.VMEM((rank, hidden), wo.dtype),
            pltpu.SMEM(lens.shape, lens.dtype),
            pltpu.SemaphoreType.DMA((len(pieces), len(steps))),
            pltpu.SemaphoreType.DMA((3,)),
        ],
        compiler_params=pltpu.CompilerParams(vmem_limit_bytes=32 << 20),
        cost_estimate=pl.CostEstimate(flops=cost, bytes_accessed=cost // 256, transcendentals=0),
    )(*map(in_hbm, (act, og, wi, wo, lens)), *after)


def unit_kernel(share, rank, size, *refs):
    parts, outs = refs[: -2 - size], refs[-2 - size : -2]
    pairs, held = refs[-2:]
    me = lax.axis_index("tensor")
    rows = rank * rank // 128
    span = rows // size
    dot = functools.partial(lax.dot_general, dimension_numbers=NT, preferred_element_type=jnp.float32)
    for k in range(share):
        full = parts[0][k]
        for part in parts[1:]:
            full = full + part[k]
        high = full.astype(jnp.bfloat16)
        low = (full - high.astype(jnp.float32)).astype(jnp.bfloat16)
        left, right = slice(None, rank), slice(rank, None)
        pairs[k] = dot(high[left], high[right]) + (dot(high[left], low[right]) + dot(low[left], high[right]))
    for k in range(share):
        even = pairs[k, pl.ds(0, rows, stride=2), :]
        odd = pairs[k, pl.ds(1, rows, stride=2), :]
        flat = jnp.concatenate([even, odd], axis=1)
        scale = jnp.sqrt(jnp.sum(flat * flat) / (rank * rank) + 1e-06)
        unit = flat / scale
        for to in range(size):
            held[to] = unit[to * span : (to + 1) * span]
        for step in range(size):
            outs[step][k] = held[me ^ step]


def units(parts, share, rank, size):
    span = rank * rank // 128 // size
    return pl.pallas_call(
        functools.partial(unit_kernel, share, rank, size),
        out_shape=[jax.ShapeDtypeStruct((share, span, 128), jnp.float32)] * size,
        in_specs=[VMEM] * len(parts),
        out_specs=[VMEM] * size,
        scratch_shapes=[pltpu.VMEM((share, rank, rank), jnp.float32), pltpu.VMEM((size, span, 128), jnp.float32)],
        compiler_params=SMALL,
    )(*parts)


def score_kernel(share, size, origins, *refs):
    unit_refs, test_refs, out, held = refs[:size], refs[size:-2], refs[-2], refs[-1]
    me, dp = lax.axis_index("tensor"), lax.axis_index("dp")
    for step in range(size):
        for k in range(share):
            held[(me ^ step) * share + k] = unit_refs[step][k]
    unit = jnp.concatenate([held[:, c, :] for c in range(held.shape[1])], axis=1).astype(jnp.bfloat16)
    tests = test_refs[0].shape[0]
    for (factor, offset, modulus), test_ref in zip(origins, test_refs):
        part = lax.dot_general(unit, test_ref[...], NT, preferred_element_type=jnp.float32)
        at = lax.rem(factor * dp + offset, modulus) * tests
        out[:, pl.ds(pl.multiple_of(at, 128), tests)] = part


def score(unit_parts, test_parts, share):
    size, groups = len(unit_parts), len(test_parts)
    tests, width = test_parts[0][0].shape
    origins = [origin for _, *origin in test_parts]
    return pl.pallas_call(
        functools.partial(score_kernel, share, size, origins),
        out_shape=jax.ShapeDtypeStruct((share * size, tests * groups), jnp.float32),
        in_specs=[VMEM] * (size + groups),
        out_specs=VMEM,
        scratch_shapes=[pltpu.VMEM((share * size, width // 128, 128), jnp.float32)],
        compiler_params=SMALL,
    )(*unit_parts, *(shard for shard, *_ in test_parts))


def gather_tests(own, groups):
    def shift(value, step):
        return lax.ppermute(value, "dp", [(i, (i + step) % groups) for i in range(groups)])

    if groups == 4:
        first = shift(own, 1)
        return [(own, 1, 0, 4), (first, 1, 3, 4), (shift(own, -1), 1, 1, 4), (shift(first, 1), 1, 2, 4)]
    return [(own, 1, 0, groups)] + [(shift(own, step), 1, groups - step, groups) for step in range(1, groups)]


def shards(size, groups, activations, out_grads, proj_in, proj_out, lengths, test_grads):
    rank = proj_in.shape[1]
    share = activations.shape[0] // size
    own_tests = cut_tests(test_grads, size)
    tests = gather_tests(own_tests, groups)

    far = [CORES * x for x in range(1, size // CORES)]
    arrays = (activations, out_grads, proj_in.T, proj_out.T, lengths)
    far_other, far_own = project(*arrays, [[step ^ 1 for step in far], far], share, 4, 512, COST, [own_tests])
    far_sum = far_own + xor_permute(far_other, "tensor", size, 1)
    sums = [xor_permute(far_sum[i * share : (i + 1) * share], "tensor", size, step) for i, step in enumerate(far)]
    here = xor_permute(tests[1][0][:16, :128], "tensor", size, 1)
    near_other, near_own = project(*arrays, [[1], [0]], share, 4, 512, LATER, [far_sum, here])
    late = tests[2][0][: near_other.shape[1], : near_other.shape[2]].astype(jnp.float32)
    pieces = [near_other[k : k + 1] for k in range(share)]
    pieces[0] = pieces[0] + 0.0 * late[None]
    arrived = jnp.concatenate([xor_permute(one, "tensor", size, 1) for one in pieces])

    unit_outs = units([near_own, arrived] + sums, share, rank, size)
    unit_parts = [unit_outs[0]] + [xor_permute(unit_outs[step], "tensor", size, step) for step in range(1, size)]
    part = score(unit_parts, tests, share)
    parts = [part] + [xor_permute(part, "tensor", size, step) for step in range(1, size)]
    while len(parts) > 1:
        parts = [parts[i] + parts[i + 1] for i in range(0, len(parts), 2)]
    return parts[0]


def solution(mesh):
    placed = (
        P(("groups", "dp"), None, "tensor"),
        P(("groups", "dp"), None, "tensor"),
        P("tensor", None),
        P("tensor", None),
        P(("groups", "dp")),
        P(("groups", "dp"), None),
    )
    return jax.shard_map(
        functools.partial(shards, mesh.shape["tensor"], mesh.shape["dp"]),
        mesh=mesh,
        in_specs=placed,
        out_specs=P(("groups", "dp"), None),
        check_vma=False,
    )
```

```python
import functools

import jax
import jax.numpy as jnp
from jax import lax
from jax.experimental import pallas as pl
from jax.experimental.pallas import tpu as pltpu
from jax.sharding import PartitionSpec as P

CORES = 2
SMALL = pltpu.CompilerParams(vmem_limit_bytes=8 << 20)
NT = (((1,), (1,)), ((), ()))
HBM = pl.BlockSpec(memory_space=pltpu.HBM)
in_hbm = functools.partial(pltpu.with_memory_space_constraint, memory_space=pltpu.HBM)
VMEM = pl.BlockSpec(memory_space=pltpu.VMEM)


def xor_permute(value, axis, size, step):
    return lax.ppermute(value, axis, [(i, i ^ step) for i in range(size)])


def cut_kernel(tests, out, sem):
    width = out.shape[1]
    start = pl.multiple_of(lax.axis_index("tensor") * width, 128)
    copy = pltpu.make_async_copy(tests.at[:, pl.ds(start, width)], out, sem)
    copy.start()
    copy.wait()


def cut_tests(tests, size):
    rows, width = tests.shape
    return pl.pallas_call(
        cut_kernel,
        out_shape=jax.ShapeDtypeStruct((rows, width // size), tests.dtype),
        in_specs=[HBM],
        out_specs=VMEM,
        scratch_shapes=[pltpu.SemaphoreType.DMA],
        compiler_params=SMALL,
    )(in_hbm(tests))


COST = 1 << 32
LATER = 1<<10


def project_kernel(steps, share, ahead, piece, after, act, og, wi, wo, lens, *refs):
    refs = refs[after:]
    outs, (buf, wibuf, wobuf, lenbuf, sem, wsem) = refs[:-6], refs[-6:]
    me = lax.axis_index("tensor")
    rank = wibuf.shape[0]
    slots = buf.shape[2]
    count = len(steps) * share
    tokens = count * slots
    small = [
        pltpu.make_async_copy(wi, wibuf, wsem.at[0]),
        pltpu.make_async_copy(wo, wobuf, wsem.at[1]),
        pltpu.make_async_copy(lens, lenbuf, wsem.at[2]),
    ]
    pieces = [(side, at) for side, ref in enumerate((act, og)) for at in range(0, ref.shape[2], piece)]
    copies = []
    for slot, (side, at) in enumerate(pieces):
        width = min(piece, (act, og)[side].shape[2] - at)
        copies.append(
            [
                pltpu.make_async_copy(
                    (act, og)[side].at[pl.ds((me ^ step) * share, share), :, pl.ds(at, width)],
                    buf.at[slot, pl.ds(i * share, share), :, pl.ds(0, width)],
                    sem.at[slot, i],
                )
                for i, step in enumerate(steps)
            ]
        )
    small[0].start()
    for slot, group in enumerate(copies):
        if slot == 1:
            small[1].start()
            small[2].start()
        if slot < ahead:
            for copy in group:
                copy.start()
    sums = [None, None]
    for slot, (side, at) in enumerate(pieces):
        if at == 0:
            small[side].wait()
        for copy in copies[slot]:
            copy.wait()
        if slot + ahead < len(pieces):
            for copy in copies[slot + ahead]:
                copy.start()
        weight = (wibuf, wobuf)[side][:, at : at + piece]
        token = buf[slot].reshape(tokens, piece)[:, : weight.shape[1]]
        part = lax.dot_general(weight, token, NT, preferred_element_type=jnp.float32)
        sums[side] = part if sums[side] is None else sums[side] + part
    small[2].wait()
    col = lax.broadcasted_iota(jnp.int32, (rank, slots), 1)
    places = [out.at[i] for out in outs for i in range(out.shape[0])]
    for slot, out in enumerate(places):
        length = lenbuf[(me ^ steps[slot // share]) * share + slot % share]
        one = sums[0][:, slot * slots : (slot + 1) * slots] * (1.0 / length.astype(jnp.float32))
        out[:rank] = jnp.where(col < length, one, 0.0)
        out[rank:] = sums[1][:, slot * slots : (slot + 1) * slots]


def project(act, og, wi, wo, lens, groups, share, ahead, piece, cost, after=()):
    steps = [step for group in groups for step in group]
    count = len(steps) * share
    slots, feat, hidden = act.shape[1], act.shape[2], og.shape[2]
    rank = wi.shape[0]
    pieces = -(-feat // piece) - (-hidden // piece)
    return pl.pallas_call(
        functools.partial(project_kernel, steps, share, ahead, piece, len(after)),
        out_shape=[jax.ShapeDtypeStruct((len(group) * share, 2 * rank, slots), jnp.float32) for group in groups],
        in_specs=[HBM] * 5 + [VMEM] * len(after),
        out_specs=[VMEM] * len(groups),
        scratch_shapes=[
            pltpu.VMEM((pieces, count, slots, piece), act.dtype),
            pltpu.VMEM((rank, feat), wi.dtype),
            pltpu.VMEM((rank, hidden), wo.dtype),
            pltpu.SMEM(lens.shape, lens.dtype),
            pltpu.SemaphoreType.DMA((pieces, len(steps))),
            pltpu.SemaphoreType.DMA((3,)),
        ],
        compiler_params=pltpu.CompilerParams(vmem_limit_bytes=32 << 20),
        cost_estimate=pl.CostEstimate(flops=cost, bytes_accessed=cost // 256, transcendentals=0),
    )(*map(in_hbm, (act, og, wi, wo, lens)), *after)


def unit_kernel(share, rank, size, *refs):
    parts, outs = refs[: -2 - size], refs[-2 - size : -2]
    pairs, held = refs[-2:]
    me = lax.axis_index("tensor")
    rows = rank * rank // 128
    span = rows // size
    dot = functools.partial(lax.dot_general, dimension_numbers=NT, preferred_element_type=jnp.float32)
    for k in range(share):
        full = parts[0][k]
        for part in parts[1:]:
            full = full + part[k]
        high = full.astype(jnp.bfloat16)
        low = (full - high.astype(jnp.float32)).astype(jnp.bfloat16)
        left, right = slice(None, rank), slice(rank, None)
        pairs[k] = dot(high[left], high[right]) + (dot(high[left], low[right]) + dot(low[left], high[right]))
    for k in range(share):
        even = pairs[k, pl.ds(0, rows, stride=2), :]
        odd = pairs[k, pl.ds(1, rows, stride=2), :]
        flat = jnp.concatenate([even, odd], axis=1)
        scale = jnp.sqrt(jnp.sum(flat * flat) / (rank * rank) + 1e-06)
        unit = flat / scale
        for to in range(size):
            held[k, to] = unit[to * span : (to + 1) * span]
        for step in range(size):
            outs[step][k] = held[k, me ^ step]


def units(parts, share, rank, size):
    span = rank * rank // 128 // size
    return pl.pallas_call(
        functools.partial(unit_kernel, share, rank, size),
        out_shape=[jax.ShapeDtypeStruct((share, span, 128), jnp.float32)] * size,
        in_specs=[VMEM] * len(parts),
        out_specs=[VMEM] * size,
        scratch_shapes=[pltpu.VMEM((share, rank, rank), jnp.float32), pltpu.VMEM((share, size, span, 128), jnp.float32)],
        compiler_params=SMALL,
    )(*parts)


def score_kernel(share, steps, origins, *refs):
    unit_refs, test_refs, out, held = refs[: len(steps)], refs[len(steps) : -2], refs[-2], refs[-1]
    me, dp = lax.axis_index("tensor"), lax.axis_index("dp")
    for step, unit_ref in zip(steps, unit_refs):
        for k in range(share):
            held[(me ^ step) * share + k] = unit_ref[k]
    unit = jnp.concatenate([held[:, c, :] for c in range(held.shape[1])], axis=1).astype(jnp.bfloat16)
    tests = test_refs[0].shape[0]
    for (factor, offset, modulus), test_ref in zip(origins, test_refs):
        part = lax.dot_general(unit, test_ref[...], NT, preferred_element_type=jnp.float32)
        at = lax.rem(factor * dp + offset, modulus) * tests
        out[:, pl.ds(pl.multiple_of(at, 128), tests)] = part


def score(unit_parts, test_parts, share):
    size, groups = len(unit_parts), len(test_parts)
    tests, width = test_parts[0][0].shape
    origins = [origin for _, *origin in test_parts]
    return pl.pallas_call(
        functools.partial(score_kernel, share, tuple(unit_parts), origins),
        out_shape=jax.ShapeDtypeStruct((share * size, tests * groups), jnp.float32),
        in_specs=[VMEM] * (size + groups),
        out_specs=VMEM,
        scratch_shapes=[pltpu.VMEM((share * size, width // 128, 128), jnp.float32)],
        compiler_params=SMALL,
    )(*unit_parts.values(), *(shard for shard, *_ in test_parts))


def gather_tests(own, groups):
    def shift(value, step):
        return lax.ppermute(value, "dp", [(i, (i + step) % groups) for i in range(groups)])

    if groups == 4:
        first = shift(own, 1)
        return [(own, 1, 0, 4), (first, 1, 3, 4), (shift(own, -1), 1, 1, 4), (shift(first, 1), 1, 2, 4)]
    return [(own, 1, 0, groups)] + [(shift(own, step), 1, groups - step, groups) for step in range(1, groups)]


def exchange(outs, size):
    return {step: xor_permute(outs[step], "tensor", size, step) for step in [*range(2, size), 1]} | {0: outs[0]}


def shards(size, groups, activations, out_grads, proj_in, proj_out, lengths, test_grads):
    rank = proj_in.shape[1]
    share = activations.shape[0] // size
    own_tests = cut_tests(test_grads, size)
    tests = gather_tests(own_tests, groups)

    far = [CORES * x for x in range(1, size // CORES)]
    arrays = (activations, out_grads, proj_in.T, proj_out.T, lengths)
    far_other, far_own = project(*arrays, [[step ^ 1 for step in far], far], share, 4, 512, COST, [own_tests])
    far_sum = far_own + xor_permute(far_other, "tensor", size, 1)
    sums = [xor_permute(far_sum[i * share : (i + 1) * share], "tensor", size, step) for i, step in enumerate(far)]
    here = xor_permute(tests[1][0][:16, :128], "tensor", size, 1)
    near_other, near_own = project(*arrays, [[1], [0]], share, 4, 512, LATER, [far_sum, here])
    late = tests[2][0][: near_other.shape[1], : near_other.shape[2]].astype(jnp.float32)
    pieces = [near_other[k : k + 1] for k in range(share)]
    pieces[0] = pieces[0] + 0.0 * late[None]
    arrived = jnp.concatenate([xor_permute(one, "tensor", size, 1) for one in pieces])

    unit_outs = units([near_own, arrived] + sums, share, rank, size)
    unit_parts = exchange(unit_outs, size)
    part = score(unit_parts, tests, share)
    parts = exchange([part] * size, size)
    parts = [parts[step ^ (size - 2)] for step in range(size)]
    while len(parts) > 1:
        parts = [parts[i] + parts[i + 1] for i in range(0, len(parts), 2)]
    return parts[0]


def solution(mesh):
    placed = (
        P(("groups", "dp"), None, "tensor"),
        P(("groups", "dp"), None, "tensor"),
        P("tensor", None),
        P("tensor", None),
        P(("groups", "dp")),
        P(("groups", "dp"), None),
    )
    return jax.shard_map(
        functools.partial(shards, mesh.shape["tensor"], mesh.shape["dp"]),
        mesh=mesh,
        in_specs=placed,
        out_specs=P(("groups", "dp"), None),
        check_vma=False,
    )
```

```python
import functools

import jax
import jax.numpy as jnp
from jax import lax
from jax.experimental import pallas as pl
from jax.experimental.pallas import tpu as pltpu
from jax.sharding import PartitionSpec as P

CORES = 2
SMALL = pltpu.CompilerParams(vmem_limit_bytes=8 << 20)
NT = (((1,), (1,)), ((), ()))
HBM = pl.BlockSpec(memory_space=pltpu.HBM)
in_hbm = functools.partial(pltpu.with_memory_space_constraint, memory_space=pltpu.HBM)
VMEM = pl.BlockSpec(memory_space=pltpu.VMEM)


def xor_permute(value, axis, size, step):
    return lax.ppermute(value, axis, [(i, i ^ step) for i in range(size)])


def cut_kernel(tests, out, sem):
    width = out.shape[1]
    start = pl.multiple_of(lax.axis_index("tensor") * width, 128)
    copy = pltpu.make_async_copy(tests.at[:, pl.ds(start, width)], out, sem)
    copy.start()
    copy.wait()


def cut_tests(tests, size):
    rows, width = tests.shape
    return pl.pallas_call(
        cut_kernel,
        out_shape=jax.ShapeDtypeStruct((rows, width // size), tests.dtype),
        in_specs=[HBM],
        out_specs=VMEM,
        scratch_shapes=[pltpu.SemaphoreType.DMA],
        compiler_params=SMALL,
    )(in_hbm(tests))


COST = 1 << 32
LATER = 1<<10


def project_kernel(steps, later, share, ahead, piece, after, act, og, wi, wo, lens, *refs):
    if later:
        refs = refs[after:]
    else:
        given, refs = refs[0], refs[1 + after :]
    outs, (buf, wibuf, wobuf, lenbuf, sem, wsem) = refs[:-6], refs[-6:]
    me = lax.axis_index("tensor")
    rank = wibuf.shape[0]
    slots = buf.shape[2]
    small = [
        pltpu.make_async_copy(wi, wibuf, wsem.at[0]),
        pltpu.make_async_copy(wo, wobuf, wsem.at[1]),
        pltpu.make_async_copy(lens, lenbuf, wsem.at[2]),
    ]
    widths = (act.shape[2], og.shape[2])
    pieces = [(1, steps, at) for at in range(0, widths[1], piece)]
    if later:
        pieces = [(0, steps, at) for at in range(0, widths[0], piece)] + pieces
        pieces += [(0, later, at) for at in range(0, widths[0], piece)]
    copies = []
    for slot, (side, owners, at) in enumerate(pieces):
        width = min(piece, widths[side] - at)
        copies.append(
            [
                pltpu.make_async_copy(
                    (act, og)[side].at[pl.ds((me ^ step) * share, share), :, pl.ds(at, width)],
                    buf.at[slot, pl.ds(i * share, share), :, pl.ds(0, width)],
                    sem.at[slot, i],
                )
                for i, step in enumerate(owners)
            ]
        )
    needed = small if later else small[1:]
    needed[0].start()
    for slot, group in enumerate(copies[:ahead]):
        if slot == 1:
            for copy in needed[1:]:
                copy.start()
        for copy in group:
            copy.start()
    for copy in needed if later else needed[:1]:
        copy.wait()
    sums = [None, None, None]
    for slot, (side, owners, at) in enumerate(pieces):
        for copy in copies[slot]:
            copy.wait()
        for copy in copies[slot + ahead] if slot + ahead < len(pieces) else ():
            copy.start()
        weight = (wibuf, wobuf)[side][:, at : at + piece]
        here = len(owners) * share
        token = buf[slot, :here].reshape(here * slots, piece)[:, : weight.shape[1]]
        part = lax.dot_general(weight, token, NT, preferred_element_type=jnp.float32)
        to = 2 if owners is later else side
        sums[to] = part if sums[to] is None else sums[to] + part
    if not later:
        for copy in needed[1:]:
            copy.wait()
    col = lax.broadcasted_iota(jnp.int32, (rank, slots), 1)
    places = [out.at[i] for out in (outs[:-1] if later else outs) for i in range(out.shape[0])]
    for slot, out in enumerate(places):
        cols = slice(slot * slots, (slot + 1) * slots)
        length = lenbuf[(me ^ steps[slot // share]) * share + slot % share]
        one = (sums[0][:, cols] if later else given[slot]) * (1.0 / length.astype(jnp.float32))
        out[:rank] = jnp.where(col < length, one, 0.0)
        out[rank:] = sums[1][:, cols]
    for slot in range(len(later) * share):
        outs[-1][slot] = sums[2][:, slot * slots : (slot + 1) * slots]


def project(act, og, wi, wo, lens, groups, later, share, ahead, piece, cost, after=(), given=()):
    steps = [step for group in groups for step in group]
    count = len(steps) * share
    slots, feat, hidden = act.shape[1], act.shape[2], og.shape[2]
    rank = wi.shape[0]
    pieces = -(-feat // piece) * (2 if later else 0) - (-hidden // piece)
    shapes = [jax.ShapeDtypeStruct((len(group) * share, 2 * rank, slots), jnp.float32) for group in groups]
    if later:
        shapes += [jax.ShapeDtypeStruct((len(later) * share, rank, slots), jnp.float32)]
    return pl.pallas_call(
        functools.partial(project_kernel, steps, later, share, ahead, piece, len(after)),
        out_shape=shapes,
        in_specs=[HBM] * 5 + [VMEM] * (len(given) + len(after)),
        out_specs=[VMEM] * len(shapes),
        scratch_shapes=[
            pltpu.VMEM((pieces, count, slots, piece), act.dtype),
            pltpu.VMEM((rank, feat), wi.dtype),
            pltpu.VMEM((rank, hidden), wo.dtype),
            pltpu.SMEM(lens.shape, lens.dtype),
            pltpu.SemaphoreType.DMA((pieces, len(steps))),
            pltpu.SemaphoreType.DMA((3,)),
        ],
        compiler_params=pltpu.CompilerParams(vmem_limit_bytes=32 << 20),
        cost_estimate=pl.CostEstimate(flops=cost, bytes_accessed=cost // 256, transcendentals=0),
    )(*map(in_hbm, (act, og, wi, wo, lens)), *given, *after)


def unit_kernel(share, rank, size, *refs):
    parts, outs = refs[: -2 - size], refs[-2 - size : -2]
    pairs, held = refs[-2:]
    me = lax.axis_index("tensor")
    rows = rank * rank // 128
    span = rows // size
    dot = functools.partial(lax.dot_general, dimension_numbers=NT, preferred_element_type=jnp.float32)
    for k in range(share):
        full = parts[0][k]
        for part in parts[1:]:
            full = full + part[k]
        high = full.astype(jnp.bfloat16)
        low = (full - high.astype(jnp.float32)).astype(jnp.bfloat16)
        left, right = slice(None, rank), slice(rank, None)
        pairs[k] = dot(high[left], high[right]) + (dot(high[left], low[right]) + dot(low[left], high[right]))
    for k in range(share):
        even = pairs[k, pl.ds(0, rows, stride=2), :]
        odd = pairs[k, pl.ds(1, rows, stride=2), :]
        flat = jnp.concatenate([even, odd], axis=1)
        scale = jnp.sqrt(jnp.sum(flat * flat) / (rank * rank) + 1e-06)
        unit = flat / scale
        for to in range(size):
            held[k, to] = unit[to * span : (to + 1) * span]
        for step in range(size):
            outs[step][k] = held[k, me ^ step]


def units(parts, share, rank, size):
    span = rank * rank // 128 // size
    return pl.pallas_call(
        functools.partial(unit_kernel, share, rank, size),
        out_shape=[jax.ShapeDtypeStruct((share, span, 128), jnp.float32)] * size,
        in_specs=[VMEM] * len(parts),
        out_specs=[VMEM] * size,
        scratch_shapes=[pltpu.VMEM((share, rank, rank), jnp.float32), pltpu.VMEM((share, size, span, 128), jnp.float32)],
        compiler_params=SMALL,
    )(*parts)


def score_kernel(share, steps, origins, *refs):
    unit_refs, test_refs, out, held = refs[: len(steps)], refs[len(steps) : -2], refs[-2], refs[-1]
    me, dp = lax.axis_index("tensor"), lax.axis_index("dp")
    for step, unit_ref in zip(steps, unit_refs):
        for k in range(share):
            held[(me ^ step) * share + k] = unit_ref[k]
    unit = jnp.concatenate([held[:, c, :] for c in range(held.shape[1])], axis=1).astype(jnp.bfloat16)
    tests = test_refs[0].shape[0]
    for (factor, offset, modulus), test_ref in zip(origins, test_refs):
        part = lax.dot_general(unit, test_ref[...], NT, preferred_element_type=jnp.float32)
        at = lax.rem(factor * dp + offset, modulus) * tests
        out[:, pl.ds(pl.multiple_of(at, 128), tests)] = part


def score(unit_parts, test_parts, share):
    size, groups = len(unit_parts), len(test_parts)
    tests, width = test_parts[0][0].shape
    origins = [origin for _, *origin in test_parts]
    return pl.pallas_call(
        functools.partial(score_kernel, share, tuple(unit_parts), origins),
        out_shape=jax.ShapeDtypeStruct((share * size, tests * groups), jnp.float32),
        in_specs=[VMEM] * (size + groups),
        out_specs=VMEM,
        scratch_shapes=[pltpu.VMEM((share * size, width // 128, 128), jnp.float32)],
        compiler_params=SMALL,
    )(*unit_parts.values(), *(shard for shard, *_ in test_parts))


def gather_tests(own, groups):
    def shift(value, step):
        return lax.ppermute(value, "dp", [(i, (i + step) % groups) for i in range(groups)])

    if groups == 4:
        first = shift(own, 1)
        return [(own, 1, 0, 4), (first, 1, 3, 4), (shift(own, -1), 1, 1, 4), (shift(first, 1), 1, 2, 4)]
    return [(own, 1, 0, groups)] + [(shift(own, step), 1, groups - step, groups) for step in range(1, groups)]


def exchange(outs, size):
    return {step: xor_permute(outs[step], "tensor", size, step) for step in [*range(2, size), 1]} | {0: outs[0]}


def shards(size, groups, activations, out_grads, proj_in, proj_out, lengths, test_grads):
    rank = proj_in.shape[1]
    share = activations.shape[0] // size
    own_tests = cut_tests(test_grads, size)
    tests = gather_tests(own_tests, groups)

    far = [CORES * x for x in range(1, size // CORES)]
    arrays = (activations, out_grads, proj_in.T, proj_out.T, lengths)
    sends, near = [[step ^ 1 for step in far], far], [1, 0]
    far_other, far_own, in_rows = project(*arrays, sends, near, share, 4, 512, COST, [own_tests])
    far_sum = far_own + xor_permute(far_other, "tensor", size, 1)
    sums = [xor_permute(far_sum[i * share : (i + 1) * share], "tensor", size, step) for i, step in enumerate(far)]
    here = xor_permute(tests[1][0][:16, :128], "tensor", size, 1)
    near_other, near_own = project(*arrays, [[1], [0]], [], share, 4, 512, LATER, [far_sum, here], [in_rows])
    late = tests[2][0][: near_other.shape[1], : near_other.shape[2]].astype(jnp.float32)
    pieces = [near_other[k : k + 1] for k in range(share)]
    pieces[0] = pieces[0] + 0.0 * late[None]
    arrived = jnp.concatenate([xor_permute(one, "tensor", size, 1) for one in pieces])

    unit_outs = units([near_own, arrived] + sums, share, rank, size)
    unit_parts = exchange(unit_outs, size)
    part = score(unit_parts, tests, share)
    parts = exchange([part] * size, size)
    parts = [parts[step ^ (size - 2)] for step in range(size)]
    while len(parts) > 1:
        parts = [parts[i] + parts[i + 1] for i in range(0, len(parts), 2)]
    return parts[0]


def solution(mesh):
    placed = (
        P(("groups", "dp"), None, "tensor"),
        P(("groups", "dp"), None, "tensor"),
        P("tensor", None),
        P("tensor", None),
        P(("groups", "dp")),
        P(("groups", "dp"), None),
    )
    return jax.shard_map(
        functools.partial(shards, mesh.shape["tensor"], mesh.shape["dp"]),
        mesh=mesh,
        in_specs=placed,
        out_specs=P(("groups", "dp"), None),
        check_vma=False,
    )
```

```python
import functools

import jax
import jax.numpy as jnp
from jax import lax
from jax.experimental import pallas as pl
from jax.experimental.pallas import tpu as pltpu
from jax.sharding import PartitionSpec as P

CORES = 2
SMALL = pltpu.CompilerParams(vmem_limit_bytes=8 << 20)
NT = (((1,), (1,)), ((), ()))
HBM = pl.BlockSpec(memory_space=pltpu.HBM)
in_hbm = functools.partial(pltpu.with_memory_space_constraint, memory_space=pltpu.HBM)
VMEM = pl.BlockSpec(memory_space=pltpu.VMEM)


def xor_permute(value, axis, size, step):
    return lax.ppermute(value, axis, [(i, i ^ step) for i in range(size)])


def cut_kernel(tests, out, sem):
    width = out.shape[1]
    start = pl.multiple_of(lax.axis_index("tensor") * width, 128)
    copy = pltpu.make_async_copy(tests.at[:, pl.ds(start, width)], out, sem)
    copy.start()
    copy.wait()


def cut_tests(tests, size):
    rows, width = tests.shape
    return pl.pallas_call(
        cut_kernel,
        out_shape=jax.ShapeDtypeStruct((rows, width // size), tests.dtype),
        in_specs=[HBM],
        out_specs=VMEM,
        scratch_shapes=[pltpu.SemaphoreType.DMA],
        compiler_params=SMALL,
    )(in_hbm(tests))


COST = 1 << 32
LATER = 1<<10


def project_kernel(steps, share, ahead, pieces, after, act, og, wi, wo, lens, *refs):
    refs = refs[after:]
    outs, (buf, wibuf, wobuf, lenbuf, sem, wsem) = refs[:-6], refs[-6:]
    me = lax.axis_index("tensor")
    rank = wibuf.shape[0]
    slots = buf.shape[2]
    count = len(steps) * share
    tokens = count * slots
    small = [
        pltpu.make_async_copy(wi, wibuf, wsem.at[0]),
        pltpu.make_async_copy(wo, wobuf, wsem.at[1]),
        pltpu.make_async_copy(lens, lenbuf, wsem.at[2]),
    ]
    copies = []
    for slot, (side, at, width) in enumerate(pieces):
        copies.append(
            [
                pltpu.make_async_copy(
                    (act, og)[side].at[pl.ds((me ^ step) * share, share), :, pl.ds(at, width)],
                    buf.at[slot, pl.ds(i * share, share), :, pl.ds(0, width)],
                    sem.at[slot, i],
                )
                for i, step in enumerate(steps)
            ]
        )
    small[0].start()
    for slot, group in enumerate(copies):
        if slot == 1:
            small[1].start()
            small[2].start()
        if slot < ahead:
            for copy in group:
                copy.start()
    sums = [None, None]
    for slot, (side, at, width) in enumerate(pieces):
        if at == 0:
            small[side].wait()
        for copy in copies[slot]:
            copy.wait()
        if slot + ahead < len(pieces):
            for copy in copies[slot + ahead]:
                copy.start()
        weight = (wibuf, wobuf)[side][:, at : at + width]
        token = buf[slot].reshape(tokens, buf.shape[3])[:, :width]
        part = lax.dot_general(weight, token, NT, preferred_element_type=jnp.float32)
        sums[side] = part if sums[side] is None else sums[side] + part
    small[2].wait()
    col = lax.broadcasted_iota(jnp.int32, (rank, slots), 1)
    places = [out.at[i] for out in outs for i in range(out.shape[0])]
    for slot, out in enumerate(places):
        length = lenbuf[(me ^ steps[slot // share]) * share + slot % share]
        one = sums[0][:, slot * slots : (slot + 1) * slots] * (1.0 / length.astype(jnp.float32))
        out[:rank] = jnp.where(col < length, one, 0.0)
        out[rank:] = sums[1][:, slot * slots : (slot + 1) * slots]


def project(act, og, wi, wo, lens, groups, share, ahead, piece, cost, after=()):
    steps = [step for group in groups for step in group]
    count = len(steps) * share
    slots, feat, hidden = act.shape[1], act.shape[2], og.shape[2]
    rank = wi.shape[0]
    pieces = [(0, at, min(512, feat - at)) for at in range(0, feat, 512)]
    pieces += [(1, at, min(piece, hidden - at)) for at in range(0, hidden, piece)]
    return pl.pallas_call(
        functools.partial(project_kernel, steps, share, ahead, pieces, len(after)),
        out_shape=[jax.ShapeDtypeStruct((len(group) * share, 2 * rank, slots), jnp.float32) for group in groups],
        in_specs=[HBM] * 5 + [VMEM] * len(after),
        out_specs=[VMEM] * len(groups),
        scratch_shapes=[
            pltpu.VMEM((len(pieces), count, slots, piece), act.dtype),
            pltpu.VMEM((rank, feat), wi.dtype),
            pltpu.VMEM((rank, hidden), wo.dtype),
            pltpu.SMEM(lens.shape, lens.dtype),
            pltpu.SemaphoreType.DMA((len(pieces), len(steps))),
            pltpu.SemaphoreType.DMA((3,)),
        ],
        compiler_params=pltpu.CompilerParams(vmem_limit_bytes=32 << 20),
        cost_estimate=pl.CostEstimate(flops=cost, bytes_accessed=cost // 256, transcendentals=0),
    )(*map(in_hbm, (act, og, wi, wo, lens)), *after)


def unit_kernel(share, rank, size, *refs):
    parts, outs = refs[: -2 - size], refs[-2 - size : -2]
    pairs, held = refs[-2:]
    me = lax.axis_index("tensor")
    rows = rank * rank // 128
    span = rows // size
    dot = functools.partial(lax.dot_general, dimension_numbers=NT, preferred_element_type=jnp.float32)
    for k in range(share):
        full = parts[0][k]
        for part in parts[1:]:
            full = full + part[k]
        high = full.astype(jnp.bfloat16)
        low = (full - high.astype(jnp.float32)).astype(jnp.bfloat16)
        left, right = slice(None, rank), slice(rank, None)
        pairs[k] = dot(high[left], high[right]) + (dot(high[left], low[right]) + dot(low[left], high[right]))
    for k in range(share):
        even = pairs[k, pl.ds(0, rows, stride=2), :]
        odd = pairs[k, pl.ds(1, rows, stride=2), :]
        flat = jnp.concatenate([even, odd], axis=1)
        scale = jnp.sqrt(jnp.sum(flat * flat) / (rank * rank) + 1e-06)
        unit = flat / scale
        for to in range(size):
            held[k, to] = unit[to * span : (to + 1) * span]
        for step in range(size):
            outs[step][k] = held[k, me ^ step]


def units(parts, share, rank, size):
    span = rank * rank // 128 // size
    return pl.pallas_call(
        functools.partial(unit_kernel, share, rank, size),
        out_shape=[jax.ShapeDtypeStruct((share, span, 128), jnp.float32)] * size,
        in_specs=[VMEM] * len(parts),
        out_specs=[VMEM] * size,
        scratch_shapes=[pltpu.VMEM((share, rank, rank), jnp.float32), pltpu.VMEM((share, size, span, 128), jnp.float32)],
        compiler_params=SMALL,
    )(*parts)


def score_kernel(share, steps, origins, *refs):
    unit_refs, test_refs, out, held = refs[: len(steps)], refs[len(steps) : -2], refs[-2], refs[-1]
    me, dp = lax.axis_index("tensor"), lax.axis_index("dp")
    for step, unit_ref in zip(steps, unit_refs):
        for k in range(share):
            held[(me ^ step) * share + k] = unit_ref[k]
    unit = jnp.concatenate([held[:, c, :] for c in range(held.shape[1])], axis=1).astype(jnp.bfloat16)
    tests = test_refs[0].shape[0]
    for (factor, offset, modulus), test_ref in zip(origins, test_refs):
        part = lax.dot_general(unit, test_ref[...], NT, preferred_element_type=jnp.float32)
        at = lax.rem(factor * dp + offset, modulus) * tests
        out[:, pl.ds(pl.multiple_of(at, 128), tests)] = part


def score(unit_parts, test_parts, share):
    size, groups = len(unit_parts), len(test_parts)
    tests, width = test_parts[0][0].shape
    origins = [origin for _, *origin in test_parts]
    return pl.pallas_call(
        functools.partial(score_kernel, share, tuple(unit_parts), origins),
        out_shape=jax.ShapeDtypeStruct((share * size, tests * groups), jnp.float32),
        in_specs=[VMEM] * (size + groups),
        out_specs=VMEM,
        scratch_shapes=[pltpu.VMEM((share * size, width // 128, 128), jnp.float32)],
        compiler_params=SMALL,
    )(*unit_parts.values(), *(shard for shard, *_ in test_parts))


def gather_tests(own, groups):
    def shift(value, step):
        return lax.ppermute(value, "dp", [(i, (i + step) % groups) for i in range(groups)])

    if groups == 4:
        first = shift(own, 1)
        return [(own, 1, 0, 4), (first, 1, 3, 4), (shift(own, -1), 1, 1, 4), (shift(first, 1), 1, 2, 4)]
    return [(own, 1, 0, groups)] + [(shift(own, step), 1, groups - step, groups) for step in range(1, groups)]


def exchange(outs, size):
    return {step: xor_permute(outs[step], "tensor", size, step) for step in [*range(2, size), 1]} | {0: outs[0]}


def shards(size, groups, activations, out_grads, proj_in, proj_out, lengths, test_grads):
    rank = proj_in.shape[1]
    share = activations.shape[0] // size
    own_tests = cut_tests(test_grads, size)
    tests = gather_tests(own_tests, groups)

    far = [CORES * x for x in range(1, size // CORES)]
    arrays = (activations, out_grads, proj_in.T, proj_out.T, lengths)
    far_other, far_own = project(*arrays, [[step ^ 1 for step in far], far], share, 3, 896, COST, [own_tests])
    far_sum = far_own + xor_permute(far_other, "tensor", size, 1)
    sums = [xor_permute(far_sum[i * share : (i + 1) * share], "tensor", size, step) for i, step in enumerate(far)]
    here = xor_permute(tests[1][0][:16, :128], "tensor", size, 1)
    near_other, near_own = project(*arrays, [[1], [0]], share, 3, 896, LATER, [far_sum, here])
    late = tests[2][0][: near_other.shape[1], : near_other.shape[2]].astype(jnp.float32)
    pieces = [near_other[k : k + 1] for k in range(share)]
    pieces[0] = pieces[0] + 0.0 * late[None]
    arrived = jnp.concatenate([xor_permute(one, "tensor", size, 1) for one in pieces])

    unit_outs = units([near_own, arrived] + sums, share, rank, size)
    unit_parts = exchange(unit_outs, size)
    part = score(unit_parts, tests, share)
    parts = exchange([part] * size, size)
    parts = [parts[step ^ (size - 2)] for step in range(size)]
    while len(parts) > 1:
        parts = [parts[i] + parts[i + 1] for i in range(0, len(parts), 2)]
    return parts[0]


def solution(mesh):
    placed = (
        P(("groups", "dp"), None, "tensor"),
        P(("groups", "dp"), None, "tensor"),
        P("tensor", None),
        P("tensor", None),
        P(("groups", "dp")),
        P(("groups", "dp"), None),
    )
    return jax.shard_map(
        functools.partial(shards, mesh.shape["tensor"], mesh.shape["dp"]),
        mesh=mesh,
        in_specs=placed,
        out_specs=P(("groups", "dp"), None),
        check_vma=False,
    )
```

```python
import functools

import jax
import jax.numpy as jnp
from jax import lax
from jax.experimental import pallas as pl
from jax.experimental.pallas import tpu as pltpu
from jax.sharding import PartitionSpec as P

CORES = 2
SMALL = pltpu.CompilerParams(vmem_limit_bytes=8 << 20)
NT = (((1,), (1,)), ((), ()))
HBM = pl.BlockSpec(memory_space=pltpu.HBM)
in_hbm = functools.partial(pltpu.with_memory_space_constraint, memory_space=pltpu.HBM)
VMEM = pl.BlockSpec(memory_space=pltpu.VMEM)


def xor_permute(value, axis, size, step):
    return lax.ppermute(value, axis, [(i, i ^ step) for i in range(size)])


def cut_kernel(tests, out, sem):
    width = out.shape[1]
    start = pl.multiple_of(lax.axis_index("tensor") * width, 128)
    copy = pltpu.make_async_copy(tests.at[:, pl.ds(start, width)], out, sem)
    copy.start()
    copy.wait()


def cut_tests(tests, size):
    rows, width = tests.shape
    return pl.pallas_call(
        cut_kernel,
        out_shape=jax.ShapeDtypeStruct((rows, width // size), tests.dtype),
        in_specs=[HBM],
        out_specs=VMEM,
        scratch_shapes=[pltpu.SemaphoreType.DMA],
        compiler_params=SMALL,
    )(in_hbm(tests))


COST = 1 << 32
LATER = 1<<10


def project_kernel(steps, share, ahead, piece, after, act, og, wi, wo, lens, *refs):
    refs = refs[after:]
    outs, (buf, wibuf, wobuf, lenbuf, sem, wsem) = refs[:-6], refs[-6:]
    me = lax.axis_index("tensor")
    rank = wibuf.shape[0]
    slots = buf.shape[2]
    count = len(steps) * share
    tokens = count * slots
    small = [
        pltpu.make_async_copy(wi, wibuf, wsem.at[0]),
        pltpu.make_async_copy(wo, wobuf, wsem.at[1]),
        pltpu.make_async_copy(lens, lenbuf, wsem.at[2]),
    ]
    pieces = [(side, at) for side, ref in enumerate((act, og)) for at in range(0, ref.shape[2], piece)]
    copies = []
    for slot, (side, at) in enumerate(pieces):
        width = min(piece, (act, og)[side].shape[2] - at)
        copies.append(
            [
                pltpu.make_async_copy(
                    (act, og)[side].at[pl.ds((me ^ step) * share, share), :, pl.ds(at, width)],
                    buf.at[slot, pl.ds(i * share, share), :, pl.ds(0, width)],
                    sem.at[slot, i],
                )
                for i, step in enumerate(steps)
            ]
        )
    small[0].start()
    for slot, group in enumerate(copies):
        if slot == 1:
            small[1].start()
            small[2].start()
        if slot < ahead:
            for copy in group:
                copy.start()
    sums = [None, None]
    for slot, (side, at) in enumerate(pieces):
        if at == 0:
            small[side].wait()
        for copy in copies[slot]:
            copy.wait()
        if slot + ahead < len(pieces):
            for copy in copies[slot + ahead]:
                copy.start()
        weight = (wibuf, wobuf)[side][:, at : at + piece]
        token = buf[slot].reshape(tokens, piece)[:, : weight.shape[1]]
        part = lax.dot_general(weight, token, NT, preferred_element_type=jnp.float32)
        sums[side] = part if sums[side] is None else sums[side] + part
    small[2].wait()
    col = lax.broadcasted_iota(jnp.int32, (rank, slots), 1)
    places = [out.at[i] for out in outs for i in range(out.shape[0])]
    for slot, out in enumerate(places):
        length = lenbuf[(me ^ steps[slot // share]) * share + slot % share]
        one = sums[0][:, slot * slots : (slot + 1) * slots] * (1.0 / length.astype(jnp.float32))
        out[:rank] = jnp.where(col < length, one, 0.0)
        out[rank:] = sums[1][:, slot * slots : (slot + 1) * slots]


def project(act, og, wi, wo, lens, groups, share, ahead, piece, cost, after=()):
    steps = [step for group in groups for step in group]
    count = len(steps) * share
    slots, feat, hidden = act.shape[1], act.shape[2], og.shape[2]
    rank = wi.shape[0]
    pieces = -(-feat // piece) - (-hidden // piece)
    return pl.pallas_call(
        functools.partial(project_kernel, steps, share, ahead, piece, len(after)),
        out_shape=[jax.ShapeDtypeStruct((len(group) * share, 2 * rank, slots), jnp.float32) for group in groups],
        in_specs=[HBM] * 5 + [VMEM] * len(after),
        out_specs=[VMEM] * len(groups),
        scratch_shapes=[
            pltpu.VMEM((pieces, count, slots, piece), act.dtype),
            pltpu.VMEM((rank, feat), wi.dtype),
            pltpu.VMEM((rank, hidden), wo.dtype),
            pltpu.SMEM(lens.shape, lens.dtype),
            pltpu.SemaphoreType.DMA((pieces, len(steps))),
            pltpu.SemaphoreType.DMA((3,)),
        ],
        compiler_params=pltpu.CompilerParams(vmem_limit_bytes=32 << 20),
        cost_estimate=pl.CostEstimate(flops=cost, bytes_accessed=cost // 256, transcendentals=0),
    )(*map(in_hbm, (act, og, wi, wo, lens)), *after)


def unit_kernel(share, rank, size, *refs):
    parts, outs = refs[: -2 - size], refs[-2 - size : -2]
    pairs, held = refs[-2:]
    me = lax.axis_index("tensor")
    rows = rank * rank // 128
    span = rows // size
    dot = functools.partial(lax.dot_general, dimension_numbers=NT, preferred_element_type=jnp.float32)
    for k in range(share):
        full = parts[0][k]
        for part in parts[1:]:
            full = full + part[k]
        high = full.astype(jnp.bfloat16)
        low = (full - high.astype(jnp.float32)).astype(jnp.bfloat16)
        left, right = slice(None, rank), slice(rank, None)
        pairs[k] = dot(high[left], high[right]) + (dot(high[left], low[right]) + dot(low[left], high[right]))
    for k in range(share):
        even = pairs[k, pl.ds(0, rows, stride=2), :]
        odd = pairs[k, pl.ds(1, rows, stride=2), :]
        flat = jnp.concatenate([even, odd], axis=1)
        scale = jnp.sqrt(jnp.sum(flat * flat) / (rank * rank) + 1e-06)
        unit = flat / scale
        for to in range(size):
            held[k, to] = unit[to * span : (to + 1) * span]
        for step in range(size):
            outs[step][k] = held[k, me ^ step]


def units(parts, share, rank, size):
    span = rank * rank // 128 // size
    return pl.pallas_call(
        functools.partial(unit_kernel, share, rank, size),
        out_shape=[jax.ShapeDtypeStruct((share, span, 128), jnp.float32)] * size,
        in_specs=[VMEM] * len(parts),
        out_specs=[VMEM] * size,
        scratch_shapes=[pltpu.VMEM((share, rank, rank), jnp.float32), pltpu.VMEM((share, size, span, 128), jnp.float32)],
        compiler_params=SMALL,
    )(*parts)


def score_kernel(share, steps, origins, *refs):
    unit_refs, test_refs, out, held = refs[: len(steps)], refs[len(steps) : -2], refs[-2], refs[-1]
    me, dp = lax.axis_index("tensor"), lax.axis_index("dp")
    for step, unit_ref in zip(steps, unit_refs):
        for k in range(share):
            held[(me ^ step) * share + k] = unit_ref[k]
    unit = jnp.concatenate([held[:, c, :] for c in range(held.shape[1])], axis=1).astype(jnp.bfloat16)
    tests = test_refs[0].shape[0]
    for (factor, offset, modulus), test_ref in zip(origins, test_refs):
        part = lax.dot_general(unit, test_ref[...], NT, preferred_element_type=jnp.float32)
        at = lax.rem(factor * dp + offset, modulus) * tests
        out[:, pl.ds(pl.multiple_of(at, 128), tests)] = part


def score(unit_parts, test_parts, share):
    size, groups = len(unit_parts), len(test_parts)
    tests, width = test_parts[0][0].shape
    origins = [origin for _, *origin in test_parts]
    return pl.pallas_call(
        functools.partial(score_kernel, share, tuple(unit_parts), origins),
        out_shape=jax.ShapeDtypeStruct((share * size, tests * groups), jnp.float32),
        in_specs=[VMEM] * (size + groups),
        out_specs=VMEM,
        scratch_shapes=[pltpu.VMEM((share * size, width // 128, 128), jnp.float32)],
        compiler_params=SMALL,
    )(*unit_parts.values(), *(shard for shard, *_ in test_parts))


def gather_tests(own, groups):
    def shift(value, step):
        return lax.ppermute(value, "dp", [(i, (i + step) % groups) for i in range(groups)])

    if groups == 4:
        first = shift(own, 1)
        return [(own, 1, 0, 4), (first, 1, 3, 4), (shift(own, -1), 1, 1, 4), (shift(first, 1), 1, 2, 4)]
    return [(own, 1, 0, groups)] + [(shift(own, step), 1, groups - step, groups) for step in range(1, groups)]


def exchange(outs, size):
    return {step: xor_permute(outs[step], "tensor", size, step) for step in [*range(2, size), 1]} | {0: outs[0]}


def shards(size, groups, activations, out_grads, proj_in, proj_out, lengths, test_grads):
    rank = proj_in.shape[1]
    share = activations.shape[0] // size
    own_tests = cut_tests(test_grads, size)
    tests = gather_tests(own_tests, groups)

    far = [CORES * x for x in range(1, size // CORES)]
    arrays = (activations, out_grads, proj_in.T, proj_out.T, lengths)
    far_other, far_own = project(*arrays, [[step ^ 1 for step in far], far], share, 5, 512, COST, [own_tests])
    far_sum = far_own + xor_permute(far_other, "tensor", size, 1)
    sums = [xor_permute(far_sum[i * share : (i + 1) * share], "tensor", size, step) for i, step in enumerate(far)]
    here = xor_permute(tests[1][0][:16, :128], "tensor", size, 1)
    near_other, near_own = project(*arrays, [[1], [0]], share, 3, 512, LATER, [far_sum, here])
    late = tests[2][0][: near_other.shape[1], : near_other.shape[2]].astype(jnp.float32)
    pieces = [near_other[k : k + 1] for k in range(share)]
    pieces[0] = pieces[0] + 0.0 * late[None]
    arrived = jnp.concatenate([xor_permute(one, "tensor", size, 1) for one in pieces])

    unit_outs = units([near_own, arrived] + sums, share, rank, size)
    unit_parts = exchange(unit_outs, size)
    part = score(unit_parts, tests, share)
    parts = exchange([part] * size, size)
    parts = [parts[step ^ (size - 2)] for step in range(size)]
    while len(parts) > 1:
        parts = [parts[i] + parts[i + 1] for i in range(0, len(parts), 2)]
    return parts[0]


def solution(mesh):
    placed = (
        P(("groups", "dp"), None, "tensor"),
        P(("groups", "dp"), None, "tensor"),
        P("tensor", None),
        P("tensor", None),
        P(("groups", "dp")),
        P(("groups", "dp"), None),
    )
    return jax.shard_map(
        functools.partial(shards, mesh.shape["tensor"], mesh.shape["dp"]),
        mesh=mesh,
        in_specs=placed,
        out_specs=P(("groups", "dp"), None),
        check_vma=False,
    )
```

```python
import functools

import jax
import jax.numpy as jnp
from jax import lax
from jax.experimental import pallas as pl
from jax.experimental.pallas import tpu as pltpu
from jax.sharding import PartitionSpec as P

CORES = 2
SMALL = pltpu.CompilerParams(vmem_limit_bytes=8 << 20)
NT = (((1,), (1,)), ((), ()))
HBM = pl.BlockSpec(memory_space=pltpu.HBM)
in_hbm = functools.partial(pltpu.with_memory_space_constraint, memory_space=pltpu.HBM)
VMEM = pl.BlockSpec(memory_space=pltpu.VMEM)


def xor_permute(value, axis, size, step):
    return lax.ppermute(value, axis, [(i, i ^ step) for i in range(size)])


def cut_kernel(tests, out, sem):
    width = out.shape[1]
    start = pl.multiple_of(lax.axis_index("tensor") * width, 128)
    copy = pltpu.make_async_copy(tests.at[:, pl.ds(start, width)], out, sem)
    copy.start()
    copy.wait()


def cut_tests(tests, size):
    rows, width = tests.shape
    return pl.pallas_call(
        cut_kernel,
        out_shape=jax.ShapeDtypeStruct((rows, width // size), tests.dtype),
        in_specs=[HBM],
        out_specs=VMEM,
        scratch_shapes=[pltpu.SemaphoreType.DMA],
        compiler_params=SMALL,
    )(in_hbm(tests))


COST = 1 << 32
LATER = 1<<10


def project_kernel(steps, share, ahead, piece, after, act, og, wi, wo, lens, *refs):
    refs = refs[after:]
    outs, (buf, wibuf, wobuf, lenbuf, sem, wsem) = refs[:-6], refs[-6:]
    me = lax.axis_index("tensor")
    rank = wibuf.shape[0]
    slots = buf.shape[2]
    count = len(steps) * share
    tokens = count * slots
    small = [
        pltpu.make_async_copy(wi, wibuf, wsem.at[0]),
        pltpu.make_async_copy(wo, wobuf, wsem.at[1]),
        pltpu.make_async_copy(lens, lenbuf, wsem.at[2]),
    ]
    pieces = [(side, at) for side, ref in enumerate((act, og)) for at in range(0, ref.shape[2], piece)]
    copies = []
    for slot, (side, at) in enumerate(pieces):
        width = min(piece, (act, og)[side].shape[2] - at)
        copies.append(
            [
                pltpu.make_async_copy(
                    (act, og)[side].at[pl.ds((me ^ step) * share, share), :, pl.ds(at, width)],
                    buf.at[slot, pl.ds(i * share, share), :, pl.ds(0, width)],
                    sem.at[slot, i],
                )
                for i, step in enumerate(steps)
            ]
        )
    small[0].start()
    for slot, group in enumerate(copies):
        if slot == 1:
            small[1].start()
            small[2].start()
        if slot < ahead:
            for copy in group:
                copy.start()
    sums = [None, None]
    for slot, (side, at) in enumerate(pieces):
        if at == 0:
            small[side].wait()
        for copy in copies[slot]:
            copy.wait()
        if slot + ahead < len(pieces):
            for copy in copies[slot + ahead]:
                copy.start()
        weight = (wibuf, wobuf)[side][:, at : at + piece]
        token = buf[slot].reshape(tokens, piece)[:, : weight.shape[1]]
        part = lax.dot_general(weight, token, NT, preferred_element_type=jnp.float32)
        sums[side] = part if sums[side] is None else sums[side] + part
    small[2].wait()
    col = lax.broadcasted_iota(jnp.int32, (rank, slots), 1)
    places = [out.at[i] for out in outs for i in range(out.shape[0])]
    for slot, out in enumerate(places):
        length = lenbuf[(me ^ steps[slot // share]) * share + slot % share]
        one = sums[0][:, slot * slots : (slot + 1) * slots] * (1.0 / length.astype(jnp.float32))
        out[:rank] = jnp.where(col < length, one, 0.0)
        out[rank:] = sums[1][:, slot * slots : (slot + 1) * slots]


def project(act, og, wi, wo, lens, groups, share, ahead, piece, cost, after=()):
    steps = [step for group in groups for step in group]
    count = len(steps) * share
    slots, feat, hidden = act.shape[1], act.shape[2], og.shape[2]
    rank = wi.shape[0]
    pieces = -(-feat // piece) - (-hidden // piece)
    return pl.pallas_call(
        functools.partial(project_kernel, steps, share, ahead, piece, len(after)),
        out_shape=[jax.ShapeDtypeStruct((len(group) * share, 2 * rank, slots), jnp.float32) for group in groups],
        in_specs=[HBM] * 5 + [VMEM] * len(after),
        out_specs=[VMEM] * len(groups),
        scratch_shapes=[
            pltpu.VMEM((pieces, count, slots, piece), act.dtype),
            pltpu.VMEM((rank, feat), wi.dtype),
            pltpu.VMEM((rank, hidden), wo.dtype),
            pltpu.SMEM(lens.shape, lens.dtype),
            pltpu.SemaphoreType.DMA((pieces, len(steps))),
            pltpu.SemaphoreType.DMA((3,)),
        ],
        compiler_params=pltpu.CompilerParams(vmem_limit_bytes=32 << 20),
        cost_estimate=pl.CostEstimate(flops=cost, bytes_accessed=cost // 256, transcendentals=0),
    )(*map(in_hbm, (act, og, wi, wo, lens)), *after)


def unit_kernel(share, rank, size, *refs):
    singles, parts, outs = refs[:share], refs[share : -2 - size], refs[-2 - size : -2]
    pairs, held = refs[-2:]
    me = lax.axis_index("tensor")
    rows = rank * rank // 128
    span = rows // size
    dot = functools.partial(lax.dot_general, dimension_numbers=NT, preferred_element_type=jnp.float32)
    for k in range(share):
        full = singles[k][0]
        for part in parts:
            full = full + part[k]
        high = full.astype(jnp.bfloat16)
        low = (full - high.astype(jnp.float32)).astype(jnp.bfloat16)
        left, right = slice(None, rank), slice(rank, None)
        pairs[k] = dot(high[left], high[right]) + (dot(high[left], low[right]) + dot(low[left], high[right]))
    for k in range(share):
        even = pairs[k, pl.ds(0, rows, stride=2), :]
        odd = pairs[k, pl.ds(1, rows, stride=2), :]
        flat = jnp.concatenate([even, odd], axis=1)
        scale = jnp.sqrt(jnp.sum(flat * flat) / (rank * rank) + 1e-06)
        unit = flat / scale
        for to in range(size):
            held[k, to] = unit[to * span : (to + 1) * span]
        for step in range(size):
            outs[step][k] = held[k, me ^ step]


def units(parts, singles, share, rank, size):
    span = rank * rank // 128 // size
    return pl.pallas_call(
        functools.partial(unit_kernel, share, rank, size),
        out_shape=[jax.ShapeDtypeStruct((share, span, 128), jnp.float32)] * size,
        in_specs=[VMEM] * (share + len(parts)),
        out_specs=[VMEM] * size,
        scratch_shapes=[pltpu.VMEM((share, rank, rank), jnp.float32), pltpu.VMEM((share, size, span, 128), jnp.float32)],
        compiler_params=SMALL,
    )(*singles, *parts)


def score_kernel(share, steps, origins, *refs):
    unit_refs, test_refs, out, held = refs[: len(steps)], refs[len(steps) : -2], refs[-2], refs[-1]
    me, dp = lax.axis_index("tensor"), lax.axis_index("dp")
    for step, unit_ref in zip(steps, unit_refs):
        for k in range(share):
            held[(me ^ step) * share + k] = unit_ref[k]
    unit = jnp.concatenate([held[:, c, :] for c in range(held.shape[1])], axis=1).astype(jnp.bfloat16)
    tests = test_refs[0].shape[0]
    for (factor, offset, modulus), test_ref in zip(origins, test_refs):
        part = lax.dot_general(unit, test_ref[...], NT, preferred_element_type=jnp.float32)
        at = lax.rem(factor * dp + offset, modulus) * tests
        out[:, pl.ds(pl.multiple_of(at, 128), tests)] = part


def score(unit_parts, test_parts, share):
    size, groups = len(unit_parts), len(test_parts)
    tests, width = test_parts[0][0].shape
    origins = [origin for _, *origin in test_parts]
    return pl.pallas_call(
        functools.partial(score_kernel, share, tuple(unit_parts), origins),
        out_shape=jax.ShapeDtypeStruct((share * size, tests * groups), jnp.float32),
        in_specs=[VMEM] * (size + groups),
        out_specs=VMEM,
        scratch_shapes=[pltpu.VMEM((share * size, width // 128, 128), jnp.float32)],
        compiler_params=SMALL,
    )(*unit_parts.values(), *(shard for shard, *_ in test_parts))


def gather_tests(own, groups):
    def shift(value, step):
        return lax.ppermute(value, "dp", [(i, (i + step) % groups) for i in range(groups)])

    if groups == 4:
        first = shift(own, 1)
        return [(own, 1, 0, 4), (first, 1, 3, 4), (shift(own, -1), 1, 1, 4), (shift(first, 1), 1, 2, 4)]
    return [(own, 1, 0, groups)] + [(shift(own, step), 1, groups - step, groups) for step in range(1, groups)]


def exchange(outs, size):
    return {step: xor_permute(outs[step], "tensor", size, step) for step in [*range(2, size), 1]} | {0: outs[0]}


def shards(size, groups, activations, out_grads, proj_in, proj_out, lengths, test_grads):
    rank = proj_in.shape[1]
    share = activations.shape[0] // size
    own_tests = cut_tests(test_grads, size)
    tests = gather_tests(own_tests, groups)

    far = [CORES * x for x in range(1, size // CORES)]
    arrays = (activations, out_grads, proj_in.T, proj_out.T, lengths)
    far_other, far_own = project(*arrays, [[step ^ 1 for step in far], far], share, 4, 512, COST, [own_tests])
    far_sum = far_own + xor_permute(far_other, "tensor", size, 1)
    sums = [xor_permute(far_sum[i * share : (i + 1) * share], "tensor", size, step) for i, step in enumerate(far)]
    here = xor_permute(tests[1][0][:16, :128], "tensor", size, 1)
    near_other, near_own = project(*arrays, [[1], [0]], share, 4, 512, LATER, [far_sum, here])
    late = tests[2][0][: near_other.shape[1], : near_other.shape[2]].astype(jnp.float32)
    pieces = [near_other[k : k + 1] for k in range(share)]
    pieces[0] = pieces[0] + 0.0 * late[None]
    arrived = [xor_permute(one, "tensor", size, 1) for one in pieces]

    unit_outs = units([near_own] + sums, arrived, share, rank, size)
    unit_parts = exchange(unit_outs, size)
    part = score(unit_parts, tests, share)
    parts = exchange([part] * size, size)
    parts = [parts[step ^ (size - 2)] for step in range(size)]
    while len(parts) > 1:
        parts = [parts[i] + parts[i + 1] for i in range(0, len(parts), 2)]
    return parts[0]


def solution(mesh):
    placed = (
        P(("groups", "dp"), None, "tensor"),
        P(("groups", "dp"), None, "tensor"),
        P("tensor", None),
        P("tensor", None),
        P(("groups", "dp")),
        P(("groups", "dp"), None),
    )
    return jax.shard_map(
        functools.partial(shards, mesh.shape["tensor"], mesh.shape["dp"]),
        mesh=mesh,
        in_specs=placed,
        out_specs=P(("groups", "dp"), None),
        check_vma=False,
    )
```

```python
import functools

import jax
import jax.numpy as jnp
from jax import lax
from jax.experimental import pallas as pl
from jax.experimental.pallas import tpu as pltpu
from jax.sharding import PartitionSpec as P

CORES = 2
SMALL = pltpu.CompilerParams(vmem_limit_bytes=8 << 20)
NT = (((1,), (1,)), ((), ()))
HBM = pl.BlockSpec(memory_space=pltpu.HBM)
in_hbm = functools.partial(pltpu.with_memory_space_constraint, memory_space=pltpu.HBM)
VMEM = pl.BlockSpec(memory_space=pltpu.VMEM)


def xor_permute(value, axis, size, step):
    return lax.ppermute(value, axis, [(i, i ^ step) for i in range(size)])


def cut_kernel(tests, out, sem):
    width = out.shape[1]
    start = pl.multiple_of(lax.axis_index("tensor") * width, 128)
    copy = pltpu.make_async_copy(tests.at[:, pl.ds(start, width)], out, sem)
    copy.start()
    copy.wait()


def cut_tests(tests, size):
    rows, width = tests.shape
    return pl.pallas_call(
        cut_kernel,
        out_shape=jax.ShapeDtypeStruct((rows, width // size), tests.dtype),
        in_specs=[HBM],
        out_specs=VMEM,
        scratch_shapes=[pltpu.SemaphoreType.DMA],
        compiler_params=SMALL,
    )(in_hbm(tests))


COST = 1 << 32
LATER = 1<<10


def project_kernel(steps, share, ahead, piece, after, act, og, wi, wo, lens, *refs):
    refs = refs[after:]
    outs, (buf, wibuf, wobuf, lenbuf, sem, wsem) = refs[:-6], refs[-6:]
    me = lax.axis_index("tensor")
    rank = wibuf.shape[0]
    slots = buf.shape[2]
    count = len(steps) * share
    tokens = count * slots
    small = [
        pltpu.make_async_copy(wi, wibuf, wsem.at[0]),
        pltpu.make_async_copy(wo, wobuf, wsem.at[1]),
        pltpu.make_async_copy(lens, lenbuf, wsem.at[2]),
    ]
    pieces = [(side, at) for side, ref in enumerate((act, og)) for at in range(0, ref.shape[2], piece)]
    copies = []
    for slot, (side, at) in enumerate(pieces):
        width = min(piece, (act, og)[side].shape[2] - at)
        copies.append(
            [
                pltpu.make_async_copy(
                    (act, og)[side].at[pl.ds((me ^ step) * share, share), :, pl.ds(at, width)],
                    buf.at[slot, pl.ds(i * share, share), :, pl.ds(0, width)],
                    sem.at[slot, i],
                )
                for i, step in enumerate(steps)
            ]
        )
    small[0].start()
    for slot, group in enumerate(copies):
        if slot == 1:
            small[1].start()
            small[2].start()
        if slot < ahead:
            for copy in group:
                copy.start()
    sums = [None, None]
    for slot, (side, at) in enumerate(pieces):
        if at == 0:
            small[side].wait()
        for copy in copies[slot]:
            copy.wait()
        if slot + ahead < len(pieces):
            for copy in copies[slot + ahead]:
                copy.start()
        weight = (wibuf, wobuf)[side][:, at : at + piece]
        token = buf[slot].reshape(tokens, piece)[:, : weight.shape[1]]
        part = lax.dot_general(weight, token, NT, preferred_element_type=jnp.float32)
        sums[side] = part if sums[side] is None else sums[side] + part
    small[2].wait()
    col = lax.broadcasted_iota(jnp.int32, (rank, slots), 1)
    places = [out.at[i] for out in outs for i in range(out.shape[0])]
    for slot, out in enumerate(places):
        length = lenbuf[(me ^ steps[slot // share]) * share + slot % share]
        one = sums[0][:, slot * slots : (slot + 1) * slots] * (1.0 / length.astype(jnp.float32))
        out[:rank] = jnp.where(col < length, one, 0.0)
        out[rank:] = sums[1][:, slot * slots : (slot + 1) * slots]


def project(act, og, wi, wo, lens, groups, share, ahead, piece, cost, after=()):
    steps = [step for group in groups for step in group]
    count = len(steps) * share
    slots, feat, hidden = act.shape[1], act.shape[2], og.shape[2]
    rank = wi.shape[0]
    pieces = -(-feat // piece) - (-hidden // piece)
    return pl.pallas_call(
        functools.partial(project_kernel, steps, share, ahead, piece, len(after)),
        out_shape=[jax.ShapeDtypeStruct((len(group) * share, 2 * rank, slots), jnp.float32) for group in groups],
        in_specs=[HBM] * 5 + [VMEM] * len(after),
        out_specs=[VMEM] * len(groups),
        scratch_shapes=[
            pltpu.VMEM((pieces, count, slots, piece), act.dtype),
            pltpu.VMEM((rank, feat), wi.dtype),
            pltpu.VMEM((rank, hidden), wo.dtype),
            pltpu.SMEM(lens.shape, lens.dtype),
            pltpu.SemaphoreType.DMA((pieces, len(steps))),
            pltpu.SemaphoreType.DMA((3,)),
        ],
        compiler_params=pltpu.CompilerParams(vmem_limit_bytes=32 << 20),
        cost_estimate=pl.CostEstimate(flops=cost, bytes_accessed=cost // 256, transcendentals=0),
    )(*map(in_hbm, (act, og, wi, wo, lens)), *after)


def unit_kernel(share, rank, size, *refs):
    singles, parts, outs = refs[:share], refs[share : -2 - size], refs[-2 - size : -2]
    pairs, held = refs[-2:]
    me = lax.axis_index("tensor")
    rows = rank * rank // 128
    span = rows // size
    dot = functools.partial(lax.dot_general, dimension_numbers=NT, preferred_element_type=jnp.float32)
    for k in range(share):
        full = singles[k][0]
        for part in parts:
            full = full + part[k]
        high = full.astype(jnp.bfloat16)
        low = (full - high.astype(jnp.float32)).astype(jnp.bfloat16)
        left, right = slice(None, rank), slice(rank, None)
        both = dot(high[left], jnp.concatenate([high[right], low[right]], axis=0))
        pairs[k] = both[:, :rank] + (both[:, rank:] + dot(low[left], high[right]))
    for k in range(share):
        even = pairs[k, pl.ds(0, rows, stride=2), :]
        odd = pairs[k, pl.ds(1, rows, stride=2), :]
        flat = jnp.concatenate([even, odd], axis=1)
        scale = jnp.sqrt(jnp.sum(flat * flat) / (rank * rank) + 1e-06)
        unit = flat / scale
        for to in range(size):
            held[k, to] = unit[to * span : (to + 1) * span]
        for step in range(size):
            outs[step][k] = held[k, me ^ step]


def units(parts, singles, share, rank, size):
    span = rank * rank // 128 // size
    return pl.pallas_call(
        functools.partial(unit_kernel, share, rank, size),
        out_shape=[jax.ShapeDtypeStruct((share, span, 128), jnp.float32)] * size,
        in_specs=[VMEM] * (share + len(parts)),
        out_specs=[VMEM] * size,
        scratch_shapes=[pltpu.VMEM((share, rank, rank), jnp.float32), pltpu.VMEM((share, size, span, 128), jnp.float32)],
        compiler_params=SMALL,
    )(*singles, *parts)


def score_kernel(share, steps, origins, *refs):
    unit_refs, test_refs, out, held = refs[: len(steps)], refs[len(steps) : -2], refs[-2], refs[-1]
    me, dp = lax.axis_index("tensor"), lax.axis_index("dp")
    for step, unit_ref in zip(steps, unit_refs):
        for k in range(share):
            held[(me ^ step) * share + k] = unit_ref[k]
    unit = jnp.concatenate([held[:, c, :] for c in range(held.shape[1])], axis=1).astype(jnp.bfloat16)
    tests = test_refs[0].shape[0]
    for (factor, offset, modulus), test_ref in zip(origins, test_refs):
        part = lax.dot_general(unit, test_ref[...], NT, preferred_element_type=jnp.float32)
        at = lax.rem(factor * dp + offset, modulus) * tests
        out[:, pl.ds(pl.multiple_of(at, 128), tests)] = part


def score(unit_parts, test_parts, share):
    size, groups = len(unit_parts), len(test_parts)
    tests, width = test_parts[0][0].shape
    origins = [origin for _, *origin in test_parts]
    return pl.pallas_call(
        functools.partial(score_kernel, share, tuple(unit_parts), origins),
        out_shape=jax.ShapeDtypeStruct((share * size, tests * groups), jnp.float32),
        in_specs=[VMEM] * (size + groups),
        out_specs=VMEM,
        scratch_shapes=[pltpu.VMEM((share * size, width // 128, 128), jnp.float32)],
        compiler_params=SMALL,
    )(*unit_parts.values(), *(shard for shard, *_ in test_parts))


def gather_tests(own, groups):
    def shift(value, step):
        return lax.ppermute(value, "dp", [(i, (i + step) % groups) for i in range(groups)])

    if groups == 4:
        first = shift(own, 1)
        return [(own, 1, 0, 4), (first, 1, 3, 4), (shift(own, -1), 1, 1, 4), (shift(first, 1), 1, 2, 4)]
    return [(own, 1, 0, groups)] + [(shift(own, step), 1, groups - step, groups) for step in range(1, groups)]


def exchange(outs, size):
    return {step: xor_permute(outs[step], "tensor", size, step) for step in [*range(2, size), 1]} | {0: outs[0]}


def shards(size, groups, activations, out_grads, proj_in, proj_out, lengths, test_grads):
    rank = proj_in.shape[1]
    share = activations.shape[0] // size
    own_tests = cut_tests(test_grads, size)
    tests = gather_tests(own_tests, groups)

    far = [CORES * x for x in range(1, size // CORES)]
    arrays = (activations, out_grads, proj_in.T, proj_out.T, lengths)
    far_other, far_own = project(*arrays, [[step ^ 1 for step in far], far], share, 4, 512, COST, [own_tests])
    far_sum = far_own + xor_permute(far_other, "tensor", size, 1)
    sums = [xor_permute(far_sum[i * share : (i + 1) * share], "tensor", size, step) for i, step in enumerate(far)]
    here = xor_permute(tests[1][0][:16, :128], "tensor", size, 1)
    near_other, near_own = project(*arrays, [[1], [0]], share, 4, 512, LATER, [far_sum, here])
    late = tests[2][0][: near_other.shape[1], : near_other.shape[2]].astype(jnp.float32)
    pieces = [near_other[k : k + 1] for k in range(share)]
    pieces[0] = pieces[0] + 0.0 * late[None]
    arrived = [xor_permute(one, "tensor", size, 1) for one in pieces]

    unit_outs = units([near_own] + sums, arrived, share, rank, size)
    unit_parts = exchange(unit_outs, size)
    part = score(unit_parts, tests, share)
    parts = exchange([part] * size, size)
    parts = [parts[step ^ (size - 2)] for step in range(size)]
    while len(parts) > 1:
        parts = [parts[i] + parts[i + 1] for i in range(0, len(parts), 2)]
    return parts[0]


def solution(mesh):
    placed = (
        P(("groups", "dp"), None, "tensor"),
        P(("groups", "dp"), None, "tensor"),
        P("tensor", None),
        P("tensor", None),
        P(("groups", "dp")),
        P(("groups", "dp"), None),
    )
    return jax.shard_map(
        functools.partial(shards, mesh.shape["tensor"], mesh.shape["dp"]),
        mesh=mesh,
        in_specs=placed,
        out_specs=P(("groups", "dp"), None),
        check_vma=False,
    )
```
